256 devices in a mesh: rep: 32 (over z, x_hi, core), fsdp: 8 (over y, x_lo).
Axes of the slice: x: 4 (x_hi: 2, x_lo: 2; x = x_hi * 2 + x_lo), y: 4, z: 8, core: 2. Of those that a mesh axis runs over, the one named last changes fastest.
Arguments:
- tokens: bfloat16 [65536, 4096], P(('rep', 'fsdp')), may hold values from -6 to 6
- cotangent: bfloat16 [65536, 1024], P(('rep', 'fsdp')), may hold values from -0.29882812 to 0.29882812
- weight: bfloat16 [4096, 1024], P('fsdp'), may hold values from -0.09375 to 0.09375
- momentum: float32 [32, 4096, 1024], P('rep', 'fsdp'), may hold values from -6 to 6
- kept_index: int32 [4096, 16, 4], P('fsdp'), may hold values from 0 to 63, as said below
Outputs:
- projected: bfloat16 [65536, 1024], P(('rep', 'fsdp'))
- new_weight: bfloat16 [4096, 1024], P('fsdp')
- new_momentum: float32 [32, 4096, 1024], P('rep', 'fsdp')
The draws below stay inside these ranges and needn't reach their ends.
Inputs may be any that keep to these rules, and one draw needn't show every extreme that they name: `kept_index`: the four indices of one block are distinct.
All inputs are finite; a program needn't handle non-finite values.
Results may differ from the reference program's by a relative error of at most 0.0049.
Values may be sent and summed in bfloat16 or wider, within the bound.
No kernel may reach another device: no remote copies, remote signals or barrier semaphores. Data moves between devices by JAX's collectives and lax.ppermute only.
A program may use at most 128 MiB of HBM per device.

```python
import jax
import jax.numpy as jnp
from jax import lax

D = 4096
KV = 1024
TOK_DEV = 256
TOKENS = 65536
N_REP = 32
N_FSDP = 8


def draw_kept_index(key, part):
    key = jax.random.fold_in(key, 7)
    scores = jax.random.randint(key, (D, KV // 64, 64), 0, 1048576, dtype=jnp.int32)
    lane_ids = lax.broadcasted_iota(jnp.int32, (D, KV // 64, 64), 2)
    row_ids = lax.broadcasted_iota(jnp.int32, (D, KV // 64, 64), 0)
    block_ids = lax.broadcasted_iota(jnp.int32, (D, KV // 64, 64), 1)
    scores = scores * 64 + lane_ids
    corner = (row_ids == 0) & (block_ids == 0) & ((lane_ids == 0) | (lane_ids == 63))
    scores = scores + jnp.where(corner, jnp.int32(268435456), jnp.int32(0))
    values, indices = lax.top_k(scores, 4)
    return indices.astype(jnp.int32)


def block_levels(key, dims, pieces, smallest, high):
    gain, own = 1.0, jax.random.fold_in(key, 6)
    for position, blocks in pieces:
        steps = jnp.exp(jax.random.uniform(jax.random.fold_in(own, position), (blocks,), jnp.float32, smallest / len(pieces), high / len(pieces)))
        gain = gain * jnp.repeat(steps, dims[position] // blocks).reshape([-1 if axis == position else 1 for axis in range(len(dims))])
    return gain


def bell_draw(key, shape, scale, most, cuts=(), kind=jnp.bfloat16):
    entries = scale * jax.random.normal(key, shape, jnp.float32)
    if cuts:
        entries = entries * block_levels(key, shape, cuts, -0.22, 0.18)
    return jnp.clip(entries, -most, most).astype(kind)


def setup_inputs(seed: int = 0) -> dict:
    arg_keys = jax.random.split(jax.random.key(seed), 6)
    tokens = bell_draw(arg_keys[0], (TOKENS, D), 1.0, 6.0, ((0, 256),))
    cotangent = bell_draw(arg_keys[1], (TOKENS, KV), 0.05, 0.29882812, ((0, 256),))
    weight = bell_draw(arg_keys[2], (D, KV), D ** -0.5, 0.09375, ((0, 8),))
    momentum = bell_draw(arg_keys[3], (N_REP, D, KV), 1.0, 6.0, ((0, 32), (1, 8)), jnp.float32)
    kept_index = draw_kept_index(jax.random.fold_in(arg_keys[5], 71), 0)
    return {"tokens": tokens, "cotangent": cotangent, "weight": weight, "momentum": momentum, "kept_index": kept_index}


beta_decay = 0.9
step_rate = 0.5

def dct_pair():
    index = jnp.arange(64, dtype=jnp.float32)
    freq = index[:, None]
    angle = jnp.pi * (2.0 * index[None, :] + 1.0) * freq / 128.0
    factor = jnp.where(freq == 0.0, jnp.sqrt(jnp.float32(1.0 / 64.0)), jnp.sqrt(jnp.float32(2.0 / 64.0)))
    single = (factor * jnp.cos(angle)).astype(jnp.float32)
    return jnp.kron(jnp.eye(2, dtype=jnp.float32), single)

def kept_lanes(kept_index):
    rows = kept_index.shape[0]
    pairs = kept_index.reshape(rows, kept_index.shape[1] // 2, 2, 4)
    pairs = pairs + (jnp.arange(2, dtype=jnp.int32) * 64)[None, None, :, None]
    return pairs.reshape(rows, kept_index.shape[1] // 2, 8)

def to_spectrum(field, basis):
    rows, width = field.shape
    flat = jnp.dot(field.reshape(-1, 128), basis.T, precision=lax.Precision.HIGHEST, preferred_element_type=jnp.float32)
    return flat.reshape(rows, width // 128, 128)

def from_spectrum(spectrum, basis):
    rows, blocks, lanes = spectrum.shape
    flat = jnp.dot(spectrum.reshape(-1, 128), basis, precision=lax.Precision.HIGHEST, preferred_element_type=jnp.float32)
    return flat.reshape(rows, blocks * lanes)

def reference(tokens, cotangent, weight, momentum, kept_index):
    basis = dct_pair()
    lanes = kept_lanes(kept_index)
    mask = lanes[..., None] == jnp.arange(128, dtype=jnp.int32)
    group_tokens = tokens.reshape(N_REP, TOK_DEV * N_FSDP, D)
    group_cot = cotangent.reshape(N_REP, TOK_DEV * N_FSDP, KV)

    def per_replica(total, items):
        feats, grads, moment_old = items
        gradient = jnp.dot(feats.T, grads, preferred_element_type=jnp.float32)
        moment = beta_decay * moment_old + gradient
        spectrum = to_spectrum(moment, basis)
        picked = lax.optimization_barrier(jnp.sum(jnp.where(mask, spectrum[:, :, None, :], jnp.float32(0.0)), axis=3))
        kept = lax.optimization_barrier(jnp.sum(jnp.where(mask, picked[..., None], jnp.float32(0.0)), axis=2))
        return (total + picked, moment - from_spectrum(kept, basis))
    start = jnp.zeros(lanes.shape, jnp.float32)
    total, new_momentum = lax.scan(per_replica, start, (group_tokens, group_cot, momentum))
    dense = lax.optimization_barrier(jnp.sum(jnp.where(mask, total[..., None], jnp.float32(0.0)), axis=2))
    delta = from_spectrum(dense, basis) / N_REP
    new_weight = (weight.astype(jnp.float32) - step_rate * delta).astype(jnp.bfloat16)
    projected = jnp.dot(tokens, new_weight, preferred_element_type=jnp.float32).astype(jnp.bfloat16)
    return (projected, new_weight, new_momentum)
```

```python
import jax
import jax.numpy as jnp
import numpy as np
from jax import lax
from jax.experimental import pallas as pl
from jax.experimental.pallas import tpu as pltpu
from jax.sharding import PartitionSpec as P

beta_decay = 0.9
step_rate = 0.5
ROWS = 512
KV = 1024
TOK = 256
BLOCK = 64
KEEP = 4
HALF = KV // 2
GROUP = 256
STEPS = KV // GROUP
PICKS = KV // BLOCK * KEEP
LANES = 128
PACK = 16
REPS = 32
VMEM_LIMIT = 24 * 1024 * 1024


def dct_group():
    n = np.arange(BLOCK, dtype=np.float64)
    single = np.cos(np.pi * (2.0 * n[None, :] + 1.0) * n[:, None] / (2 * BLOCK))
    single *= np.where(n[:, None] == 0, np.sqrt(1.0 / BLOCK), np.sqrt(2.0 / BLOCK))
    return np.kron(np.eye(GROUP // BLOCK), single).astype(np.float32)


def split_pair(values):
    high = values.astype(jnp.bfloat16)
    return high, (values - high.astype(jnp.float32)).astype(jnp.bfloat16)


def mix(left, right, dims):
    return lax.dot_general(left, right, (dims, ((), ())), preferred_element_type=jnp.float32)


def three_pass(left_pair, right_pair, dims):
    return (
        mix(left_pair[0], right_pair[0], dims)
        + mix(left_pair[0], right_pair[1], dims)
        + mix(left_pair[1], right_pair[0], dims)
    )


def expand_block(index_rows, value_rows, width):
    freq = lax.broadcasted_iota(jnp.int32, (BLOCK, width), 0)
    dense = jnp.zeros((BLOCK, width), jnp.float32)
    for j in range(KEEP):
        dense = jnp.where(index_rows[j] == freq, value_rows[j], dense)
    return dense


def spread_row(tile, row):
    return jnp.broadcast_to(tile[row : row + 1, :], (PACK, LANES)).astype(jnp.bfloat16)


def expand_tile(indices, values, dense, first, cols):
    freq = lax.broadcasted_iota(jnp.int32, (PACK, LANES), 0).astype(jnp.float32)
    for half in range(2):
        at = [spread_row(indices, half * KEEP + j) for j in range(KEEP)]
        have = [spread_row(values, half * KEEP + j) for j in range(KEEP)]
        for part in range(BLOCK // PACK):
            here = (freq + part * PACK).astype(jnp.bfloat16)
            tile = jnp.zeros((PACK, LANES), jnp.bfloat16)
            for j in range(KEEP):
                tile = jnp.where(at[j] == here, have[j], tile)
            start = first + half * BLOCK + part * PACK
            dense[start : start + PACK, cols] = tile


def four_products(cots, toks):
    total = jnp.dot(cots[0][...], toks[0][...], preferred_element_type=jnp.float32)
    for c, t in zip(cots[1:], toks[1:]):
        total += jnp.dot(c[...], t[...], preferred_element_type=jnp.float32)
    return total


def turn_kernel(cot, late_lo, late_hi, out):
    out[...] = cot[...].T


def copy_kernel(where, t0, t1, t2, t3, late, *outs):
    for t, out in zip((t0, t1, t2, t3), outs):
        out[...] = t[...]


def partial_first_kernel(c0, c1, c2, c3, t0, t1, t2, t3, idx, early, out):
    for g in range(HALF // GROUP):
        rows = slice(g * GROUP, (g + 1) * GROUP)
        cots = [c[rows, :] for c in (c0, c1, c2, c3)]
        out[rows, :] = four_products(cots, (t0, t1, t2, t3)).astype(out.dtype)
    out[HALF:, :] = idx[...].astype(jnp.float32).astype(out.dtype)


def partial_second_kernel(c0, c1, c2, c3, t0, t1, t2, t3, out):
    for g in range(HALF // GROUP):
        rows = slice(g * GROUP, (g + 1) * GROUP)
        cots = [c[rows, :] for c in (c0, c1, c2, c3)]
        out[rows, :] = four_products(cots, (t0, t1, t2, t3)).astype(out.dtype)


def own_kernel(a0, a1, a2, a3, b0, b1, b2, b3, t0, t1, t2, t3, mom, out):
    first = pl.program_id(0) < STEPS // 2
    cots = [jnp.where(first, a[...], b[...]) for a, b in zip((a0, a1, a2, a3), (b0, b1, b2, b3))]
    out[...] = four_products(cots, (t0, t1, t2, t3)) + beta_decay * mom[...].T


def received(got_a, got_b):
    first = pl.program_id(0) < STEPS // 2
    return jnp.where(first, got_a[...], got_b[...]).astype(jnp.float32)


def pick_kernel(pre, got_a, got_b, idx, ch, cl, late, picked, tiles):
    moment = pre[...] + received(got_a, got_b)
    spectrum = three_pass((ch[...], cl[...]), split_pair(moment), ((1,), (0,)))
    freq = lax.broadcasted_iota(jnp.int32, (BLOCK, ROWS), 0)
    rows = []
    for b in range(GROUP // BLOCK):
        part = spectrum[b * BLOCK : (b + 1) * BLOCK, :]
        for j in range(KEEP):
            at = idx[b * KEEP + j : b * KEEP + j + 1, :]
            rows.append(jnp.sum(jnp.where(at == freq, part, 0.0), axis=0, keepdims=True))
    values = jnp.concatenate(rows, axis=0)
    picked[...] = values
    for t in range(GROUP // BLOCK * KEEP // 8):
        for q in range(ROWS // LANES):
            tile = values[t * 8 : (t + 1) * 8, q * LANES : (q + 1) * LANES]
            tiles[t * (ROWS // LANES) + q] = tile.astype(tiles.dtype)


def share_kernel(spread, out):
    total = jnp.sum(spread[...].astype(jnp.float32), axis=0, keepdims=True)
    out[...] = jnp.broadcast_to(total, out.shape).astype(out.dtype)


def residual_kernel(pre, got_a, got_b, picked, idx, ch, cl, out):
    parts = []
    for b in range(GROUP // BLOCK):
        rows = [slice(b * KEEP + j, b * KEEP + j + 1) for j in range(KEEP)]
        parts.append(expand_block([idx[r, :] for r in rows], [picked[r, :] for r in rows], ROWS))
    kept = jnp.concatenate(parts, axis=0)
    back = three_pass((ch[...], cl[...]), split_pair(kept), ((0,), (0,)))
    out[...] = (pre[...] + received(got_a, got_b) - back).T


def base_kernel(where, o0, o1, o2, o3, p0, p1, p2, p3, w_own, w_peer, idx, got_a, *outs):
    mine = idx[...].astype(jnp.float32).astype(jnp.bfloat16)
    theirs = got_a[HALF:, :]
    first = where[0] == 0
    left, right = jnp.where(first, mine, theirs), jnp.where(first, theirs, mine)
    for own, peer, out in zip((o0, o1, o2, o3), (p0, p1, p2, p3), outs):
        total = jnp.dot(own[...], w_own[...], preferred_element_type=jnp.float32)
        total += jnp.dot(peer[...], w_peer[...], preferred_element_type=jnp.float32)
        out[:TOK, :] = total.astype(out.dtype)
        out[TOK:, :ROWS] = left
        out[TOK:, ROWS:] = right


def forward_kernel(where, tok, own, hi, far, lo, tot, ch, cl, out, dense, mixed):
    step = pl.program_id(0)
    tail = slice(TOK, TOK + PICKS)
    near = jnp.where(step == 0, own[tail, :], hi[tail, :])
    away = jnp.where(step == 2, far[tail, :], lo[tail, :])
    pairs = jnp.where(step < 2, near, away).astype(jnp.float32)

    @pl.when(step == 0)
    def _():
        mixed[...] = jnp.zeros_like(mixed)

    for g in range(STEPS):
        for t in range(2 * g, 2 * g + 2):
            for f in range(2):
                for q in range(ROWS // LANES):
                    cols = slice(f * ROWS + q * LANES, f * ROWS + (q + 1) * LANES)
                    values = tot[t * (ROWS // LANES) + q, f].astype(jnp.float32)
                    expand_tile(pairs[t * 8 : (t + 1) * 8, cols], values, dense, t * 2 * BLOCK, cols)
        span = slice(g * GROUP, (g + 1) * GROUP)
        mixed[:, span] += mix(tok[...], dense[span, :], ((1,), (1,)))

    @pl.when(step == 3)
    def _():
        for g in range(STEPS):
            span = slice(g * GROUP, (g + 1) * GROUP)
            delta = three_pass(split_pair(mixed[:, span]), (ch[...], cl[...]), ((1,), (0,)))
            base = own[:TOK, span].astype(jnp.float32) + hi[:TOK, span].astype(jnp.float32)
            base += far[:TOK, span].astype(jnp.float32) + lo[:TOK, span].astype(jnp.float32)
            out[:, span] = (base - (step_rate / REPS) * delta).astype(out.dtype)


def weight_kernel(where, weight, tot, idx, ch, cl, out, dense):
    indices = idx[...].astype(jnp.float32)
    for g in range(STEPS):
        for t in range(2 * g, 2 * g + 2):
            for q in range(ROWS // LANES):
                cols = slice(q * LANES, (q + 1) * LANES)
                values = tot[t * (ROWS // LANES) + q, 0].astype(jnp.float32)
                expand_tile(indices[t * 8 : (t + 1) * 8, cols], values, dense, t * 2 * BLOCK, cols)
        span = slice(g * GROUP, (g + 1) * GROUP)
        turned = dense[span, :].T
        delta = mix(turned, ch[...], ((1,), (0,))) + mix(turned, cl[...], ((1,), (0,)))
        out[:, span] = (weight[:, span].astype(jnp.float32) - (step_rate / REPS) * delta).astype(out.dtype)


def params():
    return pltpu.CompilerParams(vmem_limit_bytes=VMEM_LIMIT)


def cost(flops, mib):
    return pl.CostEstimate(flops=int(flops), bytes_accessed=int(mib * (1 << 20)), transcendentals=0)


def whole(*shape):
    return pl.BlockSpec(shape, lambda c, *_: (0,) * len(shape))


def by_row(rows, width):
    return pl.BlockSpec((rows, width), lambda c: (c, 0))


def by_col(rows, width):
    return pl.BlockSpec((rows, width), lambda c: (0, c))


def first_half(rows, width):
    return pl.BlockSpec((rows, width), lambda c: (jnp.minimum(c, STEPS // 2 - 1), 0))


def second_half(rows, width):
    return pl.BlockSpec((rows, width), lambda c: (jnp.maximum(c - STEPS // 2, 0), 0))


AFTER = pl.BlockSpec(memory_space=pl.ANY)
BASIS = [whole(GROUP, GROUP)] * 2
GOT = [first_half(GROUP, ROWS), second_half(GROUP, ROWS)]
BF16, F32 = jnp.bfloat16, jnp.float32


def body(tokens, cotangent, weight, momentum, kept_index):
    basis = dct_group()
    high = jnp.asarray(basis).astype(BF16)
    low = (jnp.asarray(basis) - high.astype(F32)).astype(BF16)
    fsdp = lax.axis_index("fsdp").astype(jnp.int32)
    y, side = fsdp >> 1, fsdp & 1
    other = 1 - side
    index_t = jnp.transpose(kept_index, (1, 2, 0)).reshape(PICKS, ROWS)

    plus = [(i, (i + 2) % 8) for i in range(8)]
    minus = [(i, (i + 6) % 8) for i in range(8)]
    across = [(i, (i + 4) % 8) for i in range(8)]
    swap = [(i, i ^ 1) for i in range(8)]

    def up(x):
        return lax.ppermute(x, "fsdp", plus)

    def down(x):
        return lax.ppermute(x, "fsdp", minus)

    def piece(distance, which):
        start = (((y + distance) & 3) * 2 + which) * ROWS
        return lax.dynamic_slice(tokens, (0, start), (TOK, ROWS))

    weight_peer = lax.ppermute(weight, "fsdp", swap)

    cot_a = cotangent[:, :HALF].T
    a_lo = up(cot_a)
    peer_step = down(piece(2, other))
    a_hi = down(cot_a)
    peer_lo = up(piece(1, other))
    peer_hi = down(piece(3, other))
    a_far = up(a_lo)
    peer_far = down(peer_step)
    cots_a = (cot_a, a_hi, a_far, a_lo)
    peers = (piece(0, other), peer_hi, peer_far, peer_lo)

    cot_b = pl.pallas_call(
        turn_kernel,
        grid=(1,),
        in_specs=[pl.BlockSpec((TOK, HALF), lambda c: (0, 1)), AFTER, AFTER],
        out_specs=whole(HALF, TOK),
        out_shape=jax.ShapeDtypeStruct((HALF, TOK), BF16),
        compiler_params=params(),
        cost_estimate=cost(0, 1),
    )(cotangent, a_lo, a_hi)
    b_lo = up(cot_b)
    b_hi = down(cot_b)
    b_far = down(b_hi)
    cots_b = (cot_b, b_hi, b_far, b_lo)

    own_0, own_1, own_2, own_3 = pl.pallas_call(
        copy_kernel,
        grid_spec=pltpu.PrefetchScalarGridSpec(
            num_scalar_prefetch=1,
            grid=(1,),
            in_specs=[
                pl.BlockSpec((TOK, ROWS), lambda c, s, d=d: (0, (s[0] + 2 * d) & 7)) for d in range(4)
            ]
            + [AFTER],
            out_specs=[whole(TOK, ROWS)] * 4,
        ),
        out_shape=[jax.ShapeDtypeStruct((TOK, ROWS), BF16)] * 4,
        compiler_params=params(),
        cost_estimate=cost(0, 2),
    )(fsdp.reshape(1), tokens, tokens, tokens, tokens, b_lo)
    owns = (own_0, down(own_3), up(up(own_2)), up(own_1))

    partial_a = pl.pallas_call(
        partial_first_kernel,
        grid=(1,),
        in_specs=[whole(HALF, TOK)] * 4 + [whole(TOK, ROWS)] * 4 + [whole(PICKS, ROWS), AFTER],
        out_specs=whole(HALF + PICKS, ROWS),
        out_shape=jax.ShapeDtypeStruct((HALF + PICKS, ROWS), BF16),
        compiler_params=params(),
        cost_estimate=cost(KV * KV * ROWS, 3),
    )(*cots_a, *peers, index_t, weight_peer)
    got_a = lax.ppermute(partial_a, "fsdp", swap)
    partial_b = pl.pallas_call(
        partial_second_kernel,
        grid=(1,),
        in_specs=[whole(HALF, TOK)] * 4 + [whole(TOK, ROWS)] * 4,
        out_specs=whole(HALF, ROWS),
        out_shape=jax.ShapeDtypeStruct((HALF, ROWS), BF16),
        compiler_params=params(),
        cost_estimate=cost(KV * KV * ROWS, 3),
    )(*cots_b, *peers)
    got_b = lax.ppermute(partial_b, "fsdp", swap)

    pre = pl.pallas_call(
        own_kernel,
        grid=(STEPS,),
        in_specs=[first_half(GROUP, TOK)] * 4
        + [second_half(GROUP, TOK)] * 4
        + [whole(TOK, ROWS)] * 4
        + [by_col(ROWS, GROUP)],
        out_specs=by_row(GROUP, ROWS),
        out_shape=jax.ShapeDtypeStruct((KV, ROWS), F32),
        compiler_params=params(),
        cost_estimate=cost(2 * KV * KV * ROWS, 7),
    )(*cots_a, *cots_b, *owns, momentum[0])

    based = pl.pallas_call(
        base_kernel,
        grid_spec=pltpu.PrefetchScalarGridSpec(
            num_scalar_prefetch=1,
            grid=(1,),
            in_specs=[whole(TOK, ROWS)] * 8
            + [whole(ROWS, KV)] * 2
            + [whole(PICKS, ROWS), whole(HALF + PICKS, ROWS)],
            out_specs=[whole(TOK + PICKS, KV)] * 4,
        ),
        out_shape=[jax.ShapeDtypeStruct((TOK + PICKS, KV), BF16)] * 4,
        compiler_params=params(),
        cost_estimate=cost(4 * KV * KV * ROWS, 7),
    )(side.reshape(1), *owns, *peers, weight, weight_peer, index_t, got_a)
    base_lo = up(based[1])
    base_far = lax.ppermute(based[2], "fsdp", across)
    base_hi = down(based[3])

    picked, tiles = pl.pallas_call(
        pick_kernel,
        grid=(STEPS,),
        in_specs=[by_row(GROUP, ROWS)] + GOT + [by_row(PICKS // STEPS, ROWS)] + BASIS + [AFTER],
        out_specs=[
            by_row(PICKS // STEPS, ROWS),
            pl.BlockSpec((REPS // STEPS, 8, LANES), lambda c: (c, 0, 0)),
        ],
        out_shape=[
            jax.ShapeDtypeStruct((PICKS, ROWS), F32),
            jax.ShapeDtypeStruct((REPS, 8, LANES), BF16),
        ],
        compiler_params=params(),
        cost_estimate=cost(6 * KV * GROUP * ROWS, 4),
    )(pre, got_a, got_b, index_t, high, low, based[0])

    spread = lax.all_to_all(tiles, "rep", 0, 0)
    copies = pl.pallas_call(
        share_kernel,
        grid=(1,),
        in_specs=[whole(REPS, 8, LANES)],
        out_specs=whole(REPS * 8, 8, LANES),
        out_shape=jax.ShapeDtypeStruct((REPS * 8, 8, LANES), BF16),
        compiler_params=params(),
        cost_estimate=cost(0, 1),
    )(spread)
    totals = lax.all_to_all(copies, ("rep", "fsdp"), 0, 0).reshape(REPS, 8, 8, LANES)

    new_momentum = pl.pallas_call(
        residual_kernel,
        grid=(STEPS,),
        in_specs=[by_row(GROUP, ROWS)] + GOT + [by_row(PICKS // STEPS, ROWS)] * 2 + BASIS,
        out_specs=by_col(ROWS, GROUP),
        out_shape=jax.ShapeDtypeStruct((ROWS, KV), F32),
        compiler_params=params(),
        cost_estimate=cost(6 * KV * GROUP * ROWS, 6),
    )(pre, got_a, got_b, picked, index_t, high, low)

    projected = pl.pallas_call(
        forward_kernel,
        grid_spec=pltpu.PrefetchScalarGridSpec(
            num_scalar_prefetch=1,
            grid=(4,),
            in_specs=[pl.BlockSpec((TOK, 2 * ROWS), lambda c, s: (0, (s[0] + c) & 3))]
            + [whole(TOK + PICKS, KV)] * 4
            + [pl.BlockSpec((REPS, 2, 8, LANES), lambda c, s: (0, (s[0] + c) & 3, 0, 0))]
            + BASIS,
            out_specs=whole(TOK, KV),
            scratch_shapes=[pltpu.VMEM((KV, 2 * ROWS), BF16), pltpu.VMEM((TOK, KV), F32)],
        ),
        out_shape=jax.ShapeDtypeStruct((TOK, KV), BF16),
        compiler_params=params(),
        cost_estimate=cost(8 * KV * KV * ROWS, 8),
    )(y.reshape(1), tokens, based[0], base_hi, base_far, base_lo, totals, high, low)

    new_weight = pl.pallas_call(
        weight_kernel,
        grid_spec=pltpu.PrefetchScalarGridSpec(
            num_scalar_prefetch=1,
            grid=(1,),
            in_specs=[
                whole(ROWS, KV),
                pl.BlockSpec((REPS, 1, 8, LANES), lambda c, s: (0, s[0], 0, 0)),
                whole(PICKS, ROWS),
            ]
            + BASIS,
            out_specs=whole(ROWS, KV),
            scratch_shapes=[pltpu.VMEM((KV, ROWS), BF16)],
        ),
        out_shape=jax.ShapeDtypeStruct((ROWS, KV), BF16),
        compiler_params=params(),
        cost_estimate=cost(4 * KV * GROUP * ROWS, 3),
    )(fsdp.reshape(1), weight, totals, index_t, high, low)
    return (projected, new_weight, new_momentum[None])


def solution(mesh):
    in_specs = (
        P(("rep", "fsdp"), None),
        P(("rep", "fsdp"), None),
        P("fsdp", None),
        P("rep", "fsdp", None),
        P("fsdp", None, None),
    )
    out_specs = (P(("rep", "fsdp"), None), P("fsdp", None), P("rep", "fsdp", None))
    return jax.shard_map(body, mesh=mesh, in_specs=in_specs, out_specs=out_specs, check_vma=False)
```

```python
import jax
import jax.numpy as jnp
import numpy as np
from jax import lax
from jax.experimental import pallas as pl
from jax.experimental.pallas import tpu as pltpu
from jax.sharding import PartitionSpec as P

beta_decay = 0.9
step_rate = 0.5
ROWS = 512
KV = 1024
TOK = 256
BLOCK = 64
KEEP = 4
HALF = KV // 2
GROUP = 256
STEPS = KV // GROUP
PICKS = KV // BLOCK * KEEP
LANES = 128
FAR = TOK // 2
PACK = 16
REPS = 32
VMEM_LIMIT = 24 * 1024 * 1024


def dct_group():
    n = np.arange(BLOCK, dtype=np.float64)
    single = np.cos(np.pi * (2.0 * n[None, :] + 1.0) * n[:, None] / (2 * BLOCK))
    single *= np.where(n[:, None] == 0, np.sqrt(1.0 / BLOCK), np.sqrt(2.0 / BLOCK))
    return np.kron(np.eye(GROUP // BLOCK), single).astype(np.float32)


def split_pair(values):
    high = values.astype(jnp.bfloat16)
    return high, (values - high.astype(jnp.float32)).astype(jnp.bfloat16)


def mix(left, right, dims):
    return lax.dot_general(left, right, (dims, ((), ())), preferred_element_type=jnp.float32)


def three_pass(left_pair, right_pair, dims):
    return (
        mix(left_pair[0], right_pair[0], dims)
        + mix(left_pair[0], right_pair[1], dims)
        + mix(left_pair[1], right_pair[0], dims)
    )


def expand_block(index_rows, value_rows, width):
    freq = lax.broadcasted_iota(jnp.int32, (BLOCK, width), 0)
    dense = jnp.zeros((BLOCK, width), jnp.float32)
    for j in range(KEEP):
        dense = jnp.where(index_rows[j] == freq, value_rows[j], dense)
    return dense


def spread_row(tile, row):
    return jnp.broadcast_to(tile[row : row + 1, :], (PACK, LANES)).astype(jnp.bfloat16)


def expand_tile(indices, values, dense, first, cols):
    freq = lax.broadcasted_iota(jnp.int32, (PACK, LANES), 0).astype(jnp.float32)
    for half in range(2):
        at = [spread_row(indices, half * KEEP + j) for j in range(KEEP)]
        have = [spread_row(values, half * KEEP + j) for j in range(KEEP)]
        for part in range(BLOCK // PACK):
            here = (freq + part * PACK).astype(jnp.bfloat16)
            tile = jnp.zeros((PACK, LANES), jnp.bfloat16)
            for j in range(KEEP):
                tile = jnp.where(at[j] == here, have[j], tile)
            start = first + half * BLOCK + part * PACK
            dense[start : start + PACK, cols] = tile


def four_products(cots, toks):
    total = jnp.dot(cots[0], toks[0], preferred_element_type=jnp.float32)
    for c, t in zip(cots[1:], toks[1:]):
        total += jnp.dot(c, t, preferred_element_type=jnp.float32)
    return total


def cot_of(message):
    return message[:, :TOK]


def tok_of(message):
    return jnp.concatenate([message[:TOK, TOK:], message[TOK:, TOK:]], axis=1)


def pack_first_kernel(where, cot, t0, t1, t2, t3, to_up, to_down, far, mine):
    turned = cot[...].T
    for out, t in ((to_up, t1), (to_down, t3)):
        out[:, :TOK] = turned
        out[:TOK, TOK:] = t[:, :TOK]
        out[TOK:, TOK:] = t[:, TOK:]
    far[...] = t2[...]
    mine[...] = t0[...]


def pack_second_kernel(cot, late_lo, late_hi, out):
    out[...] = cot[...].T


def pack_own_kernel(where, t0, t1, t2, t3, late, to_up, to_down, mine):
    to_up[:TOK, :] = t1[...]
    to_up[TOK:, :] = t2[...]
    to_down[...] = t3[...]
    mine[...] = t0[...]


def partial_first_kernel(sent, hi, far, lo, t0, t2, idx, early, out):
    cots = (cot_of(sent), cot_of(hi), far[...], cot_of(lo))
    toks = (t0[...], tok_of(hi), t2[...], tok_of(lo))
    out[:HALF, :] = four_products(cots, toks).astype(out.dtype)
    out[HALF:, :] = idx[...].astype(jnp.float32).astype(out.dtype)


def partial_second_kernel(c0, c1, c2, c3, t0, hi, t2, lo, out):
    cots = (c0[...], c1[...], c2[...], c3[...])
    out[...] = four_products(cots, (t0[...], tok_of(hi), t2[...], tok_of(lo))).astype(out.dtype)


def own_kernel(sent, a1, a2, a3, b0, b1, b2, b3, t0, t1, t2, t3, mom, out):
    step = pl.program_id(0)
    toks = (t0[...], t1[...], t2[...], t3[...])

    @pl.when(step < STEPS // 2)
    def _():
        cots = (sent[:, :TOK], a1[:, :TOK], a2[...], a3[:, :TOK])
        out[...] = four_products(cots, toks) + beta_decay * mom[...].T

    @pl.when(step >= STEPS // 2)
    def _():
        cots = (b0[...], b1[...], b2[...], b3[...])
        out[...] = four_products(cots, toks) + beta_decay * mom[...].T


def received(got_a, got_b):
    first = pl.program_id(0) < STEPS // 2
    return jnp.where(first, got_a[...], got_b[...]).astype(jnp.float32)


def pick_kernel(pre, got_a, got_b, idx, ch, cl, late, picked, tiles):
    moment = pre[...] + received(got_a, got_b)
    spectrum = three_pass((ch[...], cl[...]), split_pair(moment), ((1,), (0,)))
    freq = lax.broadcasted_iota(jnp.int32, (BLOCK, ROWS), 0)
    rows = []
    for b in range(GROUP // BLOCK):
        part = spectrum[b * BLOCK : (b + 1) * BLOCK, :]
        for j in range(KEEP):
            at = idx[b * KEEP + j : b * KEEP + j + 1, :]
            rows.append(jnp.sum(jnp.where(at == freq, part, 0.0), axis=0, keepdims=True))
    values = jnp.concatenate(rows, axis=0)
    picked[...] = values
    for t in range(GROUP // BLOCK * KEEP // 8):
        for q in range(ROWS // LANES):
            tile = values[t * 8 : (t + 1) * 8, q * LANES : (q + 1) * LANES]
            tiles[t * (ROWS // LANES) + q] = tile.astype(tiles.dtype)


def share_kernel(spread, late, out):
    total = jnp.sum(spread[...].astype(jnp.float32), axis=0, keepdims=True)
    out[...] = jnp.broadcast_to(total, out.shape).astype(out.dtype)


def residual_kernel(pre, got_a, got_b, picked, idx, ch, cl, late, out):
    parts = []
    for b in range(GROUP // BLOCK):
        rows = [slice(b * KEEP + j, b * KEEP + j + 1) for j in range(KEEP)]
        parts.append(expand_block([idx[r, :] for r in rows], [picked[r, :] for r in rows], ROWS))
    kept = jnp.concatenate(parts, axis=0)
    back = three_pass((ch[...], cl[...]), split_pair(kept), ((0,), (0,)))
    out[...] = (pre[...] + received(got_a, got_b) - back).T


def base_far_kernel(where, own, peer, w_own, w_peer, idx, got_a, to_up, to_down):
    total = jnp.dot(own[...], w_own[...], preferred_element_type=jnp.float32)
    total += jnp.dot(peer[...], w_peer[...], preferred_element_type=jnp.float32)
    low = total.astype(to_up.dtype)
    mine = idx[...].astype(jnp.float32).astype(jnp.bfloat16)
    theirs = got_a[HALF:, :]
    first = where[0] == 0
    left, right = jnp.where(first, mine, theirs), jnp.where(first, theirs, mine)
    for out, rows in ((to_up, low[:FAR]), (to_down, low[FAR:])):
        out[:FAR, :] = rows
        out[FAR:, :ROWS] = left
        out[FAR:, ROWS:] = right


def base_near_kernel(o0, o1, o3, p0, first_hi, first_lo, w_own, w_peer, lo, hi, late, base, to_up, to_down):
    def product(own, peer):
        total = jnp.dot(own[...], w_own[...], preferred_element_type=jnp.float32)
        return total + jnp.dot(peer, w_peer[...], preferred_element_type=jnp.float32)

    base[...] = product(o0, p0[...])
    total = product(o1, tok_of(first_hi))
    to_up[:FAR, :] = (total[:FAR] + lo[:FAR, :].astype(jnp.float32)).astype(to_up.dtype)
    to_up[FAR:TOK, :] = total[FAR:].astype(to_up.dtype)
    to_up[TOK:, :] = lo[FAR:, :]
    total = product(o3, tok_of(first_lo))
    to_down[:FAR, :] = total[:FAR].astype(to_down.dtype)
    to_down[FAR:, :] = (total[FAR:] + hi[:FAR, :].astype(jnp.float32)).astype(to_down.dtype)


def forward_kernel(where, tok, base, own, near_hi, near_lo, lo, hi, tot, weight, ch, cl, out, out_weight, dense, mixed):
    step = pl.program_id(0)
    near = jnp.where(step == 0, own[FAR:, :], near_hi[FAR:, :])
    away = jnp.where(step == 2, lo[TOK:, :], near_lo[FAR:, :])
    pairs = jnp.where(step < 2, near, away).astype(jnp.float32)

    @pl.when(step == 0)
    def _():
        mixed[...] = jnp.zeros_like(mixed)

    for g in range(STEPS):
        for t in range(2 * g, 2 * g + 2):
            for f in range(2):
                for q in range(ROWS // LANES):
                    cols = slice(f * ROWS + q * LANES, f * ROWS + (q + 1) * LANES)
                    values = tot[t * (ROWS // LANES) + q, f].astype(jnp.float32)
                    expand_tile(pairs[t * 8 : (t + 1) * 8, cols], values, dense, t * 2 * BLOCK, cols)
        span = slice(g * GROUP, (g + 1) * GROUP)
        mixed[span, :] += mix(dense[span, :], tok[...], ((1,), (1,)))

    @pl.when(step == 0)
    def _():
        cols = pl.ds(pl.multiple_of((where[0] & 1) * ROWS, ROWS), ROWS)
        for g in range(STEPS):
            span = slice(g * GROUP, (g + 1) * GROUP)
            turned = dense[span, cols].T
            delta = mix(turned, ch[...], ((1,), (0,))) + mix(turned, cl[...], ((1,), (0,)))
            new = weight[:, span].astype(jnp.float32) - (step_rate / REPS) * delta
            out_weight[:, span] = new.astype(out_weight.dtype)

    @pl.when(step == 3)
    def _():
        for g in range(STEPS):
            span = slice(g * GROUP, (g + 1) * GROUP)
            delta = three_pass(split_pair(mixed[span, :].T), (ch[...], cl[...]), ((1,), (0,)))
            near = lo[:TOK, span].astype(jnp.float32) + hi[:, span].astype(jnp.float32)
            out[:, span] = (base[:, span] + near - (step_rate / REPS) * delta).astype(out.dtype)


def params():
    return pltpu.CompilerParams(vmem_limit_bytes=VMEM_LIMIT)


def cost(flops, mib):
    return pl.CostEstimate(flops=int(flops), bytes_accessed=int(mib * (1 << 20)), transcendentals=0)


def whole(*shape):
    return pl.BlockSpec(shape, lambda c, *_: (0,) * len(shape))


def by_row(rows, width):
    return pl.BlockSpec((rows, width), lambda c: (c, 0))


def by_col(rows, width):
    return pl.BlockSpec((rows, width), lambda c: (0, c))


def first_half(rows, width):
    return pl.BlockSpec((rows, width), lambda c: (jnp.minimum(c, STEPS // 2 - 1), 0))


def second_half(rows, width):
    return pl.BlockSpec((rows, width), lambda c: (jnp.maximum(c - STEPS // 2, 0), 0))


AFTER = pl.BlockSpec(memory_space=pl.ANY)
BASIS = [whole(GROUP, GROUP)] * 2
GOT = [first_half(GROUP, ROWS), second_half(GROUP, ROWS)]
BF16, F32 = jnp.bfloat16, jnp.float32


def body(tokens, cotangent, weight, momentum, kept_index):
    basis = dct_group()
    high = jnp.asarray(basis).astype(BF16)
    low = (jnp.asarray(basis) - high.astype(F32)).astype(BF16)
    fsdp = lax.axis_index("fsdp").astype(jnp.int32)
    y, side = fsdp >> 1, fsdp & 1
    other = 1 - side
    index_t = jnp.transpose(kept_index, (1, 2, 0)).reshape(PICKS, ROWS)

    plus = [(i, (i + 2) % 8) for i in range(8)]
    minus = [(i, (i + 6) % 8) for i in range(8)]
    across = [(i, (i + 4) % 8) for i in range(8)]
    swap = [(i, i ^ 1) for i in range(8)]

    def up(x):
        return lax.ppermute(x, "fsdp", plus)

    def down(x):
        return lax.ppermute(x, "fsdp", minus)

    weight_peer = lax.ppermute(weight, "fsdp", swap)

    def columns():
        return [pl.BlockSpec((TOK, ROWS), lambda c, s, d=d: (0, (s[0] + 2 * d) & 7)) for d in range(4)]

    first_up, first_down, far_send, peer_0 = pl.pallas_call(
        pack_first_kernel,
        grid_spec=pltpu.PrefetchScalarGridSpec(
            num_scalar_prefetch=1,
            grid=(1,),
            in_specs=[whole(TOK, HALF)] + columns(),
            out_specs=[whole(HALF, 2 * TOK)] * 2 + [whole(TOK, ROWS)] * 2,
        ),
        out_shape=[jax.ShapeDtypeStruct((HALF, 2 * TOK), BF16)] * 2
        + [jax.ShapeDtypeStruct((TOK, ROWS), BF16)] * 2,
        compiler_params=params(),
        cost_estimate=cost(0, 3),
    )((fsdp ^ 1).reshape(1), cotangent, tokens, tokens, tokens, tokens)
    first_lo = up(first_up)
    first_hi = down(first_down)
    peer_far = down(down(far_send))
    a_far = up(first_lo[:, :TOK])

    cot_b = pl.pallas_call(
        pack_second_kernel,
        grid=(1,),
        in_specs=[pl.BlockSpec((TOK, HALF), lambda c: (0, 1)), AFTER, AFTER],
        out_specs=whole(HALF, TOK),
        out_shape=jax.ShapeDtypeStruct((HALF, TOK), BF16),
        compiler_params=params(),
        cost_estimate=cost(0, 1),
    )(cotangent, first_lo, first_hi)
    b_lo = up(cot_b)
    b_hi = down(cot_b)
    b_far = down(b_hi)
    cots_b = (cot_b, b_hi, b_far, b_lo)

    own_up, own_down, own_0 = pl.pallas_call(
        pack_own_kernel,
        grid_spec=pltpu.PrefetchScalarGridSpec(
            num_scalar_prefetch=1,
            grid=(1,),
            in_specs=columns() + [AFTER],
            out_specs=[whole(2 * TOK, ROWS), whole(TOK, ROWS), whole(TOK, ROWS)],
        ),
        out_shape=[
            jax.ShapeDtypeStruct((2 * TOK, ROWS), BF16),
            jax.ShapeDtypeStruct((TOK, ROWS), BF16),
            jax.ShapeDtypeStruct((TOK, ROWS), BF16),
        ],
        compiler_params=params(),
        cost_estimate=cost(0, 2),
    )(fsdp.reshape(1), tokens, tokens, tokens, tokens, b_lo)
    own_lo = up(own_up)
    own_hi = down(own_down)
    own_far = up(own_lo[TOK:])
    owns = (own_0, own_hi, own_far, own_lo)

    partial_a = pl.pallas_call(
        partial_first_kernel,
        grid=(1,),
        in_specs=[whole(HALF, 2 * TOK)] * 2
        + [whole(HALF, TOK), whole(HALF, 2 * TOK)]
        + [whole(TOK, ROWS)] * 2
        + [whole(PICKS, ROWS), AFTER],
        out_specs=whole(HALF + PICKS, ROWS),
        out_shape=jax.ShapeDtypeStruct((HALF + PICKS, ROWS), BF16),
        compiler_params=params(),
        cost_estimate=cost(KV * KV * ROWS, 3),
    )(first_up, first_hi, a_far, first_lo, peer_0, peer_far, index_t, weight_peer)
    got_a = lax.ppermute(partial_a, "fsdp", swap)
    partial_b = pl.pallas_call(
        partial_second_kernel,
        grid=(1,),
        in_specs=[whole(HALF, TOK)] * 4
        + [whole(TOK, ROWS), whole(HALF, 2 * TOK), whole(TOK, ROWS), whole(HALF, 2 * TOK)],
        out_specs=whole(HALF, ROWS),
        out_shape=jax.ShapeDtypeStruct((HALF, ROWS), BF16),
        compiler_params=params(),
        cost_estimate=cost(KV * KV * ROWS, 3),
    )(*cots_b, peer_0, first_hi, peer_far, first_lo)
    got_b = lax.ppermute(partial_b, "fsdp", swap)

    pre = pl.pallas_call(
        own_kernel,
        grid=(STEPS,),
        in_specs=[first_half(GROUP, 2 * TOK)] * 2
        + [first_half(GROUP, TOK), first_half(GROUP, 2 * TOK)]
        + [second_half(GROUP, TOK)] * 4
        + [whole(TOK, ROWS)] * 4
        + [by_col(ROWS, GROUP)],
        out_specs=by_row(GROUP, ROWS),
        out_shape=jax.ShapeDtypeStruct((KV, ROWS), F32),
        compiler_params=params(),
        cost_estimate=cost(2 * KV * KV * ROWS, 7),
    )(first_up, first_hi, a_far, first_lo, *cots_b, *owns, momentum[0])

    far_up, far_down = pl.pallas_call(
        base_far_kernel,
        grid_spec=pltpu.PrefetchScalarGridSpec(
            num_scalar_prefetch=1,
            grid=(1,),
            in_specs=[whole(TOK, ROWS)] * 2
            + [whole(ROWS, KV)] * 2
            + [whole(PICKS, ROWS), whole(HALF + PICKS, ROWS)],
            out_specs=[whole(FAR + PICKS, KV)] * 2,
        ),
        out_shape=[jax.ShapeDtypeStruct((FAR + PICKS, KV), BF16)] * 2,
        compiler_params=params(),
        cost_estimate=cost(KV * KV * ROWS, 4),
    )(side.reshape(1), own_far, peer_far, weight, weight_peer, index_t, got_a)
    far_lo = up(far_up)
    far_hi = down(far_down)

    picked, tiles = pl.pallas_call(
        pick_kernel,
        grid=(STEPS,),
        in_specs=[by_row(GROUP, ROWS)] + GOT + [by_row(PICKS // STEPS, ROWS)] + BASIS + [AFTER],
        out_specs=[
            by_row(PICKS // STEPS, ROWS),
            pl.BlockSpec((REPS // STEPS, 8, LANES), lambda c: (c, 0, 0)),
        ],
        out_shape=[
            jax.ShapeDtypeStruct((PICKS, ROWS), F32),
            jax.ShapeDtypeStruct((REPS, 8, LANES), BF16),
        ],
        compiler_params=params(),
        cost_estimate=cost(6 * KV * GROUP * ROWS, 4),
    )(pre, got_a, got_b, index_t, high, low, far_up)

    base, near_up, near_down = pl.pallas_call(
        base_near_kernel,
        grid=(1,),
        in_specs=[whole(TOK, ROWS)] * 4
        + [whole(HALF, 2 * TOK)] * 2
        + [whole(ROWS, KV)] * 2
        + [whole(FAR + PICKS, KV)] * 2 + [AFTER],
        out_specs=[whole(TOK, KV), whole(TOK + PICKS, KV), whole(TOK, KV)],
        out_shape=[
            jax.ShapeDtypeStruct((TOK, KV), F32),
            jax.ShapeDtypeStruct((TOK + PICKS, KV), BF16),
            jax.ShapeDtypeStruct((TOK, KV), BF16),
        ],
        compiler_params=params(),
        cost_estimate=cost(3 * KV * KV * ROWS, 7),
    )(own_0, own_hi, own_lo, peer_0, first_hi, first_lo, weight, weight_peer, far_lo, far_hi, tiles)
    near_lo = up(near_up)
    near_hi = down(near_down)

    spread = lax.all_to_all(tiles, "rep", 0, 0)
    copies = pl.pallas_call(
        share_kernel,
        grid=(1,),
        in_specs=[whole(REPS, 8, LANES), AFTER],
        out_specs=whole(REPS * 8, 8, LANES),
        out_shape=jax.ShapeDtypeStruct((REPS * 8, 8, LANES), BF16),
        compiler_params=params(),
        cost_estimate=cost(0, 1),
    )(spread, near_down)
    totals = lax.all_to_all(copies, ("rep", "fsdp"), 0, 0).reshape(REPS, 8, 8, LANES)

    new_momentum = pl.pallas_call(
        residual_kernel,
        grid=(STEPS,),
        in_specs=[by_row(GROUP, ROWS)] + GOT + [by_row(PICKS // STEPS, ROWS)] * 2 + BASIS + [AFTER],
        out_specs=by_col(ROWS, GROUP),
        out_shape=jax.ShapeDtypeStruct((ROWS, KV), F32),
        compiler_params=params(),
        cost_estimate=cost(6 * KV * GROUP * ROWS, 6),
    )(pre, got_a, got_b, picked, index_t, high, low, copies)

    projected, new_weight = pl.pallas_call(
        forward_kernel,
        grid_spec=pltpu.PrefetchScalarGridSpec(
            num_scalar_prefetch=1,
            grid=(4,),
            in_specs=[pl.BlockSpec((TOK, 2 * ROWS), lambda c, s: (0, ((s[0] >> 1) + c) & 3))]
            + [whole(TOK, KV)]
            + [whole(FAR + PICKS, KV)] * 3
            + [whole(TOK + PICKS, KV), whole(TOK, KV)]
            + [pl.BlockSpec((REPS, 2, 8, LANES), lambda c, s: (0, ((s[0] >> 1) + c) & 3, 0, 0))]
            + [whole(ROWS, KV)]
            + BASIS,
            out_specs=[whole(TOK, KV), whole(ROWS, KV)],
            scratch_shapes=[pltpu.VMEM((KV, 2 * ROWS), BF16), pltpu.VMEM((KV, TOK), F32)],
        ),
        out_shape=[
            jax.ShapeDtypeStruct((TOK, KV), BF16),
            jax.ShapeDtypeStruct((ROWS, KV), BF16),
        ],
        compiler_params=params(),
        cost_estimate=cost(8 * KV * KV * ROWS, 8),
    )(fsdp.reshape(1), tokens, base, far_up, far_hi, far_lo, near_lo, near_hi, totals, weight, high, low)
    return (projected, new_weight, new_momentum[None])


def solution(mesh):
    in_specs = (
        P(("rep", "fsdp"), None),
        P(("rep", "fsdp"), None),
        P("fsdp", None),
        P("rep", "fsdp", None),
        P("fsdp", None, None),
    )
    out_specs = (P(("rep", "fsdp"), None), P("fsdp", None), P("rep", "fsdp", None))
    return jax.shard_map(body, mesh=mesh, in_specs=in_specs, out_specs=out_specs, check_vma=False)
```

```python
import jax
import jax.numpy as jnp
import numpy as np
from jax import lax
from jax.experimental import pallas as pl
from jax.experimental.pallas import tpu as pltpu
from jax.sharding import PartitionSpec as P

beta_decay = 0.9
step_rate = 0.5
ROWS = 512
KV = 1024
TOK = 256
BLOCK = 64
KEEP = 4
HALF = KV // 2
GROUP = 256
STEPS = KV // GROUP
PICKS = KV // BLOCK * KEEP
LANES = 128
PACK = 16
REPS = 32
VMEM_LIMIT = 16 * 1024 * 1024
VMEM_MOST = 60 * 1024 * 1024


def dct_group():
    n = np.arange(BLOCK, dtype=np.float64)
    single = np.cos(np.pi * (2.0 * n[None, :] + 1.0) * n[:, None] / (2 * BLOCK))
    single *= np.where(n[:, None] == 0, np.sqrt(1.0 / BLOCK), np.sqrt(2.0 / BLOCK))
    return np.kron(np.eye(GROUP // BLOCK), single).astype(np.float32)


def split_pair(values):
    high = values.astype(jnp.bfloat16)
    return high, (values - high.astype(jnp.float32)).astype(jnp.bfloat16)


def mix(left, right, dims):
    return lax.dot_general(left, right, (dims, ((), ())), preferred_element_type=jnp.float32)


def three_pass(left_pair, right_pair, dims):
    return (
        mix(left_pair[0], right_pair[0], dims)
        + mix(left_pair[0], right_pair[1], dims)
        + mix(left_pair[1], right_pair[0], dims)
    )


def expand_block(index_rows, value_rows, width):
    freq = lax.broadcasted_iota(jnp.int32, (BLOCK, width), 0)
    dense = jnp.zeros((BLOCK, width), jnp.float32)
    for j in range(KEEP):
        dense = jnp.where(index_rows[j] == freq, value_rows[j], dense)
    return dense


def spread_row(tile, row):
    return jnp.broadcast_to(tile[row : row + 1, :], (PACK, LANES)).astype(jnp.bfloat16)


def expand_tile(indices, values, dense, first, cols):
    freq = lax.broadcasted_iota(jnp.int32, (PACK, LANES), 0).astype(jnp.float32)
    for half in range(2):
        at = [spread_row(indices, half * KEEP + j) for j in range(KEEP)]
        have = [spread_row(values, half * KEEP + j) for j in range(KEEP)]
        for part in range(BLOCK // PACK):
            here = (freq + part * PACK).astype(jnp.bfloat16)
            tile = jnp.zeros((PACK, LANES), jnp.bfloat16)
            for j in range(KEEP):
                tile = jnp.where(at[j] == here, have[j], tile)
            start = first + half * BLOCK + part * PACK
            dense[start : start + PACK, cols] = tile


def four_products(cots, toks):
    total = jnp.dot(cots[0], toks[0], preferred_element_type=jnp.float32)
    for c, t in zip(cots[1:], toks[1:]):
        total += jnp.dot(c, t, preferred_element_type=jnp.float32)
    return total


def cot_of(message):
    return message[:, :TOK]


def tok_of(message):
    return jnp.concatenate([message[:TOK, TOK:], message[TOK:, TOK:]], axis=1)


def flat_index(idx):
    rows = [idx[b].astype(jnp.float32) for b in range(KV // BLOCK)]
    return jnp.concatenate(rows, axis=0).astype(jnp.bfloat16)


def pack_first_kernel(where, cot, t0, t1, t2, t3, to_up, to_far, to_down, mine):
    turned = cot[...].T
    for out, t in ((to_up, t1), (to_far, t2), (to_down, t3)):
        out[:, :TOK] = turned
        out[:TOK, TOK:] = t[:, :TOK]
        out[TOK:, TOK:] = t[:, TOK:]
    mine[...] = t0[...]


def pack_second_kernel(cot, late_lo, late_hi, out):
    out[...] = cot[...].T


def pack_own_kernel(where, t0, t1, t2, t3, late_lo, late_hi, mine, to_up, to_far, to_down):
    for out, t in ((mine, t0), (to_up, t1), (to_far, t2), (to_down, t3)):
        out[...] = t[...]


def partial_first_kernel(sent, hi, far, lo, t0, idx, early, turned, out):
    cots = (cot_of(sent), cot_of(hi), cot_of(far), cot_of(lo))
    toks = (t0[...], tok_of(hi), tok_of(far), tok_of(lo))
    out[:HALF, :] = four_products(cots, toks).astype(out.dtype)
    out[HALF:, :] = flat_index(idx)


def partial_second_kernel(c0, c1, c2, c3, t0, hi, far, lo, out):
    cots = (c0[...], c1[...], c2[...], c3[...])
    toks = (t0[...], tok_of(hi), tok_of(far), tok_of(lo))
    out[...] = four_products(cots, toks).astype(out.dtype)


def own_kernel(a0, a1, a2, a3, b0, b1, b2, b3, t0, t1, t2, t3, mom, out):
    step = pl.program_id(0)
    toks = (t0[...], t1[...], t2[...], t3[...])

    @pl.when(step < STEPS // 2)
    def _():
        cots = (cot_of(a0), cot_of(a1), cot_of(a2), cot_of(a3))
        out[...] = four_products(cots, toks) + beta_decay * mom[...].T

    @pl.when(step >= STEPS // 2)
    def _():
        cots = (b0[...], b1[...], b2[...], b3[...])
        out[...] = four_products(cots, toks) + beta_decay * mom[...].T


def pick_rows(moment, idx, ch, cl):
    spectrum = three_pass((ch[...], cl[...]), split_pair(moment), ((1,), (0,)))
    freq = lax.broadcasted_iota(jnp.int32, (BLOCK, ROWS), 0)
    rows = []
    for b in range(GROUP // BLOCK):
        part = spectrum[b * BLOCK : (b + 1) * BLOCK, :]
        for j in range(KEEP):
            here = idx[b, j : j + 1, :] == freq
            rows.append(jnp.sum(jnp.where(here, part, 0.0), axis=0, keepdims=True))
    return rows


def pick_kernel(pre, got_a, got_b, idx, ch, cl, late, moment, tiles):
    first = pl.program_id(0) < STEPS // 2
    got = jnp.where(first, got_a[...], got_b[...]).astype(jnp.float32)
    total = pre[...] + got
    moment[...] = total
    values = jnp.concatenate(pick_rows(total, idx, ch, cl), axis=0)
    for t in range(GROUP // BLOCK * KEEP // 8):
        for q in range(ROWS // LANES):
            tile = values[t * 8 : (t + 1) * 8, q * LANES : (q + 1) * LANES]
            tiles[t * (ROWS // LANES) + q] = tile.astype(tiles.dtype)


def share_kernel(spread, late_0, late_1, late_2, out):
    total = jnp.sum(spread[...].astype(jnp.float32), axis=0, keepdims=True)
    out[...] = jnp.broadcast_to(total, out.shape).astype(out.dtype)


def residual_kernel(moment, idx, ch, cl, late, out):
    total = moment[...]
    rows = pick_rows(total, idx, ch, cl)
    parts = []
    for b in range(GROUP // BLOCK):
        at = [idx[b, j : j + 1, :] for j in range(KEEP)]
        parts.append(expand_block(at, rows[b * KEEP : (b + 1) * KEEP], ROWS))
    kept = jnp.concatenate(parts, axis=0)
    back = three_pass((ch[...], cl[...]), split_pair(kept), ((0,), (0,)))
    out[...] = (total - back).T


def base_kernel(where, o0, o1, o2, o3, p0, p1, p2, p3, w_own, w_peer, idx, got_a, *outs):
    mine, theirs = flat_index(idx), got_a[HALF:, :]
    first = (where[0] & 1) == 0
    left, right = jnp.where(first, mine, theirs), jnp.where(first, theirs, mine)
    peers = (p0[...], tok_of(p1), tok_of(p2), tok_of(p3))
    for own, peer, out in zip((o0, o1, o2, o3), peers, outs):
        total = jnp.dot(own[...], w_own[...], preferred_element_type=jnp.float32)
        total += jnp.dot(peer, w_peer[...], preferred_element_type=jnp.float32)
        out[:TOK, :] = total.astype(out.dtype)
        out[TOK:, :ROWS] = left
        out[TOK:, ROWS:] = right


def forward_kernel(where, tok, own, hi, far, lo, tot, weight, ch, cl, out, out_weight, dense, mixed):
    step = pl.program_id(0)
    tail = slice(TOK, TOK + PICKS)
    near = jnp.where(step == 0, own[tail, :], hi[tail, :])
    away = jnp.where(step == 2, far[tail, :], lo[tail, :])
    pairs = jnp.where(step < 2, near, away).astype(jnp.float32)

    @pl.when(step == 0)
    def _():
        mixed[...] = jnp.zeros_like(mixed)

    for g in range(STEPS):
        for t in range(2 * g, 2 * g + 2):
            for f in range(2):
                for q in range(ROWS // LANES):
                    cols = slice(f * ROWS + q * LANES, f * ROWS + (q + 1) * LANES)
                    values = tot[t * (ROWS // LANES) + q, f].astype(jnp.float32)
                    expand_tile(pairs[t * 8 : (t + 1) * 8, cols], values, dense, t * 2 * BLOCK, cols)
        span = slice(g * GROUP, (g + 1) * GROUP)
        mixed[span, :] += mix(dense[span, :], tok[...], ((1,), (1,)))

    @pl.when(step == 0)
    def _():
        cols = pl.ds(pl.multiple_of((where[0] & 1) * ROWS, ROWS), ROWS)
        for g in range(STEPS):
            span = slice(g * GROUP, (g + 1) * GROUP)
            turned = dense[span, cols].T
            delta = mix(turned, ch[...], ((1,), (0,))) + mix(turned, cl[...], ((1,), (0,)))
            new = weight[:, span].astype(jnp.float32) - (step_rate / REPS) * delta
            out_weight[:, span] = new.astype(out_weight.dtype)

    @pl.when(step == 3)
    def _():
        for g in range(STEPS):
            span = slice(g * GROUP, (g + 1) * GROUP)
            delta = three_pass(split_pair(mixed[span, :].T), (ch[...], cl[...]), ((1,), (0,)))
            base = own[:TOK, span].astype(jnp.float32) + hi[:TOK, span].astype(jnp.float32)
            base += far[:TOK, span].astype(jnp.float32) + lo[:TOK, span].astype(jnp.float32)
            out[:, span] = (base - (step_rate / REPS) * delta).astype(out.dtype)


def params(limit=VMEM_LIMIT):
    return pltpu.CompilerParams(vmem_limit_bytes=limit)


def cost(flops, mib):
    return pl.CostEstimate(flops=int(flops), bytes_accessed=int(mib * (1 << 20)), transcendentals=0)


def whole(*shape):
    return pl.BlockSpec(shape, lambda c, *_: (0,) * len(shape))


def by_row(rows, width):
    return pl.BlockSpec((rows, width), lambda c: (c, 0))


def by_col(rows, width):
    return pl.BlockSpec((rows, width), lambda c: (0, c))


def first_half(rows, width):
    return pl.BlockSpec((rows, width), lambda c: (jnp.minimum(c, STEPS // 2 - 1), 0))


def second_half(rows, width):
    return pl.BlockSpec((rows, width), lambda c: (jnp.maximum(c - STEPS // 2, 0), 0))


AFTER = pl.BlockSpec(memory_space=pl.ANY)
BASIS = [whole(GROUP, GROUP)] * 2
GOT = [first_half(GROUP, ROWS), second_half(GROUP, ROWS)]
BF16, F32 = jnp.bfloat16, jnp.float32
INDEX = pl.BlockSpec((KV // BLOCK, KEEP, ROWS), lambda c, *_: (0, 0, 0))
INDEX_STEP = pl.BlockSpec((GROUP // BLOCK, KEEP, ROWS), lambda c: (c, 0, 0))
MESSAGE = whole(HALF, 2 * TOK)
PIECE = whole(TOK, ROWS)


def shape(*dims, dtype=BF16):
    return jax.ShapeDtypeStruct(dims, dtype)


def body(tokens, cotangent, weight, momentum, kept_index):
    basis = dct_group()
    high = jnp.asarray(basis).astype(BF16)
    low = (jnp.asarray(basis) - high.astype(F32)).astype(BF16)
    place = lax.axis_index("fsdp").astype(jnp.int32).reshape(1)
    index_t = jnp.transpose(kept_index, (1, 2, 0))

    def up(x):
        return lax.ppermute(x, "fsdp", [(i, (i + 2) % 8) for i in range(8)])

    def down(x):
        return lax.ppermute(x, "fsdp", [(i, (i + 6) % 8) for i in range(8)])

    def across(x):
        return lax.ppermute(x, "fsdp", [(i, (i + 4) % 8) for i in range(8)])

    def swap(x):
        return lax.ppermute(x, "fsdp", [(i, i ^ 1) for i in range(8)])

    def columns(flip):
        return [pl.BlockSpec((TOK, ROWS), lambda c, s, d=d: (0, ((s[0] ^ flip) + 2 * d) & 7)) for d in range(4)]

    weight_peer = swap(weight)

    first_up, first_far, first_down, peer_0 = pl.pallas_call(
        pack_first_kernel,
        grid_spec=pltpu.PrefetchScalarGridSpec(
            num_scalar_prefetch=1,
            grid=(1,),
            in_specs=[whole(TOK, HALF)] + columns(1),
            out_specs=[MESSAGE] * 3 + [PIECE],
        ),
        out_shape=[shape(HALF, 2 * TOK)] * 3 + [shape(TOK, ROWS)],
        compiler_params=params(),
        cost_estimate=cost(0, 4),
    )(place, cotangent, tokens, tokens, tokens, tokens)
    first_lo = up(first_up)
    first_hi = down(first_down)
    first_x = across(first_far)
    firsts = (first_up, first_hi, first_x, first_lo)

    cot_b = pl.pallas_call(
        pack_second_kernel,
        grid=(1,),
        in_specs=[pl.BlockSpec((TOK, HALF), lambda c: (0, 1)), AFTER, AFTER],
        out_specs=whole(HALF, TOK),
        out_shape=shape(HALF, TOK),
        compiler_params=params(),
        cost_estimate=cost(0, 1),
    )(cotangent, first_lo, first_hi)
    b_lo, b_hi, b_far = up(cot_b), down(cot_b), across(cot_b)
    cots_b = (cot_b, b_hi, b_far, b_lo)

    own_0, own_up, own_across, own_down = pl.pallas_call(
        pack_own_kernel,
        grid_spec=pltpu.PrefetchScalarGridSpec(
            num_scalar_prefetch=1,
            grid=(1,),
            in_specs=columns(0) + [AFTER, AFTER],
            out_specs=[PIECE] * 4,
        ),
        out_shape=[shape(TOK, ROWS)] * 4,
        compiler_params=params(),
        cost_estimate=cost(0, 2),
    )(place, tokens, tokens, tokens, tokens, b_lo, b_hi)
    owns = (own_0, down(own_down), across(own_across), up(own_up))

    partial_a = pl.pallas_call(
        partial_first_kernel,
        grid=(1,),
        in_specs=[MESSAGE] * 4 + [PIECE, INDEX, AFTER, AFTER],
        out_specs=whole(HALF + PICKS, ROWS),
        out_shape=shape(HALF + PICKS, ROWS),
        compiler_params=params(),
        cost_estimate=cost(KV * KV * ROWS, 3),
    )(*firsts, peer_0, index_t, weight_peer, cot_b)
    got_a = swap(partial_a)
    partial_b = pl.pallas_call(
        partial_second_kernel,
        grid=(1,),
        in_specs=[whole(HALF, TOK)] * 4 + [PIECE] + [MESSAGE] * 3,
        out_specs=whole(HALF, ROWS),
        out_shape=shape(HALF, ROWS),
        compiler_params=params(),
        cost_estimate=cost(KV * KV * ROWS, 3),
    )(*cots_b, peer_0, *firsts[1:])
    got_b = swap(partial_b)

    pre = pl.pallas_call(
        own_kernel,
        grid=(STEPS,),
        in_specs=[first_half(GROUP, 2 * TOK)] * 4
        + [second_half(GROUP, TOK)] * 4
        + [PIECE] * 4
        + [by_col(ROWS, GROUP)],
        out_specs=by_row(GROUP, ROWS),
        out_shape=shape(KV, ROWS, dtype=F32),
        compiler_params=params(),
        cost_estimate=cost(2 * KV * KV * ROWS, 7),
    )(*firsts, *cots_b, *owns, momentum[0])

    base, base_up, base_across, base_down = pl.pallas_call(
        base_kernel,
        grid_spec=pltpu.PrefetchScalarGridSpec(
            num_scalar_prefetch=1,
            grid=(1,),
            in_specs=[PIECE] * 5
            + [MESSAGE] * 3
            + [whole(ROWS, KV)] * 2
            + [INDEX, whole(HALF + PICKS, ROWS)],
            out_specs=[whole(TOK + PICKS, KV)] * 4,
        ),
        out_shape=[shape(TOK + PICKS, KV)] * 4,
        compiler_params=params(2 * VMEM_LIMIT),
        cost_estimate=cost(4 * KV * KV * ROWS, 7),
    )(place, *owns, peer_0, *firsts[1:], weight, weight_peer, index_t, got_a)
    base_lo, base_hi, base_far = up(base_up), down(base_down), across(base_across)

    moment, tiles = pl.pallas_call(
        pick_kernel,
        grid=(STEPS,),
        in_specs=[by_row(GROUP, ROWS)] + GOT + [INDEX_STEP] + BASIS + [AFTER],
        out_specs=[by_row(GROUP, ROWS), pl.BlockSpec((REPS // STEPS, 8, LANES), lambda c: (c, 0, 0))],
        out_shape=[shape(KV, ROWS, dtype=F32), shape(REPS, 8, LANES)],
        compiler_params=params(),
        cost_estimate=cost(6 * KV * GROUP * ROWS, 6),
    )(pre, got_a, got_b, index_t, high, low, base)

    spread = lax.all_to_all(tiles, "rep", 0, 0)
    copies = pl.pallas_call(
        share_kernel,
        grid=(1,),
        in_specs=[whole(REPS, 8, LANES), AFTER, AFTER, AFTER],
        out_specs=whole(REPS * 8, 8, LANES),
        out_shape=shape(REPS * 8, 8, LANES),
        compiler_params=params(),
        cost_estimate=cost(0, 1),
    )(spread, base_lo, base_hi, base_far)
    totals = lax.all_to_all(copies, ("rep", "fsdp"), 0, 0).reshape(REPS, 8, 8, LANES)

    new_momentum = pl.pallas_call(
        residual_kernel,
        grid=(STEPS,),
        in_specs=[by_row(GROUP, ROWS), INDEX_STEP] + BASIS + [AFTER],
        out_specs=by_col(ROWS, GROUP),
        out_shape=shape(ROWS, KV, dtype=F32),
        compiler_params=params(VMEM_MOST),
        cost_estimate=cost(12 * KV * GROUP * ROWS, 5),
    )(moment, index_t, high, low, copies)

    projected, new_weight = pl.pallas_call(
        forward_kernel,
        grid_spec=pltpu.PrefetchScalarGridSpec(
            num_scalar_prefetch=1,
            grid=(4,),
            in_specs=[pl.BlockSpec((TOK, 2 * ROWS), lambda c, s: (0, ((s[0] >> 1) + c) & 3))]
            + [whole(TOK + PICKS, KV)] * 4
            + [pl.BlockSpec((REPS, 2, 8, LANES), lambda c, s: (0, ((s[0] >> 1) + c) & 3, 0, 0))]
            + [whole(ROWS, KV)]
            + BASIS,
            out_specs=[whole(TOK, KV), whole(ROWS, KV)],
            scratch_shapes=[pltpu.VMEM((KV, 2 * ROWS), BF16), pltpu.VMEM((KV, TOK), F32)],
        ),
        out_shape=[shape(TOK, KV), shape(ROWS, KV)],
        compiler_params=params(VMEM_MOST),
        cost_estimate=cost(8 * KV * KV * ROWS, 8),
    )(place, tokens, base, base_hi, base_far, base_lo, totals, weight, high, low)
    return (projected, new_weight, new_momentum[None])


def solution(mesh):
    in_specs = (
        P(("rep", "fsdp"), None),
        P(("rep", "fsdp"), None),
        P("fsdp", None),
        P("rep", "fsdp", None),
        P("fsdp", None, None),
    )
    out_specs = (P(("rep", "fsdp"), None), P("fsdp", None), P("rep", "fsdp", None))
    return jax.shard_map(body, mesh=mesh, in_specs=in_specs, out_specs=out_specs, check_vma=False)
```

```python
import jax
import jax.numpy as jnp
import numpy as np
from jax import lax
from jax.experimental import pallas as pl
from jax.experimental.pallas import tpu as pltpu
from jax.sharding import PartitionSpec as P

beta_decay = 0.9
step_rate = 0.5
ROWS = 512
KV = 1024
TOK = 256
BLOCK = 64
KEEP = 4
HALF = KV // 2
GROUP = 256
STEPS = KV // GROUP
PICKS = KV // BLOCK * KEEP
LANES = 128
PACK = 16
REPS = 32
TILES = PICKS * ROWS // (8 * LANES)
VMEM_LIMIT = 16 * 1024 * 1024


def dct_group():
    n = np.arange(BLOCK, dtype=np.float64)
    single = np.cos(np.pi * (2.0 * n[None, :] + 1.0) * n[:, None] / (2 * BLOCK))
    single *= np.where(n[:, None] == 0, np.sqrt(1.0 / BLOCK), np.sqrt(2.0 / BLOCK))
    return np.kron(np.eye(GROUP // BLOCK), single).astype(np.float32)


def split_pair(values):
    high = values.astype(jnp.bfloat16)
    return high, (values - high.astype(jnp.float32)).astype(jnp.bfloat16)


def mix(left, right, dims):
    return lax.dot_general(left, right, (dims, ((), ())), preferred_element_type=jnp.float32)


def three_pass(left_pair, right_pair, dims):
    return (
        mix(left_pair[0], right_pair[0], dims)
        + mix(left_pair[0], right_pair[1], dims)
        + mix(left_pair[1], right_pair[0], dims)
    )


def expand_block(index_rows, value_rows, width):
    freq = lax.broadcasted_iota(jnp.int32, (BLOCK, width), 0)
    dense = jnp.zeros((BLOCK, width), jnp.float32)
    for j in range(KEEP):
        dense = jnp.where(index_rows[j] == freq, value_rows[j], dense)
    return dense


def spread_row(tile, row):
    return jnp.broadcast_to(tile[row : row + 1, :], (PACK, LANES)).astype(jnp.bfloat16)


def expand_tile(indices, values, dense, first, cols):
    freq = lax.broadcasted_iota(jnp.int32, (PACK, LANES), 0).astype(jnp.float32)
    for half in range(2):
        at = [spread_row(indices, half * KEEP + j) for j in range(KEEP)]
        have = [spread_row(values, half * KEEP + j) for j in range(KEEP)]
        for part in range(BLOCK // PACK):
            here = (freq + part * PACK).astype(jnp.bfloat16)
            tile = jnp.zeros((PACK, LANES), jnp.bfloat16)
            for j in range(KEEP):
                tile = jnp.where(at[j] == here, have[j], tile)
            start = first + half * BLOCK + part * PACK
            dense[start : start + PACK, cols] = tile


def four_products(cots, toks):
    total = jnp.dot(cots[0], toks[0], preferred_element_type=jnp.float32)
    for c, t in zip(cots[1:], toks[1:]):
        total += jnp.dot(c, t, preferred_element_type=jnp.float32)
    return total


def cot_of(message):
    return message[:, :TOK]


def tok_of(message):
    return jnp.concatenate([message[:TOK, TOK:], message[TOK:, TOK:]], axis=1)


def flat_index(idx):
    rows = [idx[b].astype(jnp.float32) for b in range(KV // BLOCK)]
    return jnp.concatenate(rows, axis=0).astype(jnp.bfloat16)


def pack_first_kernel(where, cot, t0, t1, t2, t3, to_up, to_far, to_down, mine):
    turned = cot[...].T
    for out, t in ((to_up, t1), (to_far, t2), (to_down, t3)):
        out[:, :TOK] = turned
        out[:TOK, TOK:] = t[:, :TOK]
        out[TOK:, TOK:] = t[:, TOK:]
    mine[...] = t0[...]


def pack_second_kernel(cot, late_lo, late_hi, out):
    out[...] = cot[...].T


def pack_own_kernel(where, t0, t1, t2, t3, late_lo, late_hi, mine, to_up, to_far, to_down):
    for out, t in ((mine, t0), (to_up, t1), (to_far, t2), (to_down, t3)):
        out[...] = t[...]


def partial_first_kernel(sent, hi, far, lo, t0, idx, early, turned, out):
    cots = (cot_of(sent), cot_of(hi), cot_of(far), cot_of(lo))
    toks = (t0[...], tok_of(hi), tok_of(far), tok_of(lo))
    out[:HALF, :] = four_products(cots, toks).astype(out.dtype)
    out[HALF:, :] = flat_index(idx)


def partial_second_kernel(c0, c1, c2, c3, t0, hi, far, lo, out):
    cots = (c0[...], c1[...], c2[...], c3[...])
    toks = (t0[...], tok_of(hi), tok_of(far), tok_of(lo))
    out[...] = four_products(cots, toks).astype(out.dtype)


def own_kernel(a0, a1, a2, a3, b0, b1, b2, b3, t0, t1, t2, t3, mom, out):
    step = pl.program_id(0)
    toks = (t0[...], t1[...], t2[...], t3[...])

    @pl.when(step < STEPS // 2)
    def _():
        cots = (cot_of(a0), cot_of(a1), cot_of(a2), cot_of(a3))
        out[...] = four_products(cots, toks) + beta_decay * mom[...].T

    @pl.when(step >= STEPS // 2)
    def _():
        cots = (b0[...], b1[...], b2[...], b3[...])
        out[...] = four_products(cots, toks) + beta_decay * mom[...].T


def pick_rows(moment, idx, ch, cl):
    spectrum = three_pass((ch[...], cl[...]), split_pair(moment), ((1,), (0,)))
    freq = lax.broadcasted_iota(jnp.int32, (BLOCK, ROWS), 0)
    rows = []
    for b in range(GROUP // BLOCK):
        part = spectrum[b * BLOCK : (b + 1) * BLOCK, :]
        for j in range(KEEP):
            here = idx[b, j : j + 1, :] == freq
            rows.append(jnp.sum(jnp.where(here, part, 0.0), axis=0, keepdims=True))
    return rows


def pick_kernel(where, pre, got_a, got_b, idx, ch, cl, late, moment, picked, keep, send):
    step = pl.program_id(0)
    first = step < STEPS // 2
    got = jnp.where(first, got_a[...], got_b[...]).astype(jnp.float32)
    total = pre[...] + got
    moment[...] = total
    values = jnp.concatenate(pick_rows(total, idx, ch, cl), axis=0)
    picked[...] = values

    def put(out):
        for t in range(GROUP // BLOCK * KEEP // 8):
            for q in range(ROWS // LANES):
                tile = values[t * 8 : (t + 1) * 8, q * LANES : (q + 1) * LANES]
                out[(step & 1) * (TILES // STEPS) + t * (ROWS // LANES) + q] = tile

    here = (step >> 1) == (where[1] & 1)
    pl.when(here)(lambda: put(keep))
    pl.when(jnp.logical_not(here))(lambda: put(send))


def add_two_kernel(a, b, out):
    out[...] = (a[...] + b[...]).astype(out.dtype)


def add_four_kernel(a, b, c, d, out):
    out[...] = (a[...] + b[...]) + (c[...] + d[...])


def pair_kernel(where, half, core, across, corner, late_0, late_1, late_2, out):
    side, mine = where[0] & 1, (where[1] & 1) * (TILES // 2)
    other = TILES // 2 - mine
    out[side, pl.ds(mine, TILES // 2)] = half[...]
    out[side, pl.ds(other, TILES // 2)] = core[...]
    out[1 - side, pl.ds(mine, TILES // 2)] = across[...]
    out[1 - side, pl.ds(other, TILES // 2)] = corner[...]


def residual_kernel(moment, picked, idx, ch, cl, late, out):
    parts = []
    for b in range(GROUP // BLOCK):
        at = [idx[b, j : j + 1, :] for j in range(KEEP)]
        have = [picked[b * KEEP + j : b * KEEP + j + 1, :] for j in range(KEEP)]
        parts.append(expand_block(at, have, ROWS))
    kept = jnp.concatenate(parts, axis=0)
    back = three_pass((ch[...], cl[...]), split_pair(kept), ((0,), (0,)))
    out[...] = (moment[...] - back).T


def base_kernel(where, o0, o1, o2, o3, p0, p1, p2, p3, w_own, w_peer, idx, got_a, *outs):
    mine, theirs = flat_index(idx), got_a[HALF:, :]
    first = (where[0] & 1) == 0
    left, right = jnp.where(first, mine, theirs), jnp.where(first, theirs, mine)
    peers = (p0[...], tok_of(p1), tok_of(p2), tok_of(p3))
    for own, peer, out in zip((o0, o1, o2, o3), peers, outs):
        total = jnp.dot(own[...], w_own[...], preferred_element_type=jnp.float32)
        total += jnp.dot(peer, w_peer[...], preferred_element_type=jnp.float32)
        out[:TOK, :] = total.astype(out.dtype)
        out[TOK:, :ROWS] = left
        out[TOK:, ROWS:] = right


def expand_group(g, pairs, tot, dense):
    for t in range(2 * g, 2 * g + 2):
        for f in range(2):
            for q in range(ROWS // LANES):
                cols = slice(f * ROWS + q * LANES, f * ROWS + (q + 1) * LANES)
                values = tot[f, t * (ROWS // LANES) + q].astype(jnp.float32)
                expand_tile(pairs[t * 8 : (t + 1) * 8, cols], values, dense, t * 2 * BLOCK, cols)


def forward_own_kernel(where, tok, own, tot, weight, ch, cl, mixed, out_weight, dense):
    pairs = own[TOK:, :].astype(jnp.float32)
    cols = pl.ds(pl.multiple_of((where[0] & 1) * ROWS, ROWS), ROWS)
    for g in range(STEPS):
        expand_group(g, pairs, tot, dense)
        span = slice(g * GROUP, (g + 1) * GROUP)
        mixed[span, :] = mix(dense[span, :], tok[...], ((1,), (1,)))
        turned = dense[span, cols].T
        delta = mix(turned, ch[...], ((1,), (0,))) + mix(turned, cl[...], ((1,), (0,)))
        new = weight[:, span].astype(jnp.float32) - (step_rate / REPS) * delta
        out_weight[:, span] = new.astype(out_weight.dtype)


def forward_kernel(where, tok_1, tok_2, tok_3, own, hi, far, lo, tot_1, tot_2, tot_3, mixed, ch, cl, out, *dense):
    pairs = [near[TOK:, :].astype(jnp.float32) for near in (hi, far, lo)]
    for g in range(STEPS):
        span = slice(g * GROUP, (g + 1) * GROUP)
        total = mixed[span, :]
        for tok, index, tot, buffer in zip((tok_1, tok_2, tok_3), pairs, (tot_1, tot_2, tot_3), dense):
            expand_group(g, index, tot, buffer)
            total += mix(buffer[span, :], tok[...], ((1,), (1,)))
        delta = three_pass(split_pair(total.T), (ch[...], cl[...]), ((1,), (0,)))
        base = own[:TOK, span].astype(jnp.float32) + hi[:TOK, span].astype(jnp.float32)
        base += far[:TOK, span].astype(jnp.float32) + lo[:TOK, span].astype(jnp.float32)
        out[:, span] = (base - (step_rate / REPS) * delta).astype(out.dtype)


def params(limit=VMEM_LIMIT):
    return pltpu.CompilerParams(vmem_limit_bytes=limit)


def cost(flops, mib):
    return pl.CostEstimate(flops=int(flops), bytes_accessed=int(mib * (1 << 20)), transcendentals=0)


def whole(*shape):
    return pl.BlockSpec(shape, lambda c, *_: (0,) * len(shape))


def by_row(rows, width):
    return pl.BlockSpec((rows, width), lambda c, *_: (c, 0))


def by_col(rows, width):
    return pl.BlockSpec((rows, width), lambda c, *_: (0, c))


def first_half(rows, width):
    return pl.BlockSpec((rows, width), lambda c, *_: (jnp.minimum(c, STEPS // 2 - 1), 0))


def second_half(rows, width):
    return pl.BlockSpec((rows, width), lambda c, *_: (jnp.maximum(c - STEPS // 2, 0), 0))


AFTER = pl.BlockSpec(memory_space=pl.ANY)
BASIS = [whole(GROUP, GROUP)] * 2
GOT = [first_half(GROUP, ROWS), second_half(GROUP, ROWS)]
BF16, F32 = jnp.bfloat16, jnp.float32
INDEX = pl.BlockSpec((KV // BLOCK, KEEP, ROWS), lambda c, *_: (0, 0, 0))
INDEX_STEP = pl.BlockSpec((GROUP // BLOCK, KEEP, ROWS), lambda c, *_: (c, 0, 0))
MESSAGE = whole(HALF, 2 * TOK)
PIECE = whole(TOK, ROWS)


def shape(*dims, dtype=BF16):
    return jax.ShapeDtypeStruct(dims, dtype)


def body(tokens, cotangent, weight, momentum, kept_index):
    basis = dct_group()
    high = jnp.asarray(basis).astype(BF16)
    low = (jnp.asarray(basis) - high.astype(F32)).astype(BF16)
    place = jnp.stack([lax.axis_index("fsdp"), lax.axis_index("rep")]).astype(jnp.int32)
    index_t = jnp.transpose(kept_index, (1, 2, 0))

    def up(x):
        return lax.ppermute(x, "fsdp", [(i, (i + 2) % 8) for i in range(8)])

    def down(x):
        return lax.ppermute(x, "fsdp", [(i, (i + 6) % 8) for i in range(8)])

    def across(x):
        return lax.ppermute(x, "fsdp", [(i, (i + 4) % 8) for i in range(8)])

    def swap(x):
        return lax.ppermute(x, "fsdp", [(i, i ^ 1) for i in range(8)])

    def columns(flip):
        return [pl.BlockSpec((TOK, ROWS), lambda c, s, d=d: (0, ((s[0] ^ flip) + 2 * d) & 7)) for d in range(4)]

    weight_peer = swap(weight)

    first_up, first_far, first_down, peer_0 = pl.pallas_call(
        pack_first_kernel,
        grid_spec=pltpu.PrefetchScalarGridSpec(
            num_scalar_prefetch=1,
            grid=(1,),
            in_specs=[whole(TOK, HALF)] + columns(1),
            out_specs=[MESSAGE] * 3 + [PIECE],
        ),
        out_shape=[shape(HALF, 2 * TOK)] * 3 + [shape(TOK, ROWS)],
        compiler_params=params(),
        cost_estimate=cost(0, 4),
    )(place, cotangent, tokens, tokens, tokens, tokens)
    first_lo = up(first_up)
    first_hi = down(first_down)
    first_x = across(first_far)
    firsts = (first_up, first_hi, first_x, first_lo)

    cot_b = pl.pallas_call(
        pack_second_kernel,
        grid=(1,),
        in_specs=[pl.BlockSpec((TOK, HALF), lambda c: (0, 1)), AFTER, AFTER],
        out_specs=whole(HALF, TOK),
        out_shape=shape(HALF, TOK),
        compiler_params=params(),
        cost_estimate=cost(0, 1),
    )(cotangent, first_lo, first_hi)
    b_lo, b_hi, b_far = up(cot_b), down(cot_b), across(cot_b)
    cots_b = (cot_b, b_hi, b_far, b_lo)

    own_0, own_up, own_across, own_down = pl.pallas_call(
        pack_own_kernel,
        grid_spec=pltpu.PrefetchScalarGridSpec(
            num_scalar_prefetch=1,
            grid=(1,),
            in_specs=columns(0) + [AFTER, AFTER],
            out_specs=[PIECE] * 4,
        ),
        out_shape=[shape(TOK, ROWS)] * 4,
        compiler_params=params(),
        cost_estimate=cost(0, 2),
    )(place, tokens, tokens, tokens, tokens, b_lo, b_hi)
    owns = (own_0, down(own_down), across(own_across), up(own_up))

    partial_a = pl.pallas_call(
        partial_first_kernel,
        grid=(1,),
        in_specs=[MESSAGE] * 4 + [PIECE, INDEX, AFTER, AFTER],
        out_specs=whole(HALF + PICKS, ROWS),
        out_shape=shape(HALF + PICKS, ROWS),
        compiler_params=params(),
        cost_estimate=cost(KV * KV * ROWS, 3),
    )(*firsts, peer_0, index_t, weight_peer, cot_b)
    got_a = swap(partial_a)
    partial_b = pl.pallas_call(
        partial_second_kernel,
        grid=(1,),
        in_specs=[whole(HALF, TOK)] * 4 + [PIECE] + [MESSAGE] * 3,
        out_specs=whole(HALF, ROWS),
        out_shape=shape(HALF, ROWS),
        compiler_params=params(),
        cost_estimate=cost(KV * KV * ROWS, 3),
    )(*cots_b, peer_0, *firsts[1:])
    got_b = swap(partial_b)

    pre = pl.pallas_call(
        own_kernel,
        grid=(STEPS,),
        in_specs=[first_half(GROUP, 2 * TOK)] * 4
        + [second_half(GROUP, TOK)] * 4
        + [PIECE] * 4
        + [by_col(ROWS, GROUP)],
        out_specs=by_row(GROUP, ROWS),
        out_shape=shape(KV, ROWS, dtype=F32),
        compiler_params=params(),
        cost_estimate=cost(2 * KV * KV * ROWS, 7),
    )(*firsts, *cots_b, *owns, momentum[0])

    base, base_up, base_across, base_down = pl.pallas_call(
        base_kernel,
        grid_spec=pltpu.PrefetchScalarGridSpec(
            num_scalar_prefetch=1,
            grid=(1,),
            in_specs=[PIECE] * 5
            + [MESSAGE] * 3
            + [whole(ROWS, KV)] * 2
            + [INDEX, whole(HALF + PICKS, ROWS)],
            out_specs=[whole(TOK + PICKS, KV)] * 4,
        ),
        out_shape=[shape(TOK + PICKS, KV)] * 4,
        compiler_params=params(2 * VMEM_LIMIT),
        cost_estimate=cost(4 * KV * KV * ROWS, 7),
    )(place, *owns, peer_0, *firsts[1:], weight, weight_peer, index_t, got_a)
    base_lo, base_hi, base_far = up(base_up), down(base_down), across(base_across)

    halves = whole(TILES // 2, 8, LANES)
    half_shape = shape(TILES // 2, 8, LANES, dtype=F32)
    moment, picked, keep, send = pl.pallas_call(
        pick_kernel,
        grid_spec=pltpu.PrefetchScalarGridSpec(
            num_scalar_prefetch=1,
            grid=(STEPS,),
            in_specs=[by_row(GROUP, ROWS)] + GOT + [INDEX_STEP] + BASIS + [AFTER],
            out_specs=[by_row(GROUP, ROWS), by_row(PICKS // STEPS, ROWS), halves, halves],
        ),
        out_shape=[shape(KV, ROWS, dtype=F32), shape(PICKS, ROWS, dtype=F32), half_shape, half_shape],
        compiler_params=params(),
        cost_estimate=cost(6 * KV * GROUP * ROWS, 6),
    )(place, pre, got_a, got_b, index_t, high, low, base)

    def partner(x, bits):
        return lax.ppermute(x, "rep", [(i, i ^ bits) for i in range(REPS)])

    def add(kernel, result, *parts):
        return pl.pallas_call(
            kernel,
            grid=(1,),
            in_specs=[halves] * len(parts),
            out_specs=halves,
            out_shape=result,
            compiler_params=params(),
            cost_estimate=cost(0, 0.25),
        )(*parts)

    value = add(add_two_kernel, half_shape, keep, partner(send, 1))
    value = add(add_two_kernel, half_shape, value, partner(value, 2))
    value = add(add_four_kernel, half_shape, value, partner(value, 4), partner(value, 8), partner(value, 12))
    half = add(add_two_kernel, shape(TILES // 2, 8, LANES), value, partner(value, 16))

    corner = lax.ppermute(half, ("rep", "fsdp"), [(i, i ^ 9) for i in range(REPS * 8)])
    pair_spec = whole(2, TILES, 8, LANES)
    pair = pl.pallas_call(
        pair_kernel,
        grid_spec=pltpu.PrefetchScalarGridSpec(
            num_scalar_prefetch=1,
            grid=(1,),
            in_specs=[halves] * 4 + [AFTER] * 3,
            out_specs=pair_spec,
        ),
        out_shape=shape(2, TILES, 8, LANES),
        compiler_params=params(),
        cost_estimate=cost(0, 0.25),
    )(place, half, partner(half, 1), swap(half), corner, base_lo, base_hi, base_far)
    pair_far, pair_lo, pair_hi = across(pair), up(pair), down(pair)

    def token_block(d):
        return pl.BlockSpec((TOK, 2 * ROWS), lambda c, s: (0, ((s[0] >> 1) + d) & 3))

    mixed, new_weight = pl.pallas_call(
        forward_own_kernel,
        grid_spec=pltpu.PrefetchScalarGridSpec(
            num_scalar_prefetch=1,
            grid=(1,),
            in_specs=[token_block(0), whole(TOK + PICKS, KV), pair_spec, whole(ROWS, KV)] + BASIS,
            out_specs=[whole(KV, TOK), whole(ROWS, KV)],
            scratch_shapes=[pltpu.VMEM((KV, 2 * ROWS), BF16)],
        ),
        out_shape=[shape(KV, TOK, dtype=F32), shape(ROWS, KV)],
        compiler_params=params(),
        cost_estimate=cost(3 * KV * KV * ROWS, 4),
    )(place, tokens, base, pair, weight, high, low)

    new_momentum = pl.pallas_call(
        residual_kernel,
        grid=(STEPS,),
        in_specs=[by_row(GROUP, ROWS), by_row(PICKS // STEPS, ROWS), INDEX_STEP] + BASIS + [AFTER],
        out_specs=by_col(ROWS, GROUP),
        out_shape=shape(ROWS, KV, dtype=F32),
        compiler_params=params(),
        cost_estimate=cost(6 * KV * GROUP * ROWS, 5),
    )(moment, picked, index_t, high, low, pair)

    projected = pl.pallas_call(
        forward_kernel,
        grid_spec=pltpu.PrefetchScalarGridSpec(
            num_scalar_prefetch=1,
            grid=(1,),
            in_specs=[token_block(d) for d in (1, 2, 3)]
            + [whole(TOK + PICKS, KV)] * 4
            + [pair_spec] * 3
            + [whole(KV, TOK)]
            + BASIS,
            out_specs=whole(TOK, KV),
            scratch_shapes=[pltpu.VMEM((KV, 2 * ROWS), BF16)] * 3,
        ),
        out_shape=shape(TOK, KV),
        compiler_params=params(2 * VMEM_LIMIT),
        cost_estimate=cost(6 * KV * KV * ROWS, 7),
    )(place, tokens, tokens, tokens, base, base_hi, base_far, base_lo, pair_hi, pair_far, pair_lo, mixed, high, low)
    return (projected, new_weight, new_momentum[None])


def solution(mesh):
    in_specs = (
        P(("rep", "fsdp"), None),
        P(("rep", "fsdp"), None),
        P("fsdp", None),
        P("rep", "fsdp", None),
        P("fsdp", None, None),
    )
    out_specs = (P(("rep", "fsdp"), None), P("fsdp", None), P("rep", "fsdp", None))
    return jax.shard_map(body, mesh=mesh, in_specs=in_specs, out_specs=out_specs, check_vma=False)
```

```python
import jax
import jax.numpy as jnp
import numpy as np
from jax import lax
from jax.experimental import pallas as pl
from jax.experimental.pallas import tpu as pltpu
from jax.sharding import PartitionSpec as P

beta_decay = 0.9
step_rate = 0.5
ROWS = 512
KV = 1024
TOK = 256
BLOCK = 64
KEEP = 4
HALF = KV // 2
GROUP = 256
STEPS = KV // GROUP
PICKS = KV // BLOCK * KEEP
LANES = 128
PACK = 16
REPS = 32
TILES = PICKS * ROWS // (8 * LANES)
VMEM_LIMIT = 16 * 1024 * 1024


def dct_group():
    n = np.arange(BLOCK, dtype=np.float64)
    single = np.cos(np.pi * (2.0 * n[None, :] + 1.0) * n[:, None] / (2 * BLOCK))
    single *= np.where(n[:, None] == 0, np.sqrt(1.0 / BLOCK), np.sqrt(2.0 / BLOCK))
    return np.kron(np.eye(GROUP // BLOCK), single).astype(np.float32)


def split_pair(values):
    high = values.astype(jnp.bfloat16)
    return high, (values - high.astype(jnp.float32)).astype(jnp.bfloat16)


def mix(left, right, dims):
    return lax.dot_general(left, right, (dims, ((), ())), preferred_element_type=jnp.float32)


def three_pass(left_pair, right_pair, dims):
    return (
        mix(left_pair[0], right_pair[0], dims)
        + mix(left_pair[0], right_pair[1], dims)
        + mix(left_pair[1], right_pair[0], dims)
    )


def expand_block(index_rows, value_rows, width):
    freq = lax.broadcasted_iota(jnp.int32, (BLOCK, width), 0)
    dense = jnp.zeros((BLOCK, width), jnp.float32)
    for j in range(KEEP):
        dense = jnp.where(index_rows[j] == freq, value_rows[j], dense)
    return dense


def spread_row(tile, row):
    return jnp.broadcast_to(tile[row : row + 1, :], (PACK, LANES)).astype(jnp.bfloat16)


def expand_tile(indices, values, dense, first, cols):
    freq = lax.broadcasted_iota(jnp.int32, (PACK, LANES), 0).astype(jnp.float32)
    for half in range(2):
        at = [spread_row(indices, half * KEEP + j) for j in range(KEEP)]
        have = [spread_row(values, half * KEEP + j) for j in range(KEEP)]
        for part in range(BLOCK // PACK):
            here = (freq + part * PACK).astype(jnp.bfloat16)
            tile = jnp.zeros((PACK, LANES), jnp.bfloat16)
            for j in range(KEEP):
                tile = jnp.where(at[j] == here, have[j], tile)
            start = first + half * BLOCK + part * PACK
            dense[start : start + PACK, cols] = tile


def four_products(cots, toks):
    total = jnp.dot(cots[0], toks[0], preferred_element_type=jnp.float32)
    for c, t in zip(cots[1:], toks[1:]):
        total += jnp.dot(c, t, preferred_element_type=jnp.float32)
    return total


def cot_of(message):
    return message[:, :TOK]


def tok_of(message):
    return jnp.concatenate([message[:TOK, TOK:], message[TOK:, TOK:]], axis=1)


def flat_index(idx):
    rows = [idx[b].astype(jnp.float32) for b in range(KV // BLOCK)]
    return jnp.concatenate(rows, axis=0).astype(jnp.bfloat16)


def pack_first_kernel(where, cot, t0, t1, t2, t3, to_up, to_far, to_down, mine):
    turned = cot[...].T
    for out, t in ((to_up, t1), (to_far, t2), (to_down, t3)):
        out[:, :TOK] = turned
        out[:TOK, TOK:] = t[:, :TOK]
        out[TOK:, TOK:] = t[:, TOK:]
    mine[...] = t0[...]


def pack_second_kernel(cot, late_lo, late_hi, out):
    out[...] = cot[...].T


def pack_own_kernel(where, t0, t1, t2, t3, late, turned, mine, to_up, to_far, to_down):
    for out, t in ((mine, t0), (to_up, t1), (to_far, t2), (to_down, t3)):
        out[...] = t[...]


def partial_first_kernel(sent, hi, far, lo, t0, idx, early, turned, out):
    cots = (cot_of(sent), cot_of(hi), cot_of(far), cot_of(lo))
    toks = (t0[...], tok_of(hi), tok_of(far), tok_of(lo))
    out[:HALF, :] = four_products(cots, toks).astype(out.dtype)
    out[HALF:, :] = flat_index(idx)


def partial_second_kernel(c0, c1, c2, c3, t0, hi, far, lo, out):
    cots = (c0[...], c1[...], c2[...], c3[...])
    toks = (t0[...], tok_of(hi), tok_of(far), tok_of(lo))
    out[...] = four_products(cots, toks).astype(out.dtype)


def own_kernel(a0, a1, a2, a3, b0, b1, b2, b3, t0, t1, t2, t3, mom, out):
    step = pl.program_id(0)
    toks = (t0[...], t1[...], t2[...], t3[...])

    @pl.when(step < STEPS // 2)
    def _():
        cots = (cot_of(a0), cot_of(a1), cot_of(a2), cot_of(a3))
        out[...] = four_products(cots, toks) + beta_decay * mom[...].T

    @pl.when(step >= STEPS // 2)
    def _():
        cots = (b0[...], b1[...], b2[...], b3[...])
        out[...] = four_products(cots, toks) + beta_decay * mom[...].T


def pick_rows(moment, idx, ch, cl):
    spectrum = three_pass((ch[...], cl[...]), split_pair(moment), ((1,), (0,)))
    freq = lax.broadcasted_iota(jnp.int32, (BLOCK, ROWS), 0)
    rows = []
    for b in range(GROUP // BLOCK):
        part = spectrum[b * BLOCK : (b + 1) * BLOCK, :]
        for j in range(KEEP):
            here = idx[b, j : j + 1, :] == freq
            rows.append(jnp.sum(jnp.where(here, part, 0.0), axis=0, keepdims=True))
    return rows


def pick_kernel(where, pre, got_a, got_b, idx, ch, cl, moment, picked, keep, send):
    step = pl.program_id(0)
    first = step < STEPS // 2
    got = jnp.where(first, got_a[...], got_b[...]).astype(jnp.float32)
    total = pre[...] + got
    moment[...] = total
    values = jnp.concatenate(pick_rows(total, idx, ch, cl), axis=0)
    picked[...] = values

    def put(out):
        for t in range(GROUP // BLOCK * KEEP // 8):
            for q in range(ROWS // LANES):
                tile = values[t * 8 : (t + 1) * 8, q * LANES : (q + 1) * LANES]
                out[(step & 1) * (TILES // STEPS) + t * (ROWS // LANES) + q] = tile

    here = (step >> 1) == (where[1] & 1)
    pl.when(here)(lambda: put(keep))
    pl.when(jnp.logical_not(here))(lambda: put(send))


def add_two_kernel(a, b, late, out):
    out[...] = (a[...] + b[...]).astype(out.dtype)


def add_four_kernel(a, b, c, d, late, out):
    out[...] = (a[...] + b[...]) + (c[...] + d[...])


def pair_kernel(where, half, core, across, corner, late_0, late_1, late_2, out):
    side, mine = where[0] & 1, (where[1] & 1) * (TILES // 2)
    other = TILES // 2 - mine
    out[side, pl.ds(mine, TILES // 2)] = half[...]
    out[side, pl.ds(other, TILES // 2)] = core[...]
    out[1 - side, pl.ds(mine, TILES // 2)] = across[...]
    out[1 - side, pl.ds(other, TILES // 2)] = corner[...]


def residual_kernel(moment, picked, idx, ch, cl, late, out, mark):
    parts = []
    for b in range(GROUP // BLOCK):
        at = [idx[b, j : j + 1, :] for j in range(KEEP)]
        have = [picked[b * KEEP + j : b * KEEP + j + 1, :] for j in range(KEEP)]
        parts.append(expand_block(at, have, ROWS))
    kept = jnp.concatenate(parts, axis=0)
    back = three_pass((ch[...], cl[...]), split_pair(kept), ((0,), (0,)))
    out[...] = (moment[...] - back).T
    mark[...] = back[:8, :LANES]


def base_kernel(where, o0, o1, o2, o3, p0, p1, p2, p3, w_own, w_peer, idx, got_a, late, *outs):
    mine, theirs = flat_index(idx), got_a[HALF:, :]
    first = (where[0] & 1) == 0
    left, right = jnp.where(first, mine, theirs), jnp.where(first, theirs, mine)
    peers = (p0[...], tok_of(p1), tok_of(p2), tok_of(p3))
    for own, peer, out in zip((o0, o1, o2, o3), peers, outs):
        total = jnp.dot(own[...], w_own[...], preferred_element_type=jnp.float32)
        total += jnp.dot(peer, w_peer[...], preferred_element_type=jnp.float32)
        out[:TOK, :] = total.astype(out.dtype)
        out[TOK:, :ROWS] = left
        out[TOK:, ROWS:] = right


def expand_group(g, pairs, tot, dense):
    for t in range(2 * g, 2 * g + 2):
        for f in range(2):
            for q in range(ROWS // LANES):
                cols = slice(f * ROWS + q * LANES, f * ROWS + (q + 1) * LANES)
                values = tot[f, t * (ROWS // LANES) + q].astype(jnp.float32)
                expand_tile(pairs[t * 8 : (t + 1) * 8, cols], values, dense, t * 2 * BLOCK, cols)


def forward_own_kernel(where, tok, own, tot, weight, ch, cl, mixed, out_weight, dense):
    pairs = own[TOK:, :].astype(jnp.float32)
    cols = pl.ds(pl.multiple_of((where[0] & 1) * ROWS, ROWS), ROWS)
    for g in range(STEPS):
        expand_group(g, pairs, tot, dense)
        span = slice(g * GROUP, (g + 1) * GROUP)
        mixed[span, :] = mix(dense[span, :], tok[...], ((1,), (1,)))
        turned = dense[span, cols].T
        delta = mix(turned, ch[...], ((1,), (0,))) + mix(turned, cl[...], ((1,), (0,)))
        new = weight[:, span].astype(jnp.float32) - (step_rate / REPS) * delta
        out_weight[:, span] = new.astype(out_weight.dtype)


def forward_kernel(where, tok_1, tok_2, tok_3, own, hi, far, lo, tot_1, tot_2, tot_3, mixed, ch, cl, out, *dense):
    pairs = [near[TOK:, :].astype(jnp.float32) for near in (hi, far, lo)]
    for g in range(STEPS):
        span = slice(g * GROUP, (g + 1) * GROUP)
        total = mixed[span, :]
        for tok, index, tot, buffer in zip((tok_1, tok_2, tok_3), pairs, (tot_1, tot_2, tot_3), dense):
            expand_group(g, index, tot, buffer)
            total += mix(buffer[span, :], tok[...], ((1,), (1,)))
        delta = three_pass(split_pair(total.T), (ch[...], cl[...]), ((1,), (0,)))
        base = own[:TOK, span].astype(jnp.float32) + hi[:TOK, span].astype(jnp.float32)
        base += far[:TOK, span].astype(jnp.float32) + lo[:TOK, span].astype(jnp.float32)
        out[:, span] = (base - (step_rate / REPS) * delta).astype(out.dtype)


def params(limit=VMEM_LIMIT):
    return pltpu.CompilerParams(vmem_limit_bytes=limit)


def cost(flops, mib):
    return pl.CostEstimate(flops=int(flops), bytes_accessed=int(mib * (1 << 20)), transcendentals=0)


def whole(*shape):
    return pl.BlockSpec(shape, lambda c, *_: (0,) * len(shape))


def by_row(rows, width):
    return pl.BlockSpec((rows, width), lambda c, *_: (c, 0))


def by_col(rows, width):
    return pl.BlockSpec((rows, width), lambda c, *_: (0, c))


def first_half(rows, width):
    return pl.BlockSpec((rows, width), lambda c, *_: (jnp.minimum(c, STEPS // 2 - 1), 0))


def second_half(rows, width):
    return pl.BlockSpec((rows, width), lambda c, *_: (jnp.maximum(c - STEPS // 2, 0), 0))


AFTER = pl.BlockSpec(memory_space=pl.ANY)
BASIS = [whole(GROUP, GROUP)] * 2
GOT = [first_half(GROUP, ROWS), second_half(GROUP, ROWS)]
BF16, F32 = jnp.bfloat16, jnp.float32
INDEX = pl.BlockSpec((KV // BLOCK, KEEP, ROWS), lambda c, *_: (0, 0, 0))
INDEX_STEP = pl.BlockSpec((GROUP // BLOCK, KEEP, ROWS), lambda c, *_: (c, 0, 0))
MESSAGE = whole(HALF, 2 * TOK)
PIECE = whole(TOK, ROWS)


def shape(*dims, dtype=BF16):
    return jax.ShapeDtypeStruct(dims, dtype)


def body(tokens, cotangent, weight, momentum, kept_index):
    basis = dct_group()
    high = jnp.asarray(basis).astype(BF16)
    low = (jnp.asarray(basis) - high.astype(F32)).astype(BF16)
    place = jnp.stack([lax.axis_index("fsdp"), lax.axis_index("rep")]).astype(jnp.int32)
    index_t = jnp.transpose(kept_index, (1, 2, 0))

    def up(x):
        return lax.ppermute(x, "fsdp", [(i, (i + 2) % 8) for i in range(8)])

    def down(x):
        return lax.ppermute(x, "fsdp", [(i, (i + 6) % 8) for i in range(8)])

    def across(x):
        return lax.ppermute(x, "fsdp", [(i, (i + 4) % 8) for i in range(8)])

    def swap(x):
        return lax.ppermute(x, "fsdp", [(i, i ^ 1) for i in range(8)])

    def columns(flip):
        return [pl.BlockSpec((TOK, ROWS), lambda c, s, d=d: (0, ((s[0] ^ flip) + 2 * d) & 7)) for d in range(4)]

    weight_peer = swap(weight)

    first_up, first_far, first_down, peer_0 = pl.pallas_call(
        pack_first_kernel,
        grid_spec=pltpu.PrefetchScalarGridSpec(
            num_scalar_prefetch=1,
            grid=(1,),
            in_specs=[whole(TOK, HALF)] + columns(1),
            out_specs=[MESSAGE] * 3 + [PIECE],
        ),
        out_shape=[shape(HALF, 2 * TOK)] * 3 + [shape(TOK, ROWS)],
        compiler_params=params(),
        cost_estimate=cost(0, 4),
    )(place, cotangent, tokens, tokens, tokens, tokens)
    first_lo = up(first_up)
    first_hi = down(first_down)
    first_x = across(first_far)
    firsts = (first_up, first_hi, first_x, first_lo)

    cot_b = pl.pallas_call(
        pack_second_kernel,
        grid=(1,),
        in_specs=[pl.BlockSpec((TOK, HALF), lambda c: (0, 1)), AFTER, AFTER],
        out_specs=whole(HALF, TOK),
        out_shape=shape(HALF, TOK),
        compiler_params=params(),
        cost_estimate=cost(0, 1),
    )(cotangent, first_lo, first_hi)
    b_lo, b_hi, b_far = up(cot_b), down(cot_b), across(cot_b)
    cots_b = (cot_b, b_hi, b_far, b_lo)

    own_0, own_up, own_across, own_down = pl.pallas_call(
        pack_own_kernel,
        grid_spec=pltpu.PrefetchScalarGridSpec(
            num_scalar_prefetch=1,
            grid=(1,),
            in_specs=columns(0) + [AFTER, AFTER],
            out_specs=[PIECE] * 4,
        ),
        out_shape=[shape(TOK, ROWS)] * 4,
        compiler_params=params(),
        cost_estimate=cost(0, 2),
    )(place, tokens, tokens, tokens, tokens, first_x, cot_b)
    owns = (own_0, down(own_down), across(own_across), up(own_up))

    partial_a = pl.pallas_call(
        partial_first_kernel,
        grid=(1,),
        in_specs=[MESSAGE] * 4 + [PIECE, INDEX, AFTER, AFTER],
        out_specs=whole(HALF + PICKS, ROWS),
        out_shape=shape(HALF + PICKS, ROWS),
        compiler_params=params(),
        cost_estimate=cost(KV * KV * ROWS, 3),
    )(*firsts, peer_0, index_t, weight_peer, cot_b)
    got_a = swap(partial_a)
    partial_b = pl.pallas_call(
        partial_second_kernel,
        grid=(1,),
        in_specs=[whole(HALF, TOK)] * 4 + [PIECE] + [MESSAGE] * 3,
        out_specs=whole(HALF, ROWS),
        out_shape=shape(HALF, ROWS),
        compiler_params=params(),
        cost_estimate=cost(KV * KV * ROWS, 3),
    )(*cots_b, peer_0, *firsts[1:])
    got_b = swap(partial_b)

    pre = pl.pallas_call(
        own_kernel,
        grid=(STEPS,),
        in_specs=[first_half(GROUP, 2 * TOK)] * 4
        + [second_half(GROUP, TOK)] * 4
        + [PIECE] * 4
        + [by_col(ROWS, GROUP)],
        out_specs=by_row(GROUP, ROWS),
        out_shape=shape(KV, ROWS, dtype=F32),
        compiler_params=params(),
        cost_estimate=cost(2 * KV * KV * ROWS, 7),
    )(*firsts, *cots_b, *owns, momentum[0])

    halves = whole(TILES // 2, 8, LANES)
    half_shape = shape(TILES // 2, 8, LANES, dtype=F32)
    moment, picked, keep, send = pl.pallas_call(
        pick_kernel,
        grid_spec=pltpu.PrefetchScalarGridSpec(
            num_scalar_prefetch=1,
            grid=(STEPS,),
            in_specs=[by_row(GROUP, ROWS)] + GOT + [INDEX_STEP] + BASIS,
            out_specs=[by_row(GROUP, ROWS), by_row(PICKS // STEPS, ROWS), halves, halves],
        ),
        out_shape=[shape(KV, ROWS, dtype=F32), shape(PICKS, ROWS, dtype=F32), half_shape, half_shape],
        compiler_params=params(),
        cost_estimate=cost(6 * KV * GROUP * ROWS, 6),
    )(place, pre, got_a, got_b, index_t, high, low)

    def partner(x, bits):
        return lax.ppermute(x, "rep", [(i, i ^ bits) for i in range(REPS)])

    from_core, from_hi, from_corner = partner(send, 1), partner(keep, 2), partner(send, 3)

    base, base_up, base_across, base_down = pl.pallas_call(
        base_kernel,
        grid_spec=pltpu.PrefetchScalarGridSpec(
            num_scalar_prefetch=1,
            grid=(1,),
            in_specs=[PIECE] * 5
            + [MESSAGE] * 3
            + [whole(ROWS, KV)] * 2
            + [INDEX, whole(HALF + PICKS, ROWS), AFTER],
            out_specs=[whole(TOK + PICKS, KV)] * 4,
        ),
        out_shape=[shape(TOK + PICKS, KV)] * 4,
        compiler_params=params(2 * VMEM_LIMIT),
        cost_estimate=cost(4 * KV * KV * ROWS, 7),
    )(place, *owns, peer_0, *firsts[1:], weight, weight_peer, index_t, got_a, from_core)
    base_lo, base_hi, base_far = up(base_up), down(base_down), across(base_across)

    def add(kernel, result, after, *parts):
        return pl.pallas_call(
            kernel,
            grid=(1,),
            in_specs=[halves] * len(parts) + [AFTER],
            out_specs=halves,
            out_shape=result,
            compiler_params=params(),
            cost_estimate=cost(0, 0.25),
        )(*parts, after)

    value = add(add_four_kernel, half_shape, base, keep, from_core, from_hi, from_corner)
    value = add(
        add_four_kernel, half_shape, keep, value, partner(value, 4), partner(value, 8), partner(value, 12)
    )
    last = partner(value, 16)
    new_momentum, mark = pl.pallas_call(
        residual_kernel,
        grid=(STEPS,),
        in_specs=[by_row(GROUP, ROWS), by_row(PICKS // STEPS, ROWS), INDEX_STEP] + BASIS + [AFTER],
        out_specs=[by_col(ROWS, GROUP), whole(8, LANES)],
        out_shape=[shape(ROWS, KV, dtype=F32), shape(8, LANES, dtype=F32)],
        compiler_params=params(),
        cost_estimate=cost(6 * KV * GROUP * ROWS, 5),
    )(moment, picked, index_t, high, low, value)
    half = add(add_two_kernel, shape(TILES // 2, 8, LANES), mark, value, last)

    corner = lax.ppermute(half, ("rep", "fsdp"), [(i, i ^ 9) for i in range(REPS * 8)])
    pair_spec = whole(2, TILES, 8, LANES)
    pair = pl.pallas_call(
        pair_kernel,
        grid_spec=pltpu.PrefetchScalarGridSpec(
            num_scalar_prefetch=1,
            grid=(1,),
            in_specs=[halves] * 4 + [AFTER] * 3,
            out_specs=pair_spec,
        ),
        out_shape=shape(2, TILES, 8, LANES),
        compiler_params=params(),
        cost_estimate=cost(0, 0.25),
    )(place, half, partner(half, 1), swap(half), corner, base_lo, base_hi, base_far)
    pair_far, pair_lo, pair_hi = across(pair), up(pair), down(pair)

    def token_block(d):
        return pl.BlockSpec((TOK, 2 * ROWS), lambda c, s: (0, ((s[0] >> 1) + d) & 3))

    mixed, new_weight = pl.pallas_call(
        forward_own_kernel,
        grid_spec=pltpu.PrefetchScalarGridSpec(
            num_scalar_prefetch=1,
            grid=(1,),
            in_specs=[token_block(0), whole(TOK + PICKS, KV), pair_spec, whole(ROWS, KV)] + BASIS,
            out_specs=[whole(KV, TOK), whole(ROWS, KV)],
            scratch_shapes=[pltpu.VMEM((KV, 2 * ROWS), BF16)],
        ),
        out_shape=[shape(KV, TOK, dtype=F32), shape(ROWS, KV)],
        compiler_params=params(),
        cost_estimate=cost(3 * KV * KV * ROWS, 4),
    )(place, tokens, base, pair, weight, high, low)

    projected = pl.pallas_call(
        forward_kernel,
        grid_spec=pltpu.PrefetchScalarGridSpec(
            num_scalar_prefetch=1,
            grid=(1,),
            in_specs=[token_block(d) for d in (1, 2, 3)]
            + [whole(TOK + PICKS, KV)] * 4
            + [pair_spec] * 3
            + [whole(KV, TOK)]
            + BASIS,
            out_specs=whole(TOK, KV),
            scratch_shapes=[pltpu.VMEM((KV, 2 * ROWS), BF16)] * 3,
        ),
        out_shape=shape(TOK, KV),
        compiler_params=params(2 * VMEM_LIMIT),
        cost_estimate=cost(6 * KV * KV * ROWS, 7),
    )(place, tokens, tokens, tokens, base, base_hi, base_far, base_lo, pair_hi, pair_far, pair_lo, mixed, high, low)
    return (projected, new_weight, new_momentum[None])


def solution(mesh):
    in_specs = (
        P(("rep", "fsdp"), None),
        P(("rep", "fsdp"), None),
        P("fsdp", None),
        P("rep", "fsdp", None),
        P("fsdp", None, None),
    )
    out_specs = (P(("rep", "fsdp"), None), P("fsdp", None), P("rep", "fsdp", None))
    return jax.shard_map(body, mesh=mesh, in_specs=in_specs, out_specs=out_specs, check_vma=False)
```

```python
import jax
import jax.numpy as jnp
import numpy as np
from jax import lax
from jax.experimental import pallas as pl
from jax.experimental.pallas import tpu as pltpu
from jax.sharding import PartitionSpec as P

beta_decay = 0.9
step_rate = 0.5
ROWS = 512
KV = 1024
TOK = 256
BLOCK = 64
KEEP = 4
HALF = KV // 2
GROUP = 256
STEPS = KV // GROUP
PICKS = KV // BLOCK * KEEP
LANES = 128
PACK = 16
REPS = 32
TILES = PICKS * ROWS // (8 * LANES)
VMEM_LIMIT = 16 * 1024 * 1024


def dct_group():
    n = np.arange(BLOCK, dtype=np.float64)
    single = np.cos(np.pi * (2.0 * n[None, :] + 1.0) * n[:, None] / (2 * BLOCK))
    single *= np.where(n[:, None] == 0, np.sqrt(1.0 / BLOCK), np.sqrt(2.0 / BLOCK))
    return np.kron(np.eye(GROUP // BLOCK), single).astype(np.float32)


def split_pair(values):
    high = values.astype(jnp.bfloat16)
    return high, (values - high.astype(jnp.float32)).astype(jnp.bfloat16)


def mix(left, right, dims):
    return lax.dot_general(left, right, (dims, ((), ())), preferred_element_type=jnp.float32)


def three_pass(left_pair, right_pair, dims):
    return (
        mix(left_pair[0], right_pair[0], dims)
        + mix(left_pair[0], right_pair[1], dims)
        + mix(left_pair[1], right_pair[0], dims)
    )


def expand_block(index_rows, value_rows, width):
    freq = lax.broadcasted_iota(jnp.int32, (BLOCK, width), 0)
    dense = jnp.zeros((BLOCK, width), jnp.float32)
    for j in range(KEEP):
        dense = jnp.where(index_rows[j] == freq, value_rows[j], dense)
    return dense


def spread_row(row):
    return jnp.broadcast_to(row, (PACK, LANES)).astype(jnp.bfloat16)


def expand_tile(indices, values, dense, first, cols):
    freq = lax.broadcasted_iota(jnp.int32, (PACK, LANES), 0).astype(jnp.float32)
    for half in range(2):
        at = [spread_row(indices(half * KEEP + j)) for j in range(KEEP)]
        have = [spread_row(values(half * KEEP + j)) for j in range(KEEP)]
        for part in range(BLOCK // PACK):
            here = (freq + part * PACK).astype(jnp.bfloat16)
            tile = jnp.zeros((PACK, LANES), jnp.bfloat16)
            for j in range(KEEP):
                tile = jnp.where(at[j] == here, have[j], tile)
            start = first + half * BLOCK + part * PACK
            dense[start : start + PACK, cols] = tile


def four_products(cots, toks):
    total = jnp.dot(cots[0], toks[0], preferred_element_type=jnp.float32)
    for c, t in zip(cots[1:], toks[1:]):
        total += jnp.dot(c, t, preferred_element_type=jnp.float32)
    return total


def cot_of(message):
    return message[:, :TOK]


def tok_of(message):
    return jnp.concatenate([message[:TOK, TOK:], message[TOK:, TOK:]], axis=1)


def flat_index(idx):
    rows = [idx[b].astype(jnp.float32) for b in range(KV // BLOCK)]
    return jnp.concatenate(rows, axis=0).astype(jnp.bfloat16)


def pack_first_kernel(where, cot, tok, to_up, to_far, to_down, mine, own_cot, sems):
    head = pltpu.make_async_copy(cot.at[:, pl.ds(0, HALF)], own_cot, sems.at[0])
    head.start()
    copies = []
    for d, out in enumerate((mine, to_up, to_far, to_down)):
        first = pl.multiple_of((((where[0] ^ 1) + 2 * d) & 7) * ROWS, ROWS)
        if d == 0:
            copies.append(pltpu.make_async_copy(tok.at[:, pl.ds(first, ROWS)], out, sems.at[1]))
            continue
        for h in range(2):
            source = tok.at[:, pl.ds(first + h * TOK, TOK)]
            target = out.at[pl.ds(h * TOK, TOK), pl.ds(TOK, TOK)]
            copies.append(pltpu.make_async_copy(source, target, sems.at[2 * d + h]))
    for copy in copies:
        copy.start()
    head.wait()
    turned = own_cot[...].T
    for out in (to_up, to_far, to_down):
        out[:, :TOK] = turned
    for copy in copies:
        copy.wait()


def pack_second_kernel(where, cot, t0, t1, t2, t3, late_lo, late_hi, turned, mine, to_up, to_far, to_down):
    turned[...] = cot[...].T
    for out, t in ((mine, t0), (to_up, t1), (to_far, t2), (to_down, t3)):
        out[...] = t[...]


def partial_first_kernel(sent, hi, far, lo, t0, idx, early, turned, out):
    cots = (cot_of(sent), cot_of(hi), cot_of(far), cot_of(lo))
    toks = (t0[...], tok_of(hi), tok_of(far), tok_of(lo))
    out[:HALF, :] = four_products(cots, toks).astype(out.dtype)
    out[HALF:, :] = flat_index(idx)


def partial_second_kernel(c0, c1, c2, c3, t0, hi, far, lo, out):
    cots = (c0[...], c1[...], c2[...], c3[...])
    toks = (t0[...], tok_of(hi), tok_of(far), tok_of(lo))
    out[...] = four_products(cots, toks).astype(out.dtype)


def own_kernel(a0, a1, a2, a3, b0, b1, b2, b3, t0, t1, t2, t3, mom, out):
    step = pl.program_id(0)
    toks = (t0[...], t1[...], t2[...], t3[...])

    @pl.when(step < STEPS // 2)
    def _():
        cots = (cot_of(a0), cot_of(a1), cot_of(a2), cot_of(a3))
        out[...] = four_products(cots, toks) + beta_decay * mom[...].T

    @pl.when(step >= STEPS // 2)
    def _():
        cots = (b0[...], b1[...], b2[...], b3[...])
        out[...] = four_products(cots, toks) + beta_decay * mom[...].T


def pick_rows(moment, idx, ch, cl):
    spectrum = three_pass((ch[...], cl[...]), split_pair(moment), ((1,), (0,)))
    freq = lax.broadcasted_iota(jnp.int32, (BLOCK, ROWS), 0)
    rows = []
    for b in range(GROUP // BLOCK):
        part = spectrum[b * BLOCK : (b + 1) * BLOCK, :]
        for j in range(KEEP):
            here = idx[b, j : j + 1, :] == freq
            rows.append(jnp.sum(jnp.where(here, part, 0.0), axis=0, keepdims=True))
    return rows


def pick_kernel(where, pre, got_a, got_b, idx, ch, cl, late, moment, picked, keep, send):
    step = pl.program_id(0)
    first = step < STEPS // 2
    got = jnp.where(first, got_a[...], got_b[...]).astype(jnp.float32)
    total = pre[...] + got
    moment[...] = total
    values = jnp.concatenate(pick_rows(total, idx, ch, cl), axis=0)
    picked[...] = values

    def put(out):
        for t in range(GROUP // BLOCK * KEEP // 8):
            for q in range(ROWS // LANES):
                tile = values[t * 8 : (t + 1) * 8, q * LANES : (q + 1) * LANES]
                out[(step & 1) * (TILES // STEPS) + t * (ROWS // LANES) + q] = tile

    here = (step >> 1) == (where[1] & 1)
    pl.when(here)(lambda: put(keep))
    pl.when(jnp.logical_not(here))(lambda: put(send))


def add_two_kernel(a, b, *rest):
    out = rest[-1]
    out[...] = (a[...] + b[...]).astype(out.dtype)


def add_four_kernel(a, b, c, d, out):
    out[...] = (a[...] + b[...]) + (c[...] + d[...])


def pair_kernel(where, half, core, across, corner, late_0, late_1, late_2, out):
    side, mine = where[0] & 1, (where[1] & 1) * (TILES // 2)
    other = TILES // 2 - mine
    out[side, pl.ds(mine, TILES // 2)] = half[...]
    out[side, pl.ds(other, TILES // 2)] = core[...]
    out[1 - side, pl.ds(mine, TILES // 2)] = across[...]
    out[1 - side, pl.ds(other, TILES // 2)] = corner[...]


def residual_kernel(moment, picked, idx, ch, cl, late, out, mark):
    parts = []
    for b in range(GROUP // BLOCK):
        at = [idx[b, j : j + 1, :] for j in range(KEEP)]
        have = [picked[b * KEEP + j : b * KEEP + j + 1, :] for j in range(KEEP)]
        parts.append(expand_block(at, have, ROWS))
    kept = jnp.concatenate(parts, axis=0)
    back = three_pass((ch[...], cl[...]), split_pair(kept), ((0,), (0,)))
    out[...] = (moment[...] - back).T
    mark[...] = back[:8, :LANES]


def base_kernel(where, o0, o1, o2, o3, p0, p1, p2, p3, w_own, w_peer, idx, got_a, *outs):
    mine, theirs = flat_index(idx), got_a[HALF:, :]
    first = (where[0] & 1) == 0
    left, right = jnp.where(first, mine, theirs), jnp.where(first, theirs, mine)
    peers = (p0[...], tok_of(p1), tok_of(p2), tok_of(p3))
    for own, peer, out in zip((o0, o1, o2, o3), peers, outs):
        total = jnp.dot(own[...], w_own[...], preferred_element_type=jnp.float32)
        total += jnp.dot(peer, w_peer[...], preferred_element_type=jnp.float32)
        out[:TOK, :] = total.astype(out.dtype)
        out[TOK:, :ROWS] = left
        out[TOK:, ROWS:] = right


def expand_group(g, pairs, tot, dense):
    for t in range(2 * g, 2 * g + 2):
        for f in range(2):
            for q in range(ROWS // LANES):
                cols = slice(f * ROWS + q * LANES, f * ROWS + (q + 1) * LANES)
                tile = t * (ROWS // LANES) + q
                expand_tile(
                    lambda s, t=t, cols=cols: pairs[t * 8 + s : t * 8 + s + 1, cols],
                    lambda s, f=f, tile=tile: tot[f, tile, s : s + 1, :],
                    dense,
                    t * 2 * BLOCK,
                    cols,
                )


def forward_own_kernel(where, tok, own, tot, weight, ch, cl, mixed, out_weight, dense, pairs, values):
    pairs[...] = own[TOK:, :].astype(jnp.float32)
    values[...] = tot[...].astype(jnp.float32)
    cols = pl.ds(pl.multiple_of((where[0] & 1) * ROWS, ROWS), ROWS)
    for g in range(STEPS):
        expand_group(g, pairs, values, dense)
        span = slice(g * GROUP, (g + 1) * GROUP)
        mixed[span, :] = mix(dense[span, :], tok[...], ((1,), (1,)))
        turned = dense[span, cols].T
        delta = mix(turned, ch[...], ((1,), (0,))) + mix(turned, cl[...], ((1,), (0,)))
        new = weight[:, span].astype(jnp.float32) - (step_rate / REPS) * delta
        out_weight[:, span] = new.astype(out_weight.dtype)


def forward_kernel(where, tok_1, tok_2, tok_3, own, hi, far, lo, tot_1, tot_2, tot_3, mixed, ch, cl, out, *scratch):
    toks, dense, pairs, values = (tok_1, tok_2, tok_3), scratch[:3], scratch[3:6], scratch[6:]
    for near, pair, tot, value in zip((hi, far, lo), pairs, (tot_1, tot_2, tot_3), values):
        pair[...] = near[TOK:, :].astype(jnp.float32)
        value[...] = tot[...].astype(jnp.float32)
    for g in range(STEPS):
        span = slice(g * GROUP, (g + 1) * GROUP)
        total = mixed[span, :]
        for tok, pair, value, buffer in zip(toks, pairs, values, dense):
            expand_group(g, pair, value, buffer)
            total += mix(buffer[span, :], tok[...], ((1,), (1,)))
        delta = three_pass(split_pair(total.T), (ch[...], cl[...]), ((1,), (0,)))
        base = own[:TOK, span].astype(jnp.float32) + hi[:TOK, span].astype(jnp.float32)
        base += far[:TOK, span].astype(jnp.float32) + lo[:TOK, span].astype(jnp.float32)
        out[:, span] = (base - (step_rate / REPS) * delta).astype(out.dtype)


def params(limit=VMEM_LIMIT):
    return pltpu.CompilerParams(vmem_limit_bytes=limit)


def cost(flops, mib):
    return pl.CostEstimate(flops=int(flops), bytes_accessed=int(mib * (1 << 20)), transcendentals=0)


def whole(*shape):
    return pl.BlockSpec(shape, lambda c, *_: (0,) * len(shape))


def by_row(rows, width):
    return pl.BlockSpec((rows, width), lambda c, *_: (c, 0))


def by_col(rows, width):
    return pl.BlockSpec((rows, width), lambda c, *_: (0, c))


def first_half(rows, width):
    return pl.BlockSpec((rows, width), lambda c, *_: (jnp.minimum(c, STEPS // 2 - 1), 0))


def second_half(rows, width):
    return pl.BlockSpec((rows, width), lambda c, *_: (jnp.maximum(c - STEPS // 2, 0), 0))


AFTER = pl.BlockSpec(memory_space=pl.ANY)
BASIS = [whole(GROUP, GROUP)] * 2
GOT = [first_half(GROUP, ROWS), second_half(GROUP, ROWS)]
BF16, F32 = jnp.bfloat16, jnp.float32
INDEX = pl.BlockSpec((KV // BLOCK, KEEP, ROWS), lambda c, *_: (0, 0, 0))
INDEX_STEP = pl.BlockSpec((GROUP // BLOCK, KEEP, ROWS), lambda c, *_: (c, 0, 0))
MESSAGE = whole(HALF, 2 * TOK)
PIECE = whole(TOK, ROWS)
DENSE = pltpu.VMEM((KV, 2 * ROWS), BF16)
PAIRS = pltpu.VMEM((PICKS, 2 * ROWS), F32)
VALUES = pltpu.VMEM((2, TILES, 8, LANES), F32)


def shape(*dims, dtype=BF16):
    return jax.ShapeDtypeStruct(dims, dtype)


def body(tokens, cotangent, weight, momentum, kept_index):
    basis = dct_group()
    high = jnp.asarray(basis).astype(BF16)
    low = (jnp.asarray(basis) - high.astype(F32)).astype(BF16)
    place = jnp.stack([lax.axis_index("fsdp"), lax.axis_index("rep")]).astype(jnp.int32)
    index_t = jnp.transpose(kept_index, (1, 2, 0))

    def up(x):
        return lax.ppermute(x, "fsdp", [(i, (i + 2) % 8) for i in range(8)])

    def down(x):
        return lax.ppermute(x, "fsdp", [(i, (i + 6) % 8) for i in range(8)])

    def across(x):
        return lax.ppermute(x, "fsdp", [(i, (i + 4) % 8) for i in range(8)])

    def swap(x):
        return lax.ppermute(x, "fsdp", [(i, i ^ 1) for i in range(8)])

    def columns(flip):
        return [pl.BlockSpec((TOK, ROWS), lambda c, s, d=d: (0, ((s[0] ^ flip) + 2 * d) & 7)) for d in range(4)]

    weight_peer = swap(weight)

    first_up, first_far, first_down, peer_0 = pl.pallas_call(
        pack_first_kernel,
        grid_spec=pltpu.PrefetchScalarGridSpec(
            num_scalar_prefetch=1,
            grid=(1,),
            in_specs=[pl.BlockSpec(memory_space=pltpu.HBM)] * 2,
            out_specs=[MESSAGE] * 3 + [PIECE],
            scratch_shapes=[pltpu.VMEM((TOK, HALF), BF16), pltpu.SemaphoreType.DMA((8,))],
        ),
        out_shape=[shape(HALF, 2 * TOK)] * 3 + [shape(TOK, ROWS)],
        compiler_params=params(),
        cost_estimate=cost(0, 4),
    )(place, cotangent, tokens)
    first_lo = up(first_up)
    first_hi = down(first_down)
    first_x = across(first_far)
    firsts = (first_up, first_hi, first_x, first_lo)

    cot_b, own_0, own_up, own_across, own_down = pl.pallas_call(
        pack_second_kernel,
        grid_spec=pltpu.PrefetchScalarGridSpec(
            num_scalar_prefetch=1,
            grid=(1,),
            in_specs=[pl.BlockSpec((TOK, HALF), lambda c, *_: (0, 1))] + columns(0) + [AFTER, AFTER],
            out_specs=[whole(HALF, TOK)] + [PIECE] * 4,
        ),
        out_shape=[shape(HALF, TOK)] + [shape(TOK, ROWS)] * 4,
        compiler_params=params(),
        cost_estimate=cost(0, 3),
    )(place, cotangent, tokens, tokens, tokens, tokens, first_lo, first_hi)
    b_lo, b_hi, b_far = up(cot_b), down(cot_b), across(cot_b)
    cots_b = (cot_b, b_hi, b_far, b_lo)
    owns = (own_0, down(own_down), across(own_across), up(own_up))

    partial_a = pl.pallas_call(
        partial_first_kernel,
        grid=(1,),
        in_specs=[MESSAGE] * 4 + [PIECE, INDEX, AFTER, AFTER],
        out_specs=whole(HALF + PICKS, ROWS),
        out_shape=shape(HALF + PICKS, ROWS),
        compiler_params=params(),
        cost_estimate=cost(KV * KV * ROWS, 3),
    )(*firsts, peer_0, index_t, weight_peer, cot_b)
    got_a = swap(partial_a)
    partial_b = pl.pallas_call(
        partial_second_kernel,
        grid=(1,),
        in_specs=[whole(HALF, TOK)] * 4 + [PIECE] + [MESSAGE] * 3,
        out_specs=whole(HALF, ROWS),
        out_shape=shape(HALF, ROWS),
        compiler_params=params(),
        cost_estimate=cost(KV * KV * ROWS, 3),
    )(*cots_b, peer_0, *firsts[1:])
    got_b = swap(partial_b)

    pre = pl.pallas_call(
        own_kernel,
        grid=(STEPS,),
        in_specs=[first_half(GROUP, 2 * TOK)] * 4
        + [second_half(GROUP, TOK)] * 4
        + [PIECE] * 4
        + [by_col(ROWS, GROUP)],
        out_specs=by_row(GROUP, ROWS),
        out_shape=shape(KV, ROWS, dtype=F32),
        compiler_params=params(),
        cost_estimate=cost(2 * KV * KV * ROWS, 7),
    )(*firsts, *cots_b, *owns, momentum[0])

    base, base_up, base_across, base_down = pl.pallas_call(
        base_kernel,
        grid_spec=pltpu.PrefetchScalarGridSpec(
            num_scalar_prefetch=1,
            grid=(1,),
            in_specs=[PIECE] * 5
            + [MESSAGE] * 3
            + [whole(ROWS, KV)] * 2
            + [INDEX, whole(HALF + PICKS, ROWS)],
            out_specs=[whole(TOK + PICKS, KV)] * 4,
        ),
        out_shape=[shape(TOK + PICKS, KV)] * 4,
        compiler_params=params(2 * VMEM_LIMIT),
        cost_estimate=cost(4 * KV * KV * ROWS, 7),
    )(place, *owns, peer_0, *firsts[1:], weight, weight_peer, index_t, got_a)
    base_lo, base_hi, base_far = up(base_up), down(base_down), across(base_across)

    halves = whole(TILES // 2, 8, LANES)
    half_shape = shape(TILES // 2, 8, LANES, dtype=F32)
    moment, picked, keep, send = pl.pallas_call(
        pick_kernel,
        grid_spec=pltpu.PrefetchScalarGridSpec(
            num_scalar_prefetch=1,
            grid=(STEPS,),
            in_specs=[by_row(GROUP, ROWS)] + GOT + [INDEX_STEP] + BASIS + [AFTER],
            out_specs=[by_row(GROUP, ROWS), by_row(PICKS // STEPS, ROWS), halves, halves],
        ),
        out_shape=[shape(KV, ROWS, dtype=F32), shape(PICKS, ROWS, dtype=F32), half_shape, half_shape],
        compiler_params=params(),
        cost_estimate=cost(6 * KV * GROUP * ROWS, 6),
    )(place, pre, got_a, got_b, index_t, high, low, base)

    def partner(x, bits):
        return lax.ppermute(x, "rep", [(i, i ^ bits) for i in range(REPS)])

    def add(kernel, result, *parts, after=()):
        return pl.pallas_call(
            kernel,
            grid=(1,),
            in_specs=[halves] * len(parts) + [AFTER] * len(after),
            out_specs=halves,
            out_shape=result,
            compiler_params=params(),
            cost_estimate=cost(0, 0.25),
        )(*parts, *after)

    value = add(add_two_kernel, half_shape, keep, partner(send, 1))
    value = add(add_two_kernel, half_shape, value, partner(value, 2))
    value = add(add_four_kernel, half_shape, value, partner(value, 4), partner(value, 8), partner(value, 12))
    last = partner(value, 16)
    new_momentum, mark = pl.pallas_call(
        residual_kernel,
        grid=(STEPS,),
        in_specs=[by_row(GROUP, ROWS), by_row(PICKS // STEPS, ROWS), INDEX_STEP] + BASIS + [AFTER],
        out_specs=[by_col(ROWS, GROUP), whole(8, LANES)],
        out_shape=[shape(ROWS, KV, dtype=F32), shape(8, LANES, dtype=F32)],
        compiler_params=params(),
        cost_estimate=cost(6 * KV * GROUP * ROWS, 5),
    )(moment, picked, index_t, high, low, value)
    half = add(add_two_kernel, shape(TILES // 2, 8, LANES), value, last, after=(mark,))

    corner = lax.ppermute(half, ("rep", "fsdp"), [(i, i ^ 9) for i in range(REPS * 8)])
    pair_spec = whole(2, TILES, 8, LANES)
    pair = pl.pallas_call(
        pair_kernel,
        grid_spec=pltpu.PrefetchScalarGridSpec(
            num_scalar_prefetch=1,
            grid=(1,),
            in_specs=[halves] * 4 + [AFTER] * 3,
            out_specs=pair_spec,
        ),
        out_shape=shape(2, TILES, 8, LANES),
        compiler_params=params(),
        cost_estimate=cost(0, 0.25),
    )(place, half, partner(half, 1), swap(half), corner, base_lo, base_hi, base_far)
    pair_far, pair_lo, pair_hi = across(pair), up(pair), down(pair)

    def token_block(d):
        return pl.BlockSpec((TOK, 2 * ROWS), lambda c, s: (0, ((s[0] >> 1) + d) & 3))

    mixed, new_weight = pl.pallas_call(
        forward_own_kernel,
        grid_spec=pltpu.PrefetchScalarGridSpec(
            num_scalar_prefetch=1,
            grid=(1,),
            in_specs=[token_block(0), whole(TOK + PICKS, KV), pair_spec, whole(ROWS, KV)] + BASIS,
            out_specs=[whole(KV, TOK), whole(ROWS, KV)],
            scratch_shapes=[DENSE, PAIRS, VALUES],
        ),
        out_shape=[shape(KV, TOK, dtype=F32), shape(ROWS, KV)],
        compiler_params=params(),
        cost_estimate=cost(3 * KV * KV * ROWS, 4),
    )(place, tokens, base, pair, weight, high, low)

    projected = pl.pallas_call(
        forward_kernel,
        grid_spec=pltpu.PrefetchScalarGridSpec(
            num_scalar_prefetch=1,
            grid=(1,),
            in_specs=[token_block(d) for d in (1, 2, 3)]
            + [whole(TOK + PICKS, KV)] * 4
            + [pair_spec] * 3
            + [whole(KV, TOK)]
            + BASIS,
            out_specs=whole(TOK, KV),
            scratch_shapes=[DENSE] * 3 + [PAIRS] * 3 + [VALUES] * 3,
        ),
        out_shape=shape(TOK, KV),
        compiler_params=params(2 * VMEM_LIMIT),
        cost_estimate=cost(6 * KV * KV * ROWS, 7),
    )(place, tokens, tokens, tokens, base, base_hi, base_far, base_lo, pair_hi, pair_far, pair_lo, mixed, high, low)
    return (projected, new_weight, new_momentum[None])


def solution(mesh):
    in_specs = (
        P(("rep", "fsdp"), None),
        P(("rep", "fsdp"), None),
        P("fsdp", None),
        P("rep", "fsdp", None),
        P("fsdp", None, None),
    )
    out_specs = (P(("rep", "fsdp"), None), P("fsdp", None), P("rep", "fsdp", None))
    return jax.shard_map(body, mesh=mesh, in_specs=in_specs, out_specs=out_specs, check_vma=False)
```

```python
import jax
import jax.numpy as jnp
import numpy as np
from jax import lax
from jax.experimental import pallas as pl
from jax.experimental.pallas import tpu as pltpu
from jax.sharding import PartitionSpec as P

beta_decay = 0.9
step_rate = 0.5
ROWS = 512
KV = 1024
TOK = 256
BLOCK = 64
KEEP = 4
HALF = KV // 2
GROUP = 256
STEPS = KV // GROUP
PICKS = KV // BLOCK * KEEP
LANES = 128
PACK = 16
REPS = 32
TILES = PICKS * ROWS // (8 * LANES)
VMEM_LIMIT = 16 * 1024 * 1024


def dct_group():
    n = np.arange(BLOCK, dtype=np.float64)
    single = np.cos(np.pi * (2.0 * n[None, :] + 1.0) * n[:, None] / (2 * BLOCK))
    single *= np.where(n[:, None] == 0, np.sqrt(1.0 / BLOCK), np.sqrt(2.0 / BLOCK))
    return np.kron(np.eye(GROUP // BLOCK), single).astype(np.float32)


def split_pair(values):
    high = values.astype(jnp.bfloat16)
    return high, (values - high.astype(jnp.float32)).astype(jnp.bfloat16)


def mix(left, right, dims):
    return lax.dot_general(left, right, (dims, ((), ())), preferred_element_type=jnp.float32)


def three_pass(left_pair, right_pair, dims):
    return (
        mix(left_pair[0], right_pair[0], dims)
        + mix(left_pair[0], right_pair[1], dims)
        + mix(left_pair[1], right_pair[0], dims)
    )


def expand_block(index_rows, value_rows, width):
    freq = lax.broadcasted_iota(jnp.int32, (BLOCK, width), 0)
    dense = jnp.zeros((BLOCK, width), jnp.float32)
    for j in range(KEEP):
        dense = jnp.where(index_rows[j] == freq, value_rows[j], dense)
    return dense


def spread_row(row):
    return jnp.broadcast_to(row, (PACK, LANES)).astype(jnp.bfloat16)


def expand_tile(indices, values, dense, first, cols):
    freq = lax.broadcasted_iota(jnp.int32, (PACK, LANES), 0).astype(jnp.float32)
    for half in range(2):
        at = [spread_row(indices(half * KEEP + j)) for j in range(KEEP)]
        have = [spread_row(values(half * KEEP + j)) for j in range(KEEP)]
        for part in range(BLOCK // PACK):
            here = (freq + part * PACK).astype(jnp.bfloat16)
            tile = jnp.zeros((PACK, LANES), jnp.bfloat16)
            for j in range(KEEP):
                tile = jnp.where(at[j] == here, have[j], tile)
            start = first + half * BLOCK + part * PACK
            dense[start : start + PACK, cols] = tile


def four_products(cots, toks):
    total = jnp.dot(cots[0], toks[0], preferred_element_type=jnp.float32)
    for c, t in zip(cots[1:], toks[1:]):
        total += jnp.dot(c, t, preferred_element_type=jnp.float32)
    return total


def cot_of(message):
    return message[:, :TOK]


def tok_of(message):
    return jnp.concatenate([message[:TOK, TOK:], message[TOK:, TOK:]], axis=1)


def flat_index(idx):
    rows = [idx[b].astype(jnp.float32) for b in range(KV // BLOCK)]
    return jnp.concatenate(rows, axis=0).astype(jnp.bfloat16)


def pack_first_kernel(where, cot, tok, to_up, to_far, to_down, mine, own_cot, sems):
    head = pltpu.make_async_copy(cot.at[:, pl.ds(0, HALF)], own_cot, sems.at[0])
    head.start()
    copies = []
    for d, out in enumerate((mine, to_up, to_far, to_down)):
        first = pl.multiple_of((((where[0] ^ 1) + 2 * d) & 7) * ROWS, ROWS)
        if d == 0:
            copies.append(pltpu.make_async_copy(tok.at[:, pl.ds(first, ROWS)], out, sems.at[1]))
            continue
        for h in range(2):
            source = tok.at[:, pl.ds(first + h * TOK, TOK)]
            target = out.at[pl.ds(h * TOK, TOK), pl.ds(TOK, TOK)]
            copies.append(pltpu.make_async_copy(source, target, sems.at[2 * d + h]))
    for copy in copies:
        copy.start()
    head.wait()
    turned = own_cot[...].T
    for out in (to_up, to_far, to_down):
        out[:, :TOK] = turned
    for copy in copies:
        copy.wait()


def pack_second_kernel(cot, late_lo, late_hi, late_far, turned):
    turned[...] = cot[...].T


def pack_own_kernel(where, t0, t1, t2, t3, late, mine, to_up, to_far, to_down):
    for out, t in ((mine, t0), (to_up, t1), (to_far, t2), (to_down, t3)):
        out[...] = t[...]


def partial_first_kernel(sent, hi, far, lo, t0, idx, early, turned, out):
    cots = (cot_of(sent), cot_of(hi), cot_of(far), cot_of(lo))
    toks = (t0[...], tok_of(hi), tok_of(far), tok_of(lo))
    out[:HALF, :] = four_products(cots, toks).astype(out.dtype)
    out[HALF:, :] = flat_index(idx)


def partial_second_kernel(c0, c1, c2, c3, t0, hi, far, lo, out):
    cots = (c0[...], c1[...], c2[...], c3[...])
    toks = (t0[...], tok_of(hi), tok_of(far), tok_of(lo))
    out[...] = four_products(cots, toks).astype(out.dtype)


def own_kernel(a0, a1, a2, a3, b0, b1, b2, b3, t0, t1, t2, t3, mom, out):
    step = pl.program_id(0)
    toks = (t0[...], t1[...], t2[...], t3[...])

    @pl.when(step < STEPS // 2)
    def _():
        cots = (cot_of(a0), cot_of(a1), cot_of(a2), cot_of(a3))
        out[...] = four_products(cots, toks) + beta_decay * mom[...].T

    @pl.when(step >= STEPS // 2)
    def _():
        cots = (b0[...], b1[...], b2[...], b3[...])
        out[...] = four_products(cots, toks) + beta_decay * mom[...].T


def pick_rows(moment, idx, ch, cl):
    spectrum = three_pass((ch[...], cl[...]), split_pair(moment), ((1,), (0,)))
    freq = lax.broadcasted_iota(jnp.int32, (BLOCK, ROWS), 0)
    rows = []
    for b in range(GROUP // BLOCK):
        part = spectrum[b * BLOCK : (b + 1) * BLOCK, :]
        for j in range(KEEP):
            here = idx[b, j : j + 1, :] == freq
            rows.append(jnp.sum(jnp.where(here, part, 0.0), axis=0, keepdims=True))
    return rows


def pick_kernel(where, pre, got_a, got_b, idx, ch, cl, moment, picked, keep, send):
    step = pl.program_id(0)
    first = step < STEPS // 2
    got = jnp.where(first, got_a[...], got_b[...]).astype(jnp.float32)
    total = pre[...] + got
    moment[...] = total
    values = jnp.concatenate(pick_rows(total, idx, ch, cl), axis=0)
    picked[...] = values

    def put(out):
        for t in range(GROUP // BLOCK * KEEP // 8):
            for q in range(ROWS // LANES):
                tile = values[t * 8 : (t + 1) * 8, q * LANES : (q + 1) * LANES]
                out[(step & 1) * (TILES // STEPS) + t * (ROWS // LANES) + q] = tile

    here = (step >> 1) == (where[1] & 1)
    pl.when(here)(lambda: put(keep))
    pl.when(jnp.logical_not(here))(lambda: put(send))


def add_two_kernel(a, b, *rest):
    out = rest[-1]
    out[...] = (a[...] + b[...]).astype(out.dtype)


def add_release_kernel(a, b, *rest):
    out = rest[3]
    out[...] = a[...] + b[...]


def pair_kernel(where, half, core, across, corner, late_0, late_1, late_2, out):
    side, mine = where[0] & 1, (where[1] & 1) * (TILES // 2)
    other = TILES // 2 - mine
    out[side, pl.ds(mine, TILES // 2)] = half[...]
    out[side, pl.ds(other, TILES // 2)] = core[...]
    out[1 - side, pl.ds(mine, TILES // 2)] = across[...]
    out[1 - side, pl.ds(other, TILES // 2)] = corner[...]


def residual_kernel(moment, picked, idx, ch, cl, late, out, mark):
    parts = []
    for b in range(GROUP // BLOCK):
        at = [idx[b, j : j + 1, :] for j in range(KEEP)]
        have = [picked[b * KEEP + j : b * KEEP + j + 1, :] for j in range(KEEP)]
        parts.append(expand_block(at, have, ROWS))
    kept = jnp.concatenate(parts, axis=0)
    back = three_pass((ch[...], cl[...]), split_pair(kept), ((0,), (0,)))
    out[...] = (moment[...] - back).T
    mark[...] = back[:8, :LANES]


def base_kernel(where, o0, o1, o2, o3, p0, p1, p2, p3, w_own, w_peer, idx, got_a, late, *outs):
    mine, theirs = flat_index(idx), got_a[HALF:, :]
    first = (where[0] & 1) == 0
    left, right = jnp.where(first, mine, theirs), jnp.where(first, theirs, mine)
    peers = (p0[...], tok_of(p1), tok_of(p2), tok_of(p3))
    for own, peer, out in zip((o0, o1, o2, o3), peers, outs):
        total = jnp.dot(own[...], w_own[...], preferred_element_type=jnp.float32)
        total += jnp.dot(peer, w_peer[...], preferred_element_type=jnp.float32)
        out[:TOK, :] = total.astype(out.dtype)
        out[TOK:, :ROWS] = left
        out[TOK:, ROWS:] = right


def expand_group(g, pairs, tot, dense):
    for t in range(2 * g, 2 * g + 2):
        for f in range(2):
            for q in range(ROWS // LANES):
                cols = slice(f * ROWS + q * LANES, f * ROWS + (q + 1) * LANES)
                tile = t * (ROWS // LANES) + q
                expand_tile(
                    lambda s, t=t, cols=cols: pairs[t * 8 + s : t * 8 + s + 1, cols],
                    lambda s, f=f, tile=tile: tot[f, tile, s : s + 1, :],
                    dense,
                    t * 2 * BLOCK,
                    cols,
                )


def forward_own_kernel(where, tok, own, tot, weight, ch, cl, mixed, out_weight, dense, pairs, values):
    pairs[...] = own[TOK:, :].astype(jnp.float32)
    values[...] = tot[...].astype(jnp.float32)
    cols = pl.ds(pl.multiple_of((where[0] & 1) * ROWS, ROWS), ROWS)
    for g in range(STEPS):
        expand_group(g, pairs, values, dense)
        span = slice(g * GROUP, (g + 1) * GROUP)
        turned = dense[span, cols].T
        delta = mix(turned, ch[...], ((1,), (0,))) + mix(turned, cl[...], ((1,), (0,)))
        new = weight[:, span].astype(jnp.float32) - (step_rate / REPS) * delta
        out_weight[:, span] = new.astype(out_weight.dtype)
    mixed[...] = mix(dense[...], tok[...], ((1,), (1,)))


def forward_kernel(where, tok_1, tok_2, tok_3, own, hi, far, lo, tot_1, tot_2, tot_3, mixed, ch, cl, out, *scratch):
    toks, dense, pairs, values = (tok_1, tok_2, tok_3), scratch[:3], scratch[3:6], scratch[6:9]
    total = scratch[9]
    for near, pair, tot, value in zip((hi, far, lo), pairs, (tot_1, tot_2, tot_3), values):
        pair[...] = near[TOK:, :].astype(jnp.float32)
        value[...] = tot[...].astype(jnp.float32)
    before = mixed
    for tok, pair, value, buffer in zip(toks, pairs, values, dense):
        for g in range(STEPS):
            expand_group(g, pair, value, buffer)
        total[...] = before[...] + mix(buffer[...], tok[...], ((1,), (1,)))
        before = total
    for g in range(STEPS):
        span = slice(g * GROUP, (g + 1) * GROUP)
        delta = three_pass(split_pair(total[span, :].T), (ch[...], cl[...]), ((1,), (0,)))
        base = own[:TOK, span].astype(jnp.float32) + hi[:TOK, span].astype(jnp.float32)
        base += far[:TOK, span].astype(jnp.float32) + lo[:TOK, span].astype(jnp.float32)
        out[:, span] = (base - (step_rate / REPS) * delta).astype(out.dtype)


def params(limit=VMEM_LIMIT):
    return pltpu.CompilerParams(vmem_limit_bytes=limit)


def cost(flops, mib):
    return pl.CostEstimate(flops=int(flops), bytes_accessed=int(mib * (1 << 20)), transcendentals=0)


def whole(*shape):
    return pl.BlockSpec(shape, lambda c, *_: (0,) * len(shape))


def by_row(rows, width):
    return pl.BlockSpec((rows, width), lambda c, *_: (c, 0))


def by_col(rows, width):
    return pl.BlockSpec((rows, width), lambda c, *_: (0, c))


def first_half(rows, width):
    return pl.BlockSpec((rows, width), lambda c, *_: (jnp.minimum(c, STEPS // 2 - 1), 0))


def second_half(rows, width):
    return pl.BlockSpec((rows, width), lambda c, *_: (jnp.maximum(c - STEPS // 2, 0), 0))


AFTER = pl.BlockSpec(memory_space=pl.ANY)
BASIS = [whole(GROUP, GROUP)] * 2
GOT = [first_half(GROUP, ROWS), second_half(GROUP, ROWS)]
BF16, F32 = jnp.bfloat16, jnp.float32
INDEX = pl.BlockSpec((KV // BLOCK, KEEP, ROWS), lambda c, *_: (0, 0, 0))
INDEX_STEP = pl.BlockSpec((GROUP // BLOCK, KEEP, ROWS), lambda c, *_: (c, 0, 0))
MESSAGE = whole(HALF, 2 * TOK)
PIECE = whole(TOK, ROWS)
DENSE = pltpu.VMEM((KV, 2 * ROWS), BF16)
PAIRS = pltpu.VMEM((PICKS, 2 * ROWS), F32)
VALUES = pltpu.VMEM((2, TILES, 8, LANES), F32)


def shape(*dims, dtype=BF16):
    return jax.ShapeDtypeStruct(dims, dtype)


def body(tokens, cotangent, weight, momentum, kept_index):
    basis = dct_group()
    high = jnp.asarray(basis).astype(BF16)
    low = (jnp.asarray(basis) - high.astype(F32)).astype(BF16)
    place = jnp.stack([lax.axis_index("fsdp"), lax.axis_index("rep")]).astype(jnp.int32)
    index_t = jnp.transpose(kept_index, (1, 2, 0))

    def up(x):
        return lax.ppermute(x, "fsdp", [(i, (i + 2) % 8) for i in range(8)])

    def down(x):
        return lax.ppermute(x, "fsdp", [(i, (i + 6) % 8) for i in range(8)])

    def across(x):
        return lax.ppermute(x, "fsdp", [(i, (i + 4) % 8) for i in range(8)])

    def swap(x):
        return lax.ppermute(x, "fsdp", [(i, i ^ 1) for i in range(8)])

    def columns(flip):
        return [pl.BlockSpec((TOK, ROWS), lambda c, s, d=d: (0, ((s[0] ^ flip) + 2 * d) & 7)) for d in range(4)]

    weight_peer = swap(weight)

    first_up, first_far, first_down, peer_0 = pl.pallas_call(
        pack_first_kernel,
        grid_spec=pltpu.PrefetchScalarGridSpec(
            num_scalar_prefetch=1,
            grid=(1,),
            in_specs=[pl.BlockSpec(memory_space=pltpu.HBM)] * 2,
            out_specs=[MESSAGE] * 3 + [PIECE],
            scratch_shapes=[pltpu.VMEM((TOK, HALF), BF16), pltpu.SemaphoreType.DMA((8,))],
        ),
        out_shape=[shape(HALF, 2 * TOK)] * 3 + [shape(TOK, ROWS)],
        compiler_params=params(),
        cost_estimate=cost(0, 4),
    )(place, cotangent, tokens)
    first_lo = up(first_up)
    first_hi = down(first_down)
    first_x = across(first_far)
    firsts = (first_up, first_hi, first_x, first_lo)

    cot_b = pl.pallas_call(
        pack_second_kernel,
        grid=(1,),
        in_specs=[pl.BlockSpec((TOK, HALF), lambda c: (0, 1)), AFTER, AFTER, AFTER],
        out_specs=whole(HALF, TOK),
        out_shape=shape(HALF, TOK),
        compiler_params=params(),
        cost_estimate=cost(0, 1),
    )(cotangent, first_lo, first_hi, first_x)
    b_lo, b_hi, b_far = up(cot_b), down(cot_b), across(cot_b)
    cots_b = (cot_b, b_hi, b_far, b_lo)

    partial_a = pl.pallas_call(
        partial_first_kernel,
        grid=(1,),
        in_specs=[MESSAGE] * 4 + [PIECE, INDEX, AFTER, AFTER],
        out_specs=whole(HALF + PICKS, ROWS),
        out_shape=shape(HALF + PICKS, ROWS),
        compiler_params=params(),
        cost_estimate=cost(KV * KV * ROWS, 3),
    )(*firsts, peer_0, index_t, weight_peer, cot_b)
    got_a = swap(partial_a)
    partial_b = pl.pallas_call(
        partial_second_kernel,
        grid=(1,),
        in_specs=[whole(HALF, TOK)] * 4 + [PIECE] + [MESSAGE] * 3,
        out_specs=whole(HALF, ROWS),
        out_shape=shape(HALF, ROWS),
        compiler_params=params(),
        cost_estimate=cost(KV * KV * ROWS, 3),
    )(*cots_b, peer_0, *firsts[1:])
    got_b = swap(partial_b)

    own_0, own_up, own_across, own_down = pl.pallas_call(
        pack_own_kernel,
        grid_spec=pltpu.PrefetchScalarGridSpec(
            num_scalar_prefetch=1,
            grid=(1,),
            in_specs=columns(0) + [AFTER],
            out_specs=[PIECE] * 4,
        ),
        out_shape=[shape(TOK, ROWS)] * 4,
        compiler_params=params(),
        cost_estimate=cost(0, 2),
    )(place, tokens, tokens, tokens, tokens, partial_b)
    owns = (own_0, down(own_down), across(own_across), up(own_up))

    pre = pl.pallas_call(
        own_kernel,
        grid=(STEPS,),
        in_specs=[first_half(GROUP, 2 * TOK)] * 4
        + [second_half(GROUP, TOK)] * 4
        + [PIECE] * 4
        + [by_col(ROWS, GROUP)],
        out_specs=by_row(GROUP, ROWS),
        out_shape=shape(KV, ROWS, dtype=F32),
        compiler_params=params(),
        cost_estimate=cost(2 * KV * KV * ROWS, 7),
    )(*firsts, *cots_b, *owns, momentum[0])

    halves = whole(TILES // 2, 8, LANES)
    half_shape = shape(TILES // 2, 8, LANES, dtype=F32)
    moment, picked, keep, send = pl.pallas_call(
        pick_kernel,
        grid_spec=pltpu.PrefetchScalarGridSpec(
            num_scalar_prefetch=1,
            grid=(STEPS,),
            in_specs=[by_row(GROUP, ROWS)] + GOT + [INDEX_STEP] + BASIS,
            out_specs=[by_row(GROUP, ROWS), by_row(PICKS // STEPS, ROWS), halves, halves],
        ),
        out_shape=[shape(KV, ROWS, dtype=F32), shape(PICKS, ROWS, dtype=F32), half_shape, half_shape],
        compiler_params=params(),
        cost_estimate=cost(6 * KV * GROUP * ROWS, 6),
    )(place, pre, got_a, got_b, index_t, high, low)

    def partner(x, bits):
        return lax.ppermute(x, "rep", [(i, i ^ bits) for i in range(REPS)])

    def add(kernel, result, *parts, after=()):
        return pl.pallas_call(
            kernel,
            grid=(1,),
            in_specs=[halves] * len(parts) + [AFTER] * len(after),
            out_specs=halves,
            out_shape=result,
            compiler_params=params(),
            cost_estimate=cost(0, 0.25),
        )(*parts, *after)

    value = add(add_two_kernel, half_shape, keep, partner(send, 1))
    from_hi = partner(value, 2)

    base, base_up, base_across, base_down = pl.pallas_call(
        base_kernel,
        grid_spec=pltpu.PrefetchScalarGridSpec(
            num_scalar_prefetch=1,
            grid=(1,),
            in_specs=[PIECE] * 5
            + [MESSAGE] * 3
            + [whole(ROWS, KV)] * 2
            + [INDEX, whole(HALF + PICKS, ROWS), AFTER],
            out_specs=[whole(TOK + PICKS, KV)] * 4,
        ),
        out_shape=[shape(TOK + PICKS, KV)] * 4,
        compiler_params=params(2 * VMEM_LIMIT),
        cost_estimate=cost(0, 0),
    )(place, *owns, peer_0, *firsts[1:], weight, weight_peer, index_t, got_a, value)
    value, base_up, base_across, base_down = pl.pallas_call(
        add_release_kernel,
        grid=(1,),
        in_specs=[halves] * 2 + [AFTER] * 3,
        out_specs=[halves] + [AFTER] * 3,
        out_shape=[half_shape] + [shape(TOK + PICKS, KV)] * 3,
        input_output_aliases={2: 1, 3: 2, 4: 3},
        compiler_params=params(),
        cost_estimate=cost(0, 0.25),
    )(value, from_hi, base_up, base_across, base_down)
    base_lo, base_hi, base_far = up(base_up), down(base_down), across(base_across)
    value = add(add_two_kernel, half_shape, value, partner(value, 4))
    value = add(add_two_kernel, half_shape, value, partner(value, 8))
    last = partner(value, 16)
    new_momentum, mark = pl.pallas_call(
        residual_kernel,
        grid=(STEPS,),
        in_specs=[by_row(GROUP, ROWS), by_row(PICKS // STEPS, ROWS), INDEX_STEP] + BASIS + [AFTER],
        out_specs=[by_col(ROWS, GROUP), whole(8, LANES)],
        out_shape=[shape(ROWS, KV, dtype=F32), shape(8, LANES, dtype=F32)],
        compiler_params=params(),
        cost_estimate=cost(6 * KV * GROUP * ROWS, 5),
    )(moment, picked, index_t, high, low, value)
    half = add(add_two_kernel, shape(TILES // 2, 8, LANES), value, last, after=(mark,))

    corner = lax.ppermute(half, ("rep", "fsdp"), [(i, i ^ 9) for i in range(REPS * 8)])
    pair_spec = whole(2, TILES, 8, LANES)
    pair = pl.pallas_call(
        pair_kernel,
        grid_spec=pltpu.PrefetchScalarGridSpec(
            num_scalar_prefetch=1,
            grid=(1,),
            in_specs=[halves] * 4 + [AFTER] * 3,
            out_specs=pair_spec,
        ),
        out_shape=shape(2, TILES, 8, LANES),
        compiler_params=params(),
        cost_estimate=cost(0, 0.25),
    )(place, half, partner(half, 1), swap(half), corner, base_lo, base_hi, base_far)
    pair_far, pair_lo, pair_hi = across(pair), up(pair), down(pair)

    def token_block(d):
        return pl.BlockSpec((TOK, 2 * ROWS), lambda c, s: (0, ((s[0] >> 1) + d) & 3))

    mixed, new_weight = pl.pallas_call(
        forward_own_kernel,
        grid_spec=pltpu.PrefetchScalarGridSpec(
            num_scalar_prefetch=1,
            grid=(1,),
            in_specs=[token_block(0), whole(TOK + PICKS, KV), pair_spec, whole(ROWS, KV)] + BASIS,
            out_specs=[whole(KV, TOK), whole(ROWS, KV)],
            scratch_shapes=[DENSE, PAIRS, VALUES],
        ),
        out_shape=[shape(KV, TOK, dtype=F32), shape(ROWS, KV)],
        compiler_params=params(),
        cost_estimate=cost(3 * KV * KV * ROWS, 4),
    )(place, tokens, base, pair, weight, high, low)

    projected = pl.pallas_call(
        forward_kernel,
        grid_spec=pltpu.PrefetchScalarGridSpec(
            num_scalar_prefetch=1,
            grid=(1,),
            in_specs=[token_block(d) for d in (1, 2, 3)]
            + [whole(TOK + PICKS, KV)] * 4
            + [pair_spec] * 3
            + [whole(KV, TOK)]
            + BASIS,
            out_specs=whole(TOK, KV),
            scratch_shapes=[DENSE] * 3 + [PAIRS] * 3 + [VALUES] * 3 + [pltpu.VMEM((KV, TOK), F32)],
        ),
        out_shape=shape(TOK, KV),
        compiler_params=params(2 * VMEM_LIMIT),
        cost_estimate=cost(6 * KV * KV * ROWS, 7),
    )(place, tokens, tokens, tokens, base, base_hi, base_far, base_lo, pair_hi, pair_far, pair_lo, mixed, high, low)
    return (projected, new_weight, new_momentum[None])


def solution(mesh):
    in_specs = (
        P(("rep", "fsdp"), None),
        P(("rep", "fsdp"), None),
        P("fsdp", None),
        P("rep", "fsdp", None),
        P("fsdp", None, None),
    )
    out_specs = (P(("rep", "fsdp"), None), P("fsdp", None), P("rep", "fsdp", None))
    return jax.shard_map(body, mesh=mesh, in_specs=in_specs, out_specs=out_specs, check_vma=False)
```

```python
import jax
import jax.numpy as jnp
import numpy as np
from jax import lax
from jax.experimental import pallas as pl
from jax.experimental.pallas import tpu as pltpu
from jax.sharding import PartitionSpec as P

beta_decay = 0.9
step_rate = 0.5
ROWS = 512
KV = 1024
TOK = 256
BLOCK = 64
KEEP = 4
HALF = KV // 2
GROUP = 256
STEPS = KV // GROUP
PICKS = KV // BLOCK * KEEP
LANES = 128
PACK = 16
REPS = 32
TILES = PICKS * ROWS // (8 * LANES)
VMEM_LIMIT = 16 * 1024 * 1024


def dct_group():
    n = np.arange(BLOCK, dtype=np.float64)
    single = np.cos(np.pi * (2.0 * n[None, :] + 1.0) * n[:, None] / (2 * BLOCK))
    single *= np.where(n[:, None] == 0, np.sqrt(1.0 / BLOCK), np.sqrt(2.0 / BLOCK))
    return np.kron(np.eye(GROUP // BLOCK), single).astype(np.float32)


def split_pair(values):
    high = values.astype(jnp.bfloat16)
    return high, (values - high.astype(jnp.float32)).astype(jnp.bfloat16)


def mix(left, right, dims):
    return lax.dot_general(left, right, (dims, ((), ())), preferred_element_type=jnp.float32)


def three_pass(left_pair, right_pair, dims):
    return (
        mix(left_pair[0], right_pair[0], dims)
        + mix(left_pair[0], right_pair[1], dims)
        + mix(left_pair[1], right_pair[0], dims)
    )


def expand_block(index_rows, value_rows, width):
    freq = lax.broadcasted_iota(jnp.int32, (BLOCK, width), 0)
    dense = jnp.zeros((BLOCK, width), jnp.float32)
    for j in range(KEEP):
        dense = jnp.where(index_rows[j] == freq, value_rows[j], dense)
    return dense


def spread_row(row):
    return jnp.broadcast_to(row, (PACK, LANES)).astype(jnp.bfloat16)


def expand_tile(indices, values, dense, first, cols):
    freq = lax.broadcasted_iota(jnp.int32, (PACK, LANES), 0).astype(jnp.float32)
    for half in range(2):
        at = [spread_row(indices(half * KEEP + j)) for j in range(KEEP)]
        have = [spread_row(values(half * KEEP + j)) for j in range(KEEP)]
        for part in range(BLOCK // PACK):
            here = (freq + part * PACK).astype(jnp.bfloat16)
            tile = jnp.zeros((PACK, LANES), jnp.bfloat16)
            for j in range(KEEP):
                tile = jnp.where(at[j] == here, have[j], tile)
            start = first + half * BLOCK + part * PACK
            dense[start : start + PACK, cols] = tile


def four_products(cots, toks):
    total = jnp.dot(cots[0], toks[0], preferred_element_type=jnp.float32)
    for c, t in zip(cots[1:], toks[1:]):
        total += jnp.dot(c, t, preferred_element_type=jnp.float32)
    return total


def cot_of(message):
    return message[:, :TOK]


def tok_of(message):
    return jnp.concatenate([message[:TOK, TOK:], message[TOK:, TOK:]], axis=1)


def flat_index(idx):
    rows = [idx[b].astype(jnp.float32) for b in range(KV // BLOCK)]
    return jnp.concatenate(rows, axis=0).astype(jnp.bfloat16)


def pack_first_kernel(where, cot, tok, to_up, to_down, far, mine, own_cot, sems):
    head = pltpu.make_async_copy(cot.at[:, pl.ds(0, HALF)], own_cot, sems.at[0])
    head.start()
    copies = []
    for d, out in enumerate((mine, to_up, far, to_down)):
        first = pl.multiple_of((((where[0] ^ 1) + 2 * d) & 7) * ROWS, ROWS)
        if d in (0, 2):
            copies.append(pltpu.make_async_copy(tok.at[:, pl.ds(first, ROWS)], out, sems.at[2 * d + 1]))
            continue
        for h in range(2):
            source = tok.at[:, pl.ds(first + h * TOK, TOK)]
            target = out.at[pl.ds(h * TOK, TOK), pl.ds(TOK, TOK)]
            copies.append(pltpu.make_async_copy(source, target, sems.at[2 * d + h]))
    for copy in copies:
        copy.start()
    head.wait()
    turned = own_cot[...].T
    for out in (to_up, to_down):
        out[:, :TOK] = turned
    for copy in copies:
        copy.wait()


def pack_second_kernel(first, cot, late, relay, turned):
    relay[...] = cot_of(first)
    turned[...] = cot[...].T


def pack_own_kernel(where, t0, t1, t2, t3, late_lo, late_hi, mine, to_up, to_far, to_down):
    for out, t in ((mine, t0), (to_up, t1), (to_far, t2), (to_down, t3)):
        out[...] = t[...]


def partial_first_kernel(sent, hi, far, lo, t0, t2, idx, early, turned, out):
    cots = (cot_of(sent), cot_of(hi), far[...], cot_of(lo))
    toks = (t0[...], tok_of(hi), t2[...], tok_of(lo))
    out[:HALF, :] = four_products(cots, toks).astype(out.dtype)
    out[HALF:, :] = flat_index(idx)


def partial_second_kernel(c0, c1, c2, c3, t0, hi, t2, lo, out):
    cots = (c0[...], c1[...], c2[...], c3[...])
    toks = (t0[...], tok_of(hi), t2[...], tok_of(lo))
    out[...] = four_products(cots, toks).astype(out.dtype)


def own_kernel(a0, a1, a2, a3, b0, b1, b2, b3, t0, t1, t2, t3, mom, out):
    step = pl.program_id(0)
    toks = (t0[...], t1[...], t2[...], t3[...])

    @pl.when(step < STEPS // 2)
    def _():
        cots = (cot_of(a0), cot_of(a1), a2[...], cot_of(a3))
        out[...] = four_products(cots, toks) + beta_decay * mom[...].T

    @pl.when(step >= STEPS // 2)
    def _():
        cots = (b0[...], b1[...], b2[...], b3[...])
        out[...] = four_products(cots, toks) + beta_decay * mom[...].T


def pick_rows(moment, idx, ch, cl):
    spectrum = three_pass((ch[...], cl[...]), split_pair(moment), ((1,), (0,)))
    freq = lax.broadcasted_iota(jnp.int32, (BLOCK, ROWS), 0)
    rows = []
    for b in range(GROUP // BLOCK):
        part = spectrum[b * BLOCK : (b + 1) * BLOCK, :]
        for j in range(KEEP):
            here = idx[b, j : j + 1, :] == freq
            rows.append(jnp.sum(jnp.where(here, part, 0.0), axis=0, keepdims=True))
    return rows


def pick_kernel(where, pre, got_a, got_b, idx, ch, cl, late, moment, picked, keep, send):
    step = pl.program_id(0)
    first = step < STEPS // 2
    got = jnp.where(first, got_a[...], got_b[...]).astype(jnp.float32)
    total = pre[...] + got
    moment[...] = total
    values = jnp.concatenate(pick_rows(total, idx, ch, cl), axis=0)
    picked[...] = values

    def put(out):
        for t in range(GROUP // BLOCK * KEEP // 8):
            for q in range(ROWS // LANES):
                tile = values[t * 8 : (t + 1) * 8, q * LANES : (q + 1) * LANES]
                out[(step & 1) * (TILES // STEPS) + t * (ROWS // LANES) + q] = tile

    here = (step >> 1) == (where[1] & 1)
    pl.when(here)(lambda: put(keep))
    pl.when(jnp.logical_not(here))(lambda: put(send))


def add_two_kernel(a, b, *rest):
    out = rest[-1]
    out[...] = (a[...] + b[...]).astype(out.dtype)


def pair_kernel(where, half, core, across, corner, late_0, late_1, late_2, out):
    side, mine = where[0] & 1, (where[1] & 1) * (TILES // 2)
    other = TILES // 2 - mine
    out[side, pl.ds(mine, TILES // 2)] = half[...]
    out[side, pl.ds(other, TILES // 2)] = core[...]
    out[1 - side, pl.ds(mine, TILES // 2)] = across[...]
    out[1 - side, pl.ds(other, TILES // 2)] = corner[...]


def residual_kernel(moment, picked, idx, ch, cl, late, out, mark):
    parts = []
    for b in range(GROUP // BLOCK):
        at = [idx[b, j : j + 1, :] for j in range(KEEP)]
        have = [picked[b * KEEP + j : b * KEEP + j + 1, :] for j in range(KEEP)]
        parts.append(expand_block(at, have, ROWS))
    kept = jnp.concatenate(parts, axis=0)
    back = three_pass((ch[...], cl[...]), split_pair(kept), ((0,), (0,)))
    out[...] = (moment[...] - back).T
    mark[...] = back[:8, :LANES]


def base_kernel(where, o0, o1, o2, o3, p0, p1, p2, p3, w_own, w_peer, idx, got_a, *outs):
    mine, theirs = flat_index(idx), got_a[HALF:, :]
    first = (where[0] & 1) == 0
    left, right = jnp.where(first, mine, theirs), jnp.where(first, theirs, mine)
    peers = (p0[...], tok_of(p1), p2[...], tok_of(p3))
    for own, peer, out in zip((o0, o1, o2, o3), peers, outs):
        total = jnp.dot(own[...], w_own[...], preferred_element_type=jnp.float32)
        total += jnp.dot(peer, w_peer[...], preferred_element_type=jnp.float32)
        out[:TOK, :] = total.astype(out.dtype)
        out[TOK:, :ROWS] = left
        out[TOK:, ROWS:] = right


def expand_group(g, pairs, tot, dense):
    for t in range(2 * g, 2 * g + 2):
        for f in range(2):
            for q in range(ROWS // LANES):
                cols = slice(f * ROWS + q * LANES, f * ROWS + (q + 1) * LANES)
                tile = t * (ROWS // LANES) + q
                expand_tile(
                    lambda s, t=t, cols=cols: pairs[t * 8 + s : t * 8 + s + 1, cols],
                    lambda s, f=f, tile=tile: tot[f, tile, s : s + 1, :],
                    dense,
                    t * 2 * BLOCK,
                    cols,
                )


def forward_own_kernel(where, tok, own, tot, weight, ch, cl, mixed, out_weight, dense, pairs, values):
    pairs[...] = own[TOK:, :].astype(jnp.float32)
    values[...] = tot[...].astype(jnp.float32)
    cols = pl.ds(pl.multiple_of((where[0] & 1) * ROWS, ROWS), ROWS)
    for g in range(STEPS):
        expand_group(g, pairs, values, dense)
        span = slice(g * GROUP, (g + 1) * GROUP)
        turned = dense[span, cols].T
        delta = mix(turned, ch[...], ((1,), (0,))) + mix(turned, cl[...], ((1,), (0,)))
        new = weight[:, span].astype(jnp.float32) - (step_rate / REPS) * delta
        out_weight[:, span] = new.astype(out_weight.dtype)
    mixed[...] = mix(dense[...], tok[...], ((1,), (1,)))


def forward_kernel(where, tok_1, tok_2, tok_3, own, hi, far, lo, tot_1, tot_2, tot_3, mixed, ch, cl, out, *scratch):
    toks, dense, pairs, values = (tok_1, tok_2, tok_3), scratch[:3], scratch[3:6], scratch[6:9]
    total = scratch[9]
    for near, pair, tot, value in zip((hi, far, lo), pairs, (tot_1, tot_2, tot_3), values):
        pair[...] = near[TOK:, :].astype(jnp.float32)
        value[...] = tot[...].astype(jnp.float32)
    before = mixed
    for tok, pair, value, buffer in zip(toks, pairs, values, dense):
        for g in range(STEPS):
            expand_group(g, pair, value, buffer)
        total[...] = before[...] + mix(buffer[...], tok[...], ((1,), (1,)))
        before = total
    for g in range(STEPS):
        span = slice(g * GROUP, (g + 1) * GROUP)
        delta = three_pass(split_pair(total[span, :].T), (ch[...], cl[...]), ((1,), (0,)))
        base = own[:TOK, span].astype(jnp.float32) + hi[:TOK, span].astype(jnp.float32)
        base += far[:TOK, span].astype(jnp.float32) + lo[:TOK, span].astype(jnp.float32)
        out[:, span] = (base - (step_rate / REPS) * delta).astype(out.dtype)


def params(limit=VMEM_LIMIT):
    return pltpu.CompilerParams(vmem_limit_bytes=limit)


def cost(flops, mib):
    return pl.CostEstimate(flops=int(flops), bytes_accessed=int(mib * (1 << 20)), transcendentals=0)


def whole(*shape):
    return pl.BlockSpec(shape, lambda c, *_: (0,) * len(shape))


def by_row(rows, width):
    return pl.BlockSpec((rows, width), lambda c, *_: (c, 0))


def by_col(rows, width):
    return pl.BlockSpec((rows, width), lambda c, *_: (0, c))


def first_half(rows, width):
    return pl.BlockSpec((rows, width), lambda c, *_: (jnp.minimum(c, STEPS // 2 - 1), 0))


def second_half(rows, width):
    return pl.BlockSpec((rows, width), lambda c, *_: (jnp.maximum(c - STEPS // 2, 0), 0))


AFTER = pl.BlockSpec(memory_space=pl.ANY)
BASIS = [whole(GROUP, GROUP)] * 2
GOT = [first_half(GROUP, ROWS), second_half(GROUP, ROWS)]
BF16, F32 = jnp.bfloat16, jnp.float32
INDEX = pl.BlockSpec((KV // BLOCK, KEEP, ROWS), lambda c, *_: (0, 0, 0))
INDEX_STEP = pl.BlockSpec((GROUP // BLOCK, KEEP, ROWS), lambda c, *_: (c, 0, 0))
MESSAGE = whole(HALF, 2 * TOK)
PIECE = whole(TOK, ROWS)
DENSE = pltpu.VMEM((KV, 2 * ROWS), BF16)
PAIRS = pltpu.VMEM((PICKS, 2 * ROWS), F32)
VALUES = pltpu.VMEM((2, TILES, 8, LANES), F32)


def shape(*dims, dtype=BF16):
    return jax.ShapeDtypeStruct(dims, dtype)


def body(tokens, cotangent, weight, momentum, kept_index):
    basis = dct_group()
    high = jnp.asarray(basis).astype(BF16)
    low = (jnp.asarray(basis) - high.astype(F32)).astype(BF16)
    place = jnp.stack([lax.axis_index("fsdp"), lax.axis_index("rep")]).astype(jnp.int32)
    index_t = jnp.transpose(kept_index, (1, 2, 0))

    def up(x):
        return lax.ppermute(x, "fsdp", [(i, (i + 2) % 8) for i in range(8)])

    def down(x):
        return lax.ppermute(x, "fsdp", [(i, (i + 6) % 8) for i in range(8)])

    def across(x):
        return lax.ppermute(x, "fsdp", [(i, (i + 4) % 8) for i in range(8)])

    def swap(x):
        return lax.ppermute(x, "fsdp", [(i, i ^ 1) for i in range(8)])

    def columns(flip):
        return [pl.BlockSpec((TOK, ROWS), lambda c, s, d=d: (0, ((s[0] ^ flip) + 2 * d) & 7)) for d in range(4)]

    weight_peer = swap(weight)

    first_up, first_down, far_send, peer_0 = pl.pallas_call(
        pack_first_kernel,
        grid_spec=pltpu.PrefetchScalarGridSpec(
            num_scalar_prefetch=1,
            grid=(1,),
            in_specs=[pl.BlockSpec(memory_space=pltpu.HBM)] * 2,
            out_specs=[MESSAGE] * 2 + [PIECE] * 2,
            scratch_shapes=[pltpu.VMEM((TOK, HALF), BF16), pltpu.SemaphoreType.DMA((8,))],
        ),
        out_shape=[shape(HALF, 2 * TOK)] * 2 + [shape(TOK, ROWS)] * 2,
        compiler_params=params(),
        cost_estimate=cost(0, 4),
    )(place, cotangent, tokens)
    first_lo = up(first_up)
    first_hi = down(first_down)
    peer_far = across(far_send)

    relay, cot_b = pl.pallas_call(
        pack_second_kernel,
        grid=(1,),
        in_specs=[MESSAGE, pl.BlockSpec((TOK, HALF), lambda c: (0, 1)), AFTER],
        out_specs=[whole(HALF, TOK)] * 2,
        out_shape=[shape(HALF, TOK)] * 2,
        compiler_params=params(),
        cost_estimate=cost(0, 1),
    )(first_lo, cotangent, first_hi)
    a_far = up(relay)
    b_lo, b_hi = up(cot_b), down(cot_b)
    b_far = down(b_hi)
    firsts = (first_up, first_hi, a_far, first_lo)
    cots_b = (cot_b, b_hi, b_far, b_lo)

    own_0, own_up, own_across, own_down = pl.pallas_call(
        pack_own_kernel,
        grid_spec=pltpu.PrefetchScalarGridSpec(
            num_scalar_prefetch=1,
            grid=(1,),
            in_specs=columns(0) + [AFTER, AFTER],
            out_specs=[PIECE] * 4,
        ),
        out_shape=[shape(TOK, ROWS)] * 4,
        compiler_params=params(),
        cost_estimate=cost(0, 2),
    )(place, tokens, tokens, tokens, tokens, b_lo, b_hi)
    owns = (own_0, down(own_down), across(own_across), up(own_up))

    partial_a = pl.pallas_call(
        partial_first_kernel,
        grid=(1,),
        in_specs=[MESSAGE] * 2 + [whole(HALF, TOK), MESSAGE, PIECE, PIECE, INDEX, AFTER, AFTER],
        out_specs=whole(HALF + PICKS, ROWS),
        out_shape=shape(HALF + PICKS, ROWS),
        compiler_params=params(),
        cost_estimate=cost(KV * KV * ROWS, 3),
    )(*firsts, peer_0, peer_far, index_t, weight_peer, cot_b)
    got_a = swap(partial_a)
    partial_b = pl.pallas_call(
        partial_second_kernel,
        grid=(1,),
        in_specs=[whole(HALF, TOK)] * 4 + [PIECE, MESSAGE, PIECE, MESSAGE],
        out_specs=whole(HALF, ROWS),
        out_shape=shape(HALF, ROWS),
        compiler_params=params(),
        cost_estimate=cost(KV * KV * ROWS, 3),
    )(*cots_b, peer_0, first_hi, peer_far, first_lo)
    got_b = swap(partial_b)

    pre = pl.pallas_call(
        own_kernel,
        grid=(STEPS,),
        in_specs=[first_half(GROUP, 2 * TOK)] * 2
        + [first_half(GROUP, TOK), first_half(GROUP, 2 * TOK)]
        + [second_half(GROUP, TOK)] * 4
        + [PIECE] * 4
        + [by_col(ROWS, GROUP)],
        out_specs=by_row(GROUP, ROWS),
        out_shape=shape(KV, ROWS, dtype=F32),
        compiler_params=params(),
        cost_estimate=cost(2 * KV * KV * ROWS, 7),
    )(*firsts, *cots_b, *owns, momentum[0])

    base, base_up, base_across, base_down = pl.pallas_call(
        base_kernel,
        grid_spec=pltpu.PrefetchScalarGridSpec(
            num_scalar_prefetch=1,
            grid=(1,),
            in_specs=[PIECE] * 5
            + [MESSAGE, PIECE, MESSAGE]
            + [whole(ROWS, KV)] * 2
            + [INDEX, whole(HALF + PICKS, ROWS)],
            out_specs=[whole(TOK + PICKS, KV)] * 4,
        ),
        out_shape=[shape(TOK + PICKS, KV)] * 4,
        compiler_params=params(2 * VMEM_LIMIT),
        cost_estimate=cost(4 * KV * KV * ROWS, 7),
    )(place, *owns, peer_0, first_hi, peer_far, first_lo, weight, weight_peer, index_t, got_a)
    base_lo, base_hi, base_far = up(base_up), down(base_down), across(base_across)

    halves = whole(TILES // 2, 8, LANES)
    half_shape = shape(TILES // 2, 8, LANES, dtype=F32)
    moment, picked, keep, send = pl.pallas_call(
        pick_kernel,
        grid_spec=pltpu.PrefetchScalarGridSpec(
            num_scalar_prefetch=1,
            grid=(STEPS,),
            in_specs=[by_row(GROUP, ROWS)] + GOT + [INDEX_STEP] + BASIS + [AFTER],
            out_specs=[by_row(GROUP, ROWS), by_row(PICKS // STEPS, ROWS), halves, halves],
        ),
        out_shape=[shape(KV, ROWS, dtype=F32), shape(PICKS, ROWS, dtype=F32), half_shape, half_shape],
        compiler_params=params(),
        cost_estimate=cost(6 * KV * GROUP * ROWS, 6),
    )(place, pre, got_a, got_b, index_t, high, low, base)

    def partner(x, bits):
        return lax.ppermute(x, "rep", [(i, i ^ bits) for i in range(REPS)])

    def add(kernel, result, *parts, after=()):
        return pl.pallas_call(
            kernel,
            grid=(1,),
            in_specs=[halves] * len(parts) + [AFTER] * len(after),
            out_specs=halves,
            out_shape=result,
            compiler_params=params(),
            cost_estimate=cost(0, 0.25),
        )(*parts, *after)

    value = add(add_two_kernel, half_shape, keep, partner(send, 1))
    value = add(add_two_kernel, half_shape, value, partner(value, 2))
    value = add(add_two_kernel, half_shape, value, partner(value, 4))
    value = add(add_two_kernel, half_shape, value, partner(value, 8))
    last = partner(value, 16)
    new_momentum, mark = pl.pallas_call(
        residual_kernel,
        grid=(STEPS,),
        in_specs=[by_row(GROUP, ROWS), by_row(PICKS // STEPS, ROWS), INDEX_STEP] + BASIS + [AFTER],
        out_specs=[by_col(ROWS, GROUP), whole(8, LANES)],
        out_shape=[shape(ROWS, KV, dtype=F32), shape(8, LANES, dtype=F32)],
        compiler_params=params(),
        cost_estimate=cost(6 * KV * GROUP * ROWS, 5),
    )(moment, picked, index_t, high, low, value)
    half = add(add_two_kernel, shape(TILES // 2, 8, LANES), value, last, after=(mark,))

    corner = lax.ppermute(half, ("rep", "fsdp"), [(i, i ^ 9) for i in range(REPS * 8)])
    pair_spec = whole(2, TILES, 8, LANES)
    pair = pl.pallas_call(
        pair_kernel,
        grid_spec=pltpu.PrefetchScalarGridSpec(
            num_scalar_prefetch=1,
            grid=(1,),
            in_specs=[halves] * 4 + [AFTER] * 3,
            out_specs=pair_spec,
        ),
        out_shape=shape(2, TILES, 8, LANES),
        compiler_params=params(),
        cost_estimate=cost(0, 0.25),
    )(place, half, partner(half, 1), swap(half), corner, base_lo, base_hi, base_far)
    pair_far, pair_lo, pair_hi = across(pair), up(pair), down(pair)

    def token_block(d):
        return pl.BlockSpec((TOK, 2 * ROWS), lambda c, s: (0, ((s[0] >> 1) + d) & 3))

    mixed, new_weight = pl.pallas_call(
        forward_own_kernel,
        grid_spec=pltpu.PrefetchScalarGridSpec(
            num_scalar_prefetch=1,
            grid=(1,),
            in_specs=[token_block(0), whole(TOK + PICKS, KV), pair_spec, whole(ROWS, KV)] + BASIS,
            out_specs=[whole(KV, TOK), whole(ROWS, KV)],
            scratch_shapes=[DENSE, PAIRS, VALUES],
        ),
        out_shape=[shape(KV, TOK, dtype=F32), shape(ROWS, KV)],
        compiler_params=params(),
        cost_estimate=cost(3 * KV * KV * ROWS, 4),
    )(place, tokens, base, pair, weight, high, low)

    projected = pl.pallas_call(
        forward_kernel,
        grid_spec=pltpu.PrefetchScalarGridSpec(
            num_scalar_prefetch=1,
            grid=(1,),
            in_specs=[token_block(d) for d in (1, 2, 3)]
            + [whole(TOK + PICKS, KV)] * 4
            + [pair_spec] * 3
            + [whole(KV, TOK)]
            + BASIS,
            out_specs=whole(TOK, KV),
            scratch_shapes=[DENSE] * 3 + [PAIRS] * 3 + [VALUES] * 3 + [pltpu.VMEM((KV, TOK), F32)],
        ),
        out_shape=shape(TOK, KV),
        compiler_params=params(2 * VMEM_LIMIT),
        cost_estimate=cost(6 * KV * KV * ROWS, 7),
    )(place, tokens, tokens, tokens, base, base_hi, base_far, base_lo, pair_hi, pair_far, pair_lo, mixed, high, low)
    return (projected, new_weight, new_momentum[None])


def solution(mesh):
    in_specs = (
        P(("rep", "fsdp"), None),
        P(("rep", "fsdp"), None),
        P("fsdp", None),
        P("rep", "fsdp", None),
        P("fsdp", None, None),
    )
    out_specs = (P(("rep", "fsdp"), None), P("fsdp", None), P("rep", "fsdp", None))
    return jax.shard_map(body, mesh=mesh, in_specs=in_specs, out_specs=out_specs, check_vma=False)
```

```python
import jax
import jax.numpy as jnp
import numpy as np
from jax import lax
from jax.experimental import pallas as pl
from jax.experimental.pallas import tpu as pltpu
from jax.sharding import PartitionSpec as P

beta_decay = 0.9
step_rate = 0.5
ROWS = 512
KV = 1024
TOK = 256
BLOCK = 64
KEEP = 4
HALF = KV // 2
GROUP = 256
STEPS = KV // GROUP
PICKS = KV // BLOCK * KEEP
LANES = 128
PACK = 16
REPS = 32
TILES = PICKS * ROWS // (8 * LANES)
VMEM_LIMIT = 16 * 1024 * 1024


def dct_group():
    n = np.arange(BLOCK, dtype=np.float64)
    single = np.cos(np.pi * (2.0 * n[None, :] + 1.0) * n[:, None] / (2 * BLOCK))
    single *= np.where(n[:, None] == 0, np.sqrt(1.0 / BLOCK), np.sqrt(2.0 / BLOCK))
    return np.kron(np.eye(GROUP // BLOCK), single).astype(np.float32)


def split_pair(values):
    high = values.astype(jnp.bfloat16)
    return high, (values - high.astype(jnp.float32)).astype(jnp.bfloat16)


def mix(left, right, dims):
    return lax.dot_general(left, right, (dims, ((), ())), preferred_element_type=jnp.float32)


def three_pass(left_pair, right_pair, dims):
    return (
        mix(left_pair[0], right_pair[0], dims)
        + mix(left_pair[0], right_pair[1], dims)
        + mix(left_pair[1], right_pair[0], dims)
    )


def expand_block(index_rows, value_rows, width):
    freq = lax.broadcasted_iota(jnp.int32, (BLOCK, width), 0)
    dense = jnp.zeros((BLOCK, width), jnp.float32)
    for j in range(KEEP):
        dense = jnp.where(index_rows[j] == freq, value_rows[j], dense)
    return dense


def spread_row(row):
    return jnp.broadcast_to(row, (PACK, LANES)).astype(jnp.bfloat16)


def expand_tile(indices, values, dense, first, cols):
    freq = lax.broadcasted_iota(jnp.int32, (PACK, LANES), 0).astype(jnp.float32)
    for half in range(2):
        at = [spread_row(indices(half * KEEP + j)) for j in range(KEEP)]
        have = [spread_row(values(half * KEEP + j)) for j in range(KEEP)]
        for part in range(BLOCK // PACK):
            here = (freq + part * PACK).astype(jnp.bfloat16)
            tile = jnp.zeros((PACK, LANES), jnp.bfloat16)
            for j in range(KEEP):
                tile = jnp.where(at[j] == here, have[j], tile)
            start = first + half * BLOCK + part * PACK
            dense[start : start + PACK, cols] = tile


def four_products(cots, toks):
    total = jnp.dot(cots[0], toks[0], preferred_element_type=jnp.float32)
    for c, t in zip(cots[1:], toks[1:]):
        total += jnp.dot(c, t, preferred_element_type=jnp.float32)
    return total


def cot_of(message):
    return message[:, :TOK]


def tok_of(message):
    return jnp.concatenate([message[:TOK, TOK:], message[TOK:, TOK:]], axis=1)


def flat_index(idx):
    rows = [idx[b].astype(jnp.float32) for b in range(KV // BLOCK)]
    return jnp.concatenate(rows, axis=0).astype(jnp.bfloat16)


def pack_first_kernel(where, cot, t0, t1, t2, t3, to_up, to_far, to_down, mine):
    turned = cot[...].T
    for out, t in ((to_up, t1), (to_far, t2), (to_down, t3)):
        out[:, :TOK] = turned
        out[:TOK, TOK:] = t[:, :TOK]
        out[TOK:, TOK:] = t[:, TOK:]
    mine[...] = t0[...]


def pack_second_kernel(cot, late_lo, late_hi, out):
    out[...] = cot[...].T


def pack_own_kernel(where, t0, t1, t2, t3, late_lo, late_hi, mine, to_up, to_far, to_down):
    for out, t in ((mine, t0), (to_up, t1), (to_far, t2), (to_down, t3)):
        out[...] = t[...]


def partial_first_kernel(sent, hi, far, lo, t0, idx, early, turned, out):
    cots = (cot_of(sent), cot_of(hi), cot_of(far), cot_of(lo))
    toks = (t0[...], tok_of(hi), tok_of(far), tok_of(lo))
    out[:HALF, :] = four_products(cots, toks).astype(out.dtype)
    out[HALF:, :] = flat_index(idx)


def partial_second_kernel(c0, c1, c2, c3, t0, hi, far, lo, out):
    cots = (c0[...], c1[...], c2[...], c3[...])
    toks = (t0[...], tok_of(hi), tok_of(far), tok_of(lo))
    out[...] = four_products(cots, toks).astype(out.dtype)


def own_kernel(a0, a1, a2, a3, b0, b1, b2, b3, t0, t1, t2, t3, mom, out):
    step = pl.program_id(0)
    toks = (t0[...], t1[...], t2[...], t3[...])

    @pl.when(step < STEPS // 2)
    def _():
        cots = (cot_of(a0), cot_of(a1), cot_of(a2), cot_of(a3))
        out[...] = four_products(cots, toks) + beta_decay * mom[...].T

    @pl.when(step >= STEPS // 2)
    def _():
        cots = (b0[...], b1[...], b2[...], b3[...])
        out[...] = four_products(cots, toks) + beta_decay * mom[...].T


def pick_rows(moment, idx, ch, cl):
    spectrum = three_pass((ch[...], cl[...]), split_pair(moment), ((1,), (0,)))
    freq = lax.broadcasted_iota(jnp.int32, (BLOCK, ROWS), 0)
    rows = []
    for b in range(GROUP // BLOCK):
        part = spectrum[b * BLOCK : (b + 1) * BLOCK, :]
        for j in range(KEEP):
            here = idx[b, j : j + 1, :] == freq
            rows.append(jnp.sum(jnp.where(here, part, 0.0), axis=0, keepdims=True))
    return rows


def pick_kernel(where, pre, got_a, got_b, idx, ch, cl, late, moment, picked, keep, send):
    step = pl.program_id(0)
    first = step < STEPS // 2
    got = jnp.where(first, got_a[...], got_b[...]).astype(jnp.float32)
    total = pre[...] + got
    moment[...] = total
    values = jnp.concatenate(pick_rows(total, idx, ch, cl), axis=0)
    picked[...] = values

    def put(out):
        for t in range(GROUP // BLOCK * KEEP // 8):
            for q in range(ROWS // LANES):
                tile = values[t * 8 : (t + 1) * 8, q * LANES : (q + 1) * LANES]
                out[(step & 1) * (TILES // STEPS) + t * (ROWS // LANES) + q] = tile

    here = (step >> 1) == (where[1] & 1)
    pl.when(here)(lambda: put(keep))
    pl.when(jnp.logical_not(here))(lambda: put(send))


def add_two_kernel(a, b, *rest):
    out = rest[-1]
    out[...] = (a[...] + b[...]).astype(out.dtype)


def pair_kernel(where, half, core, across, corner, late_0, late_1, late_2, out):
    side, mine = where[0] & 1, (where[1] & 1) * (TILES // 2)
    other = TILES // 2 - mine
    out[side, pl.ds(mine, TILES // 2)] = half[...]
    out[side, pl.ds(other, TILES // 2)] = core[...]
    out[1 - side, pl.ds(mine, TILES // 2)] = across[...]
    out[1 - side, pl.ds(other, TILES // 2)] = corner[...]


def residual_kernel(moment, picked, idx, ch, cl, late, out, mark):
    parts = []
    for b in range(GROUP // BLOCK):
        at = [idx[b, j : j + 1, :] for j in range(KEEP)]
        have = [picked[b * KEEP + j : b * KEEP + j + 1, :] for j in range(KEEP)]
        parts.append(expand_block(at, have, ROWS))
    kept = jnp.concatenate(parts, axis=0)
    back = three_pass((ch[...], cl[...]), split_pair(kept), ((0,), (0,)))
    out[...] = (moment[...] - back).T
    mark[...] = back[:8, :LANES]


def base_kernel(where, o0, o1, o2, o3, p0, p1, p2, p3, w_own, w_peer, idx, got_a, *outs):
    mine, theirs = flat_index(idx), got_a[HALF:, :]
    first = (where[0] & 1) == 0
    left, right = jnp.where(first, mine, theirs), jnp.where(first, theirs, mine)
    peers = (p0[...], tok_of(p1), tok_of(p2), tok_of(p3))
    for own, peer, out in zip((o0, o1, o2, o3), peers, outs):
        total = jnp.dot(own[...], w_own[...], preferred_element_type=jnp.float32)
        total += jnp.dot(peer, w_peer[...], preferred_element_type=jnp.float32)
        out[:TOK, :] = total.astype(out.dtype)
        out[TOK:, :ROWS] = left
        out[TOK:, ROWS:] = right


def expand_group(g, pairs, tot, dense):
    for t in range(2 * g, 2 * g + 2):
        for f in range(2):
            for q in range(ROWS // LANES):
                cols = slice(f * ROWS + q * LANES, f * ROWS + (q + 1) * LANES)
                tile = t * (ROWS // LANES) + q
                expand_tile(
                    lambda s, t=t, cols=cols: pairs[t * 8 + s : t * 8 + s + 1, cols],
                    lambda s, f=f, tile=tile: tot[f, tile, s : s + 1, :],
                    dense,
                    t * 2 * BLOCK,
                    cols,
                )


def forward_own_kernel(where, tok, own, tot, weight, ch, cl, mixed, out_weight, dense, pairs, values):
    pairs[...] = own[TOK:, :].astype(jnp.float32)
    values[...] = tot[...].astype(jnp.float32)
    cols = pl.ds(pl.multiple_of((where[0] & 1) * ROWS, ROWS), ROWS)
    for g in range(STEPS):
        expand_group(g, pairs, values, dense)
        span = slice(g * GROUP, (g + 1) * GROUP)
        turned = dense[span, cols].T
        delta = mix(turned, ch[...], ((1,), (0,))) + mix(turned, cl[...], ((1,), (0,)))
        new = weight[:, span].astype(jnp.float32) - (step_rate / REPS) * delta
        out_weight[:, span] = new.astype(out_weight.dtype)
    mixed[...] = mix(dense[...], tok[...], ((1,), (1,)))


def expand_all(near, tot, dense, pairs, values):
    pairs[...] = near[TOK:, :].astype(jnp.float32)
    values[...] = tot[...].astype(jnp.float32)
    for g in range(STEPS):
        expand_group(g, pairs, values, dense)


def forward_near_kernel(where, tok_1, tok_3, hi, lo, tot_1, tot_3, before, out, *scratch):
    expand_all(hi, tot_1, scratch[0], scratch[2], scratch[4])
    total = before[...] + mix(scratch[0][...], tok_1[...], ((1,), (1,)))
    expand_all(lo, tot_3, scratch[1], scratch[3], scratch[5])
    out[...] = total + mix(scratch[1][...], tok_3[...], ((1,), (1,)))


def forward_far_kernel(where, tok, own, hi, far, lo, tot, before, ch, cl, out, dense, pairs, values, total):
    expand_all(far, tot, dense, pairs, values)
    total[...] = before[...] + mix(dense[...], tok[...], ((1,), (1,)))
    for g in range(STEPS):
        span = slice(g * GROUP, (g + 1) * GROUP)
        delta = three_pass(split_pair(total[span, :].T), (ch[...], cl[...]), ((1,), (0,)))
        base = own[:TOK, span].astype(jnp.float32) + hi[:TOK, span].astype(jnp.float32)
        base += far[:TOK, span].astype(jnp.float32) + lo[:TOK, span].astype(jnp.float32)
        out[:, span] = (base - (step_rate / REPS) * delta).astype(out.dtype)


def params(limit=VMEM_LIMIT):
    return pltpu.CompilerParams(vmem_limit_bytes=limit)


def cost(flops, mib):
    return pl.CostEstimate(flops=int(flops), bytes_accessed=int(mib * (1 << 20)), transcendentals=0)


def whole(*shape):
    return pl.BlockSpec(shape, lambda c, *_: (0,) * len(shape))


def by_row(rows, width):
    return pl.BlockSpec((rows, width), lambda c, *_: (c, 0))


def by_col(rows, width):
    return pl.BlockSpec((rows, width), lambda c, *_: (0, c))


def first_half(rows, width):
    return pl.BlockSpec((rows, width), lambda c, *_: (jnp.minimum(c, STEPS // 2 - 1), 0))


def second_half(rows, width):
    return pl.BlockSpec((rows, width), lambda c, *_: (jnp.maximum(c - STEPS // 2, 0), 0))


AFTER = pl.BlockSpec(memory_space=pl.ANY)
BASIS = [whole(GROUP, GROUP)] * 2
GOT = [first_half(GROUP, ROWS), second_half(GROUP, ROWS)]
BF16, F32 = jnp.bfloat16, jnp.float32
INDEX = pl.BlockSpec((KV // BLOCK, KEEP, ROWS), lambda c, *_: (0, 0, 0))
INDEX_STEP = pl.BlockSpec((GROUP // BLOCK, KEEP, ROWS), lambda c, *_: (c, 0, 0))
MESSAGE = whole(HALF, 2 * TOK)
PIECE = whole(TOK, ROWS)
DENSE = pltpu.VMEM((KV, 2 * ROWS), BF16)
PAIRS = pltpu.VMEM((PICKS, 2 * ROWS), F32)
VALUES = pltpu.VMEM((2, TILES, 8, LANES), F32)


def shape(*dims, dtype=BF16):
    return jax.ShapeDtypeStruct(dims, dtype)


def body(tokens, cotangent, weight, momentum, kept_index):
    basis = dct_group()
    high = jnp.asarray(basis).astype(BF16)
    low = (jnp.asarray(basis) - high.astype(F32)).astype(BF16)
    place = jnp.stack([lax.axis_index("fsdp"), lax.axis_index("rep")]).astype(jnp.int32)
    index_t = jnp.transpose(kept_index, (1, 2, 0))

    def up(x):
        return lax.ppermute(x, "fsdp", [(i, (i + 2) % 8) for i in range(8)])

    def down(x):
        return lax.ppermute(x, "fsdp", [(i, (i + 6) % 8) for i in range(8)])

    def across(x):
        return lax.ppermute(x, "fsdp", [(i, (i + 4) % 8) for i in range(8)])

    def swap(x):
        return lax.ppermute(x, "fsdp", [(i, i ^ 1) for i in range(8)])

    def columns(flip):
        return [pl.BlockSpec((TOK, ROWS), lambda c, s, d=d: (0, ((s[0] ^ flip) + 2 * d) & 7)) for d in range(4)]

    weight_peer = swap(weight)

    first_up, first_far, first_down, peer_0 = pl.pallas_call(
        pack_first_kernel,
        grid_spec=pltpu.PrefetchScalarGridSpec(
            num_scalar_prefetch=1,
            grid=(1,),
            in_specs=[whole(TOK, HALF)] + columns(1),
            out_specs=[MESSAGE] * 3 + [PIECE],
        ),
        out_shape=[shape(HALF, 2 * TOK)] * 3 + [shape(TOK, ROWS)],
        compiler_params=params(),
        cost_estimate=cost(0, 4),
    )(place, cotangent, tokens, tokens, tokens, tokens)
    first_lo = up(first_up)
    first_hi = down(first_down)
    first_x = across(first_far)
    firsts = (first_up, first_hi, first_x, first_lo)

    cot_b = pl.pallas_call(
        pack_second_kernel,
        grid=(1,),
        in_specs=[pl.BlockSpec((TOK, HALF), lambda c: (0, 1)), AFTER, AFTER],
        out_specs=whole(HALF, TOK),
        out_shape=shape(HALF, TOK),
        compiler_params=params(),
        cost_estimate=cost(0, 1),
    )(cotangent, first_lo, first_hi)
    b_lo, b_hi, b_far = up(cot_b), down(cot_b), across(cot_b)
    cots_b = (cot_b, b_hi, b_far, b_lo)

    own_0, own_up, own_across, own_down = pl.pallas_call(
        pack_own_kernel,
        grid_spec=pltpu.PrefetchScalarGridSpec(
            num_scalar_prefetch=1,
            grid=(1,),
            in_specs=columns(0) + [AFTER, AFTER],
            out_specs=[PIECE] * 4,
        ),
        out_shape=[shape(TOK, ROWS)] * 4,
        compiler_params=params(),
        cost_estimate=cost(0, 2),
    )(place, tokens, tokens, tokens, tokens, b_lo, b_hi)
    owns = (own_0, down(own_down), across(own_across), up(own_up))

    partial_a = pl.pallas_call(
        partial_first_kernel,
        grid=(1,),
        in_specs=[MESSAGE] * 4 + [PIECE, INDEX, AFTER, AFTER],
        out_specs=whole(HALF + PICKS, ROWS),
        out_shape=shape(HALF + PICKS, ROWS),
        compiler_params=params(),
        cost_estimate=cost(KV * KV * ROWS, 3),
    )(*firsts, peer_0, index_t, weight_peer, cot_b)
    got_a = swap(partial_a)
    partial_b = pl.pallas_call(
        partial_second_kernel,
        grid=(1,),
        in_specs=[whole(HALF, TOK)] * 4 + [PIECE] + [MESSAGE] * 3,
        out_specs=whole(HALF, ROWS),
        out_shape=shape(HALF, ROWS),
        compiler_params=params(),
        cost_estimate=cost(KV * KV * ROWS, 3),
    )(*cots_b, peer_0, *firsts[1:])
    got_b = swap(partial_b)

    pre = pl.pallas_call(
        own_kernel,
        grid=(STEPS,),
        in_specs=[first_half(GROUP, 2 * TOK)] * 4
        + [second_half(GROUP, TOK)] * 4
        + [PIECE] * 4
        + [by_col(ROWS, GROUP)],
        out_specs=by_row(GROUP, ROWS),
        out_shape=shape(KV, ROWS, dtype=F32),
        compiler_params=params(),
        cost_estimate=cost(2 * KV * KV * ROWS, 7),
    )(*firsts, *cots_b, *owns, momentum[0])

    base, base_up, base_across, base_down = pl.pallas_call(
        base_kernel,
        grid_spec=pltpu.PrefetchScalarGridSpec(
            num_scalar_prefetch=1,
            grid=(1,),
            in_specs=[PIECE] * 5
            + [MESSAGE] * 3
            + [whole(ROWS, KV)] * 2
            + [INDEX, whole(HALF + PICKS, ROWS)],
            out_specs=[whole(TOK + PICKS, KV)] * 4,
        ),
        out_shape=[shape(TOK + PICKS, KV)] * 4,
        compiler_params=params(2 * VMEM_LIMIT),
        cost_estimate=cost(4 * KV * KV * ROWS, 7),
    )(place, *owns, peer_0, *firsts[1:], weight, weight_peer, index_t, got_a)
    base_lo, base_hi, base_far = up(base_up), down(base_down), across(base_across)

    halves = whole(TILES // 2, 8, LANES)
    half_shape = shape(TILES // 2, 8, LANES, dtype=F32)
    moment, picked, keep, send = pl.pallas_call(
        pick_kernel,
        grid_spec=pltpu.PrefetchScalarGridSpec(
            num_scalar_prefetch=1,
            grid=(STEPS,),
            in_specs=[by_row(GROUP, ROWS)] + GOT + [INDEX_STEP] + BASIS + [AFTER],
            out_specs=[by_row(GROUP, ROWS), by_row(PICKS // STEPS, ROWS), halves, halves],
        ),
        out_shape=[shape(KV, ROWS, dtype=F32), shape(PICKS, ROWS, dtype=F32), half_shape, half_shape],
        compiler_params=params(),
        cost_estimate=cost(6 * KV * GROUP * ROWS, 6),
    )(place, pre, got_a, got_b, index_t, high, low, base)

    def partner(x, bits):
        return lax.ppermute(x, "rep", [(i, i ^ bits) for i in range(REPS)])

    def add(kernel, result, *parts, after=()):
        return pl.pallas_call(
            kernel,
            grid=(1,),
            in_specs=[halves] * len(parts) + [AFTER] * len(after),
            out_specs=halves,
            out_shape=result,
            compiler_params=params(),
            cost_estimate=cost(0, 0.25),
        )(*parts, *after)

    value = add(add_two_kernel, half_shape, keep, partner(send, 1))
    from_hi = partner(value, 2)

    value = add(add_two_kernel, half_shape, value, from_hi)
    value = add(add_two_kernel, half_shape, value, partner(value, 4))
    value = add(add_two_kernel, half_shape, value, partner(value, 8))
    last = partner(value, 16)
    new_momentum, mark = pl.pallas_call(
        residual_kernel,
        grid=(STEPS,),
        in_specs=[by_row(GROUP, ROWS), by_row(PICKS // STEPS, ROWS), INDEX_STEP] + BASIS + [AFTER],
        out_specs=[by_col(ROWS, GROUP), whole(8, LANES)],
        out_shape=[shape(ROWS, KV, dtype=F32), shape(8, LANES, dtype=F32)],
        compiler_params=params(),
        cost_estimate=cost(6 * KV * GROUP * ROWS, 5),
    )(moment, picked, index_t, high, low, value)
    half = add(add_two_kernel, shape(TILES // 2, 8, LANES), value, last, after=(mark,))

    corner = lax.ppermute(half, ("rep", "fsdp"), [(i, i ^ 9) for i in range(REPS * 8)])
    pair_spec = whole(2, TILES, 8, LANES)
    pair = pl.pallas_call(
        pair_kernel,
        grid_spec=pltpu.PrefetchScalarGridSpec(
            num_scalar_prefetch=1,
            grid=(1,),
            in_specs=[halves] * 4 + [AFTER] * 3,
            out_specs=pair_spec,
        ),
        out_shape=shape(2, TILES, 8, LANES),
        compiler_params=params(),
        cost_estimate=cost(0, 0.25),
    )(place, half, partner(half, 1), swap(half), corner, base_lo, base_hi, base_far)
    pair_far, pair_lo, pair_hi = across(pair), up(pair), down(pair)

    def token_block(d):
        return pl.BlockSpec((TOK, 2 * ROWS), lambda c, s: (0, ((s[0] >> 1) + d) & 3))

    mixed, new_weight = pl.pallas_call(
        forward_own_kernel,
        grid_spec=pltpu.PrefetchScalarGridSpec(
            num_scalar_prefetch=1,
            grid=(1,),
            in_specs=[token_block(0), whole(TOK + PICKS, KV), pair_spec, whole(ROWS, KV)] + BASIS,
            out_specs=[whole(KV, TOK), whole(ROWS, KV)],
            scratch_shapes=[DENSE, PAIRS, VALUES],
        ),
        out_shape=[shape(KV, TOK, dtype=F32), shape(ROWS, KV)],
        compiler_params=params(),
        cost_estimate=cost(3 * KV * KV * ROWS, 4),
    )(place, tokens, base, pair, weight, high, low)

    mixed = pl.pallas_call(
        forward_near_kernel,
        grid_spec=pltpu.PrefetchScalarGridSpec(
            num_scalar_prefetch=1,
            grid=(1,),
            in_specs=[token_block(1), token_block(3)]
            + [whole(TOK + PICKS, KV)] * 2
            + [pair_spec] * 2
            + [whole(KV, TOK)],
            out_specs=whole(KV, TOK),
            scratch_shapes=[DENSE] * 2 + [PAIRS] * 2 + [VALUES] * 2,
        ),
        out_shape=shape(KV, TOK, dtype=F32),
        compiler_params=params(2 * VMEM_LIMIT),
        cost_estimate=cost(4 * KV * KV * ROWS, 5),
    )(place, tokens, tokens, base_hi, base_lo, pair_hi, pair_lo, mixed)

    projected = pl.pallas_call(
        forward_far_kernel,
        grid_spec=pltpu.PrefetchScalarGridSpec(
            num_scalar_prefetch=1,
            grid=(1,),
            in_specs=[token_block(2)]
            + [whole(TOK + PICKS, KV)] * 4
            + [pair_spec, whole(KV, TOK)]
            + BASIS,
            out_specs=whole(TOK, KV),
            scratch_shapes=[DENSE, PAIRS, VALUES, pltpu.VMEM((KV, TOK), F32)],
        ),
        out_shape=shape(TOK, KV),
        compiler_params=params(2 * VMEM_LIMIT),
        cost_estimate=cost(3 * KV * KV * ROWS, 5),
    )(place, tokens, base, base_hi, base_far, base_lo, pair_far, mixed, high, low)
    return (projected, new_weight, new_momentum[None])


def solution(mesh):
    in_specs = (
        P(("rep", "fsdp"), None),
        P(("rep", "fsdp"), None),
        P("fsdp", None),
        P("rep", "fsdp", None),
        P("fsdp", None, None),
    )
    out_specs = (P(("rep", "fsdp"), None), P("fsdp", None), P("rep", "fsdp", None))
    return jax.shard_map(body, mesh=mesh, in_specs=in_specs, out_specs=out_specs, check_vma=False)
```

```python
import jax
import jax.numpy as jnp
import numpy as np
from jax import lax
from jax.experimental import pallas as pl
from jax.experimental.pallas import tpu as pltpu
from jax.sharding import PartitionSpec as P

beta_decay = 0.9
step_rate = 0.5
ROWS = 512
KV = 1024
TOK = 256
BLOCK = 64
KEEP = 4
HALF = KV // 2
GROUP = 256
STEPS = KV // GROUP
PICKS = KV // BLOCK * KEEP
LANES = 128
PACK = 16
REPS = 32
TILES = PICKS * ROWS // (8 * LANES)
VMEM_LIMIT = 16 * 1024 * 1024


def dct_group():
    n = np.arange(BLOCK, dtype=np.float64)
    single = np.cos(np.pi * (2.0 * n[None, :] + 1.0) * n[:, None] / (2 * BLOCK))
    single *= np.where(n[:, None] == 0, np.sqrt(1.0 / BLOCK), np.sqrt(2.0 / BLOCK))
    return np.kron(np.eye(GROUP // BLOCK), single).astype(np.float32)


def split_pair(values):
    high = values.astype(jnp.bfloat16)
    return high, (values - high.astype(jnp.float32)).astype(jnp.bfloat16)


def mix(left, right, dims):
    return lax.dot_general(left, right, (dims, ((), ())), preferred_element_type=jnp.float32)


def three_pass(left_pair, right_pair, dims):
    return (
        mix(left_pair[0], right_pair[0], dims)
        + mix(left_pair[0], right_pair[1], dims)
        + mix(left_pair[1], right_pair[0], dims)
    )


def expand_block(index_rows, value_rows, width):
    freq = lax.broadcasted_iota(jnp.int32, (BLOCK, width), 0)
    dense = jnp.zeros((BLOCK, width), jnp.float32)
    for j in range(KEEP):
        dense = jnp.where(index_rows[j] == freq, value_rows[j], dense)
    return dense


def spread_row(row):
    return jnp.broadcast_to(row, (PACK, LANES)).astype(jnp.bfloat16)


def expand_tile(indices, values, dense, first, cols):
    freq = lax.broadcasted_iota(jnp.int32, (PACK, LANES), 0).astype(jnp.float32)
    for half in range(2):
        at = [spread_row(indices(half * KEEP + j)) for j in range(KEEP)]
        have = [spread_row(values(half * KEEP + j)) for j in range(KEEP)]
        for part in range(BLOCK // PACK):
            here = (freq + part * PACK).astype(jnp.bfloat16)
            tile = jnp.zeros((PACK, LANES), jnp.bfloat16)
            for j in range(KEEP):
                tile = jnp.where(at[j] == here, have[j], tile)
            start = first + half * BLOCK + part * PACK
            dense[start : start + PACK, cols] = tile


def four_products(cots, toks):
    total = jnp.dot(cots[0], toks[0], preferred_element_type=jnp.float32)
    for c, t in zip(cots[1:], toks[1:]):
        total += jnp.dot(c, t, preferred_element_type=jnp.float32)
    return total


def cot_of(message):
    return message[:, :TOK]


def tok_of(message):
    return jnp.concatenate([message[:TOK, TOK:], message[TOK:, TOK:]], axis=1)


def flat_index(idx):
    rows = [idx[b].astype(jnp.float32) for b in range(KV // BLOCK)]
    return jnp.concatenate(rows, axis=0).astype(jnp.bfloat16)


def pack_first_kernel(where, cot, t0, t1, t2, t3, to_up, to_far, to_down, mine):
    turned = cot[...].T
    for out, t in ((to_up, t1), (to_far, t2), (to_down, t3)):
        out[:, :TOK] = turned
        out[:TOK, TOK:] = t[:, :TOK]
        out[TOK:, TOK:] = t[:, TOK:]
    mine[...] = t0[...]


def pack_second_kernel(cot, late_lo, late_hi, out):
    out[...] = cot[...].T


def pack_own_kernel(where, t0, t1, t2, t3, late_lo, late_hi, mine, to_up, to_far, to_down):
    for out, t in ((mine, t0), (to_up, t1), (to_far, t2), (to_down, t3)):
        out[...] = t[...]


def partial_first_kernel(sent, hi, far, lo, t0, idx, early, turned, out):
    cots = (cot_of(sent), cot_of(hi), cot_of(far), cot_of(lo))
    toks = (t0[...], tok_of(hi), tok_of(far), tok_of(lo))
    out[:HALF, :] = four_products(cots, toks).astype(out.dtype)
    out[HALF:, :] = flat_index(idx)


def partial_second_kernel(c0, c1, c2, c3, t0, hi, far, lo, out):
    cots = (c0[...], c1[...], c2[...], c3[...])
    toks = (t0[...], tok_of(hi), tok_of(far), tok_of(lo))
    out[...] = four_products(cots, toks).astype(out.dtype)


def pick_rows(moment, idx, ch, cl):
    upper, lower = split_pair(moment)
    both = jnp.concatenate([ch[...], cl[...]], axis=0)
    product = jnp.dot(both, upper, preferred_element_type=jnp.float32)
    spectrum = product[:GROUP] + product[GROUP:]
    spectrum += jnp.dot(ch[...], lower, preferred_element_type=jnp.float32)
    freq = lax.broadcasted_iota(jnp.int32, (BLOCK, ROWS), 0)
    rows = []
    for b in range(GROUP // BLOCK):
        part = spectrum[b * BLOCK : (b + 1) * BLOCK, :]
        for j in range(KEEP):
            here = idx[b, j : j + 1, :] == freq
            rows.append(jnp.sum(jnp.where(here, part, 0.0), axis=0, keepdims=True))
    return rows


def pick_kernel(
    where, a0, a1, a2, a3, b0, b1, b2, b3, t0, t1, t2, t3, mom, got_a, got_b, idx, ch, cl, late, moment, picked, keep, send
):
    step = pl.program_id(0)
    toks = (t0[...], t1[...], t2[...], t3[...])

    @pl.when(step < STEPS // 2)
    def _():
        cots = (cot_of(a0), cot_of(a1), cot_of(a2), cot_of(a3))
        moment[...] = four_products(cots, toks) + got_a[...].astype(jnp.float32)

    @pl.when(step >= STEPS // 2)
    def _():
        cots = (b0[...], b1[...], b2[...], b3[...])
        moment[...] = four_products(cots, toks) + got_b[...].astype(jnp.float32)

    total = moment[...] + beta_decay * mom[...].T
    moment[...] = total
    values = jnp.concatenate(pick_rows(total, idx, ch, cl), axis=0)
    picked[...] = values

    def put(out):
        for t in range(GROUP // BLOCK * KEEP // 8):
            for q in range(ROWS // LANES):
                tile = values[t * 8 : (t + 1) * 8, q * LANES : (q + 1) * LANES]
                out[(step & 1) * (TILES // STEPS) + t * (ROWS // LANES) + q] = tile

    here = (step >> 1) == (where[1] & 1)
    pl.when(here)(lambda: put(keep))
    pl.when(jnp.logical_not(here))(lambda: put(send))


def add_two_kernel(a, b, *rest):
    out = rest[-1]
    out[...] = (a[...] + b[...]).astype(out.dtype)


def pair_kernel(where, half, core, across, corner, late_0, late_1, late_2, out):
    side, mine = where[0] & 1, (where[1] & 1) * (TILES // 2)
    other = TILES // 2 - mine
    out[side, pl.ds(mine, TILES // 2)] = half[...]
    out[side, pl.ds(other, TILES // 2)] = core[...]
    out[1 - side, pl.ds(mine, TILES // 2)] = across[...]
    out[1 - side, pl.ds(other, TILES // 2)] = corner[...]


def residual_kernel(moment, picked, idx, ch, cl, late, out, mark):
    parts = []
    for b in range(GROUP // BLOCK):
        at = [idx[b, j : j + 1, :] for j in range(KEEP)]
        have = [picked[b * KEEP + j : b * KEEP + j + 1, :] for j in range(KEEP)]
        parts.append(expand_block(at, have, ROWS))
    kept = jnp.concatenate(parts, axis=0)
    back = three_pass((ch[...], cl[...]), split_pair(kept), ((0,), (0,)))
    out[...] = (moment[...] - back).T
    mark[...] = back[:8, :LANES]


def base_kernel(where, o0, o1, o2, o3, p0, p1, p2, p3, w_own, w_peer, idx, got_a, *outs):
    pairs, outs = outs[-1], outs[:-1]
    step = pl.program_id(0)

    @pl.when(step == 0)
    def _():
        mine, theirs = flat_index(idx), got_a[HALF:, :]
        first = (where[0] & 1) == 0
        pairs[:, :ROWS] = jnp.where(first, mine, theirs)
        pairs[:, ROWS:] = jnp.where(first, theirs, mine)

    here = pairs[:, pl.ds(pl.multiple_of(step * GROUP, GROUP), GROUP)]
    peers = (p0[...], tok_of(p1), tok_of(p2), tok_of(p3))
    for own, peer, out in zip((o0, o1, o2, o3), peers, outs):
        total = jnp.dot(own[...], w_own[...], preferred_element_type=jnp.float32)
        total += jnp.dot(peer, w_peer[...], preferred_element_type=jnp.float32)
        out[:TOK, :] = total.astype(out.dtype)
        out[TOK:, :] = here


def expand_group(g, pairs, tot, dense):
    for t in range(2 * g, 2 * g + 2):
        for f in range(2):
            for q in range(ROWS // LANES):
                cols = slice(f * ROWS + q * LANES, f * ROWS + (q + 1) * LANES)
                tile = t * (ROWS // LANES) + q
                expand_tile(
                    lambda s, t=t, cols=cols: pairs[t * 8 + s : t * 8 + s + 1, cols],
                    lambda s, f=f, tile=tile: tot[f, tile, s : s + 1, :],
                    dense,
                    t * 2 * BLOCK,
                    cols,
                )


def forward_own_kernel(where, tok, own, hi, far, lo, tot, weight, ch, cl, mixed, out_weight, base, dense, pairs, values):
    pairs[...] = own[TOK:, :].astype(jnp.float32)
    values[...] = tot[...].astype(jnp.float32)
    cols = pl.ds(pl.multiple_of((where[0] & 1) * ROWS, ROWS), ROWS)
    for g in range(STEPS):
        expand_group(g, pairs, values, dense)
        span = slice(g * GROUP, (g + 1) * GROUP)
        turned = dense[span, cols].T
        delta = mix(turned, ch[...], ((1,), (0,))) + mix(turned, cl[...], ((1,), (0,)))
        new = weight[:, span].astype(jnp.float32) - (step_rate / REPS) * delta
        out_weight[:, span] = new.astype(out_weight.dtype)
    mixed[...] = mix(dense[...], tok[...], ((1,), (1,)))
    near = own[:TOK, :].astype(jnp.float32) + hi[:TOK, :].astype(jnp.float32)
    base[...] = near + far[:TOK, :].astype(jnp.float32) + lo[:TOK, :].astype(jnp.float32)


def expand_all(index, tot, dense, pairs, values):
    pairs[...] = index[...].astype(jnp.float32)
    values[...] = tot[...].astype(jnp.float32)
    for g in range(STEPS):
        expand_group(g, pairs, values, dense)


def forward_near_kernel(where, tok_1, tok_3, hi, lo, tot_1, tot_3, before, out, *scratch):
    expand_all(hi, tot_1, scratch[0], scratch[2], scratch[4])
    total = before[...] + mix(scratch[0][...], tok_1[...], ((1,), (1,)))
    expand_all(lo, tot_3, scratch[1], scratch[3], scratch[5])
    out[...] = total + mix(scratch[1][...], tok_3[...], ((1,), (1,)))


def forward_far_kernel(where, tok, base, far, tot, before, ch, cl, out, dense, pairs, values, total):
    expand_all(far, tot, dense, pairs, values)
    total[...] = before[...] + mix(dense[...], tok[...], ((1,), (1,)))
    groups = [total[g * GROUP : (g + 1) * GROUP, :].T for g in range(STEPS)]
    delta = three_pass(split_pair(jnp.concatenate(groups, axis=0)), (ch[...], cl[...]), ((1,), (0,)))
    for g in range(STEPS):
        span = slice(g * GROUP, (g + 1) * GROUP)
        part = delta[g * TOK : (g + 1) * TOK]
        out[:, span] = (base[:, span] - (step_rate / REPS) * part).astype(out.dtype)


def params(limit=VMEM_LIMIT):
    return pltpu.CompilerParams(vmem_limit_bytes=limit)


def cost(flops, mib):
    return pl.CostEstimate(flops=int(flops), bytes_accessed=int(mib * (1 << 20)), transcendentals=0)


def whole(*shape):
    return pl.BlockSpec(shape, lambda c, *_: (0,) * len(shape))


def by_row(rows, width):
    return pl.BlockSpec((rows, width), lambda c, *_: (c, 0))


def by_col(rows, width):
    return pl.BlockSpec((rows, width), lambda c, *_: (0, c))


def first_half(rows, width):
    return pl.BlockSpec((rows, width), lambda c, *_: (jnp.minimum(c, STEPS // 2 - 1), 0))


def second_half(rows, width):
    return pl.BlockSpec((rows, width), lambda c, *_: (jnp.maximum(c - STEPS // 2, 0), 0))


AFTER = pl.BlockSpec(memory_space=pl.ANY)
BASIS = [whole(GROUP, GROUP)] * 2
GOT = [first_half(GROUP, ROWS), second_half(GROUP, ROWS)]
BF16, F32 = jnp.bfloat16, jnp.float32
INDEX = pl.BlockSpec((KV // BLOCK, KEEP, ROWS), lambda c, *_: (0, 0, 0))
INDEX_STEP = pl.BlockSpec((GROUP // BLOCK, KEEP, ROWS), lambda c, *_: (c, 0, 0))
MESSAGE = whole(HALF, 2 * TOK)
PIECE = whole(TOK, ROWS)
DENSE = pltpu.VMEM((KV, 2 * ROWS), BF16)
PAIRS = pltpu.VMEM((PICKS, 2 * ROWS), F32)
VALUES = pltpu.VMEM((2, TILES, 8, LANES), F32)


def shape(*dims, dtype=BF16):
    return jax.ShapeDtypeStruct(dims, dtype)


def body(tokens, cotangent, weight, momentum, kept_index):
    basis = dct_group()
    high = jnp.asarray(basis).astype(BF16)
    low = (jnp.asarray(basis) - high.astype(F32)).astype(BF16)
    place = jnp.stack([lax.axis_index("fsdp"), lax.axis_index("rep")]).astype(jnp.int32)
    index_t = jnp.transpose(kept_index, (1, 2, 0))

    def up(x):
        return lax.ppermute(x, "fsdp", [(i, (i + 2) % 8) for i in range(8)])

    def down(x):
        return lax.ppermute(x, "fsdp", [(i, (i + 6) % 8) for i in range(8)])

    def across(x):
        return lax.ppermute(x, "fsdp", [(i, (i + 4) % 8) for i in range(8)])

    def swap(x):
        return lax.ppermute(x, "fsdp", [(i, i ^ 1) for i in range(8)])

    def columns(flip):
        return [pl.BlockSpec((TOK, ROWS), lambda c, s, d=d: (0, ((s[0] ^ flip) + 2 * d) & 7)) for d in range(4)]

    weight_peer = swap(weight)

    first_up, first_far, first_down, peer_0 = pl.pallas_call(
        pack_first_kernel,
        grid_spec=pltpu.PrefetchScalarGridSpec(
            num_scalar_prefetch=1,
            grid=(1,),
            in_specs=[whole(TOK, HALF)] + columns(1),
            out_specs=[MESSAGE] * 3 + [PIECE],
        ),
        out_shape=[shape(HALF, 2 * TOK)] * 3 + [shape(TOK, ROWS)],
        compiler_params=params(),
        cost_estimate=cost(0, 4),
    )(place, cotangent, tokens, tokens, tokens, tokens)
    first_lo = up(first_up)
    first_hi = down(first_down)
    first_x = across(first_far)
    firsts = (first_up, first_hi, first_x, first_lo)

    cot_b = pl.pallas_call(
        pack_second_kernel,
        grid=(1,),
        in_specs=[pl.BlockSpec((TOK, HALF), lambda c: (0, 1)), AFTER, AFTER],
        out_specs=whole(HALF, TOK),
        out_shape=shape(HALF, TOK),
        compiler_params=params(),
        cost_estimate=cost(0, 1),
    )(cotangent, first_lo, first_hi)
    b_lo, b_hi, b_far = up(cot_b), down(cot_b), across(cot_b)
    cots_b = (cot_b, b_hi, b_far, b_lo)

    own_0, own_up, own_across, own_down = pl.pallas_call(
        pack_own_kernel,
        grid_spec=pltpu.PrefetchScalarGridSpec(
            num_scalar_prefetch=1,
            grid=(1,),
            in_specs=columns(0) + [AFTER, AFTER],
            out_specs=[PIECE] * 4,
        ),
        out_shape=[shape(TOK, ROWS)] * 4,
        compiler_params=params(),
        cost_estimate=cost(0, 2),
    )(place, tokens, tokens, tokens, tokens, b_lo, b_hi)
    owns = (own_0, down(own_down), across(own_across), up(own_up))

    partial_a = pl.pallas_call(
        partial_first_kernel,
        grid=(1,),
        in_specs=[MESSAGE] * 4 + [PIECE, INDEX, AFTER, AFTER],
        out_specs=whole(HALF + PICKS, ROWS),
        out_shape=shape(HALF + PICKS, ROWS),
        compiler_params=params(),
        cost_estimate=cost(KV * KV * ROWS, 3),
    )(*firsts, peer_0, index_t, weight_peer, cot_b)
    got_a = swap(partial_a)
    partial_b = pl.pallas_call(
        partial_second_kernel,
        grid=(1,),
        in_specs=[whole(HALF, TOK)] * 4 + [PIECE] + [MESSAGE] * 3,
        out_specs=whole(HALF, ROWS),
        out_shape=shape(HALF, ROWS),
        compiler_params=params(),
        cost_estimate=cost(KV * KV * ROWS, 3),
    )(*cots_b, peer_0, *firsts[1:])
    got_b = swap(partial_b)

    base, base_up, base_across, base_down = pl.pallas_call(
        base_kernel,
        grid_spec=pltpu.PrefetchScalarGridSpec(
            num_scalar_prefetch=1,
            grid=(STEPS,),
            in_specs=[PIECE] * 5
            + [MESSAGE] * 3
            + [by_col(ROWS, GROUP)] * 2
            + [INDEX, whole(HALF + PICKS, ROWS)],
            out_specs=[by_col(TOK + PICKS, GROUP)] * 4,
            scratch_shapes=[pltpu.VMEM((PICKS, KV), BF16)],
        ),
        out_shape=[shape(TOK + PICKS, KV)] * 4,
        compiler_params=params(2 * VMEM_LIMIT),
        cost_estimate=cost(4 * KV * KV * ROWS, 7),
    )(place, *owns, peer_0, *firsts[1:], weight, weight_peer, index_t, got_a)
    base_lo, base_hi, base_far = up(base_up), down(base_down), across(base_across)

    halves = whole(TILES // 2, 8, LANES)
    half_shape = shape(TILES // 2, 8, LANES, dtype=F32)
    moment, picked, keep, send = pl.pallas_call(
        pick_kernel,
        grid_spec=pltpu.PrefetchScalarGridSpec(
            num_scalar_prefetch=1,
            grid=(STEPS,),
            in_specs=[first_half(GROUP, 2 * TOK)] * 4
            + [second_half(GROUP, TOK)] * 4
            + [PIECE] * 4
            + [by_col(ROWS, GROUP)]
            + GOT
            + [INDEX_STEP]
            + BASIS
            + [AFTER],
            out_specs=[by_row(GROUP, ROWS), by_row(PICKS // STEPS, ROWS), halves, halves],
        ),
        out_shape=[shape(KV, ROWS, dtype=F32), shape(PICKS, ROWS, dtype=F32), half_shape, half_shape],
        compiler_params=params(),
        cost_estimate=cost(2 * KV * KV * ROWS, 12),
    )(place, *firsts, *cots_b, *owns, momentum[0], got_a, got_b, index_t, high, low, base)

    def partner(x, bits):
        return lax.ppermute(x, "rep", [(i, i ^ bits) for i in range(REPS)])

    def add(kernel, result, *parts, after=()):
        return pl.pallas_call(
            kernel,
            grid=(1,),
            in_specs=[halves] * len(parts) + [AFTER] * len(after),
            out_specs=halves,
            out_shape=result,
            compiler_params=params(),
            cost_estimate=cost(0, 0.25),
        )(*parts, *after)

    value = add(add_two_kernel, half_shape, keep, partner(send, 1))
    from_hi = partner(value, 2)

    value = add(add_two_kernel, half_shape, value, from_hi)
    value = add(add_two_kernel, half_shape, value, partner(value, 4))
    value = add(add_two_kernel, half_shape, value, partner(value, 8))
    last = partner(value, 16)
    new_momentum, mark = pl.pallas_call(
        residual_kernel,
        grid=(STEPS,),
        in_specs=[by_row(GROUP, ROWS), by_row(PICKS // STEPS, ROWS), INDEX_STEP] + BASIS + [AFTER],
        out_specs=[by_col(ROWS, GROUP), whole(8, LANES)],
        out_shape=[shape(ROWS, KV, dtype=F32), shape(8, LANES, dtype=F32)],
        compiler_params=params(),
        cost_estimate=cost(6 * KV * GROUP * ROWS, 5),
    )(moment, picked, index_t, high, low, value)
    half = add(add_two_kernel, shape(TILES // 2, 8, LANES), value, last, after=(mark,))

    corner = lax.ppermute(half, ("rep", "fsdp"), [(i, i ^ 9) for i in range(REPS * 8)])
    pair_spec = whole(2, TILES, 8, LANES)
    pair = pl.pallas_call(
        pair_kernel,
        grid_spec=pltpu.PrefetchScalarGridSpec(
            num_scalar_prefetch=1,
            grid=(1,),
            in_specs=[halves] * 4 + [AFTER] * 3,
            out_specs=pair_spec,
        ),
        out_shape=shape(2, TILES, 8, LANES),
        compiler_params=params(),
        cost_estimate=cost(0, 0.25),
    )(place, half, partner(half, 1), swap(half), corner, base_lo, base_hi, base_far)
    pair_far, pair_lo, pair_hi = across(pair), up(pair), down(pair)

    def token_block(d):
        return pl.BlockSpec((TOK, 2 * ROWS), lambda c, s: (0, ((s[0] >> 1) + d) & 3))

    mixed, new_weight, base_sum = pl.pallas_call(
        forward_own_kernel,
        grid_spec=pltpu.PrefetchScalarGridSpec(
            num_scalar_prefetch=1,
            grid=(1,),
            in_specs=[token_block(0)] + [whole(TOK + PICKS, KV)] * 4 + [pair_spec, whole(ROWS, KV)] + BASIS,
            out_specs=[whole(KV, TOK), whole(ROWS, KV), whole(TOK, KV)],
            scratch_shapes=[DENSE, PAIRS, VALUES],
        ),
        out_shape=[shape(KV, TOK, dtype=F32), shape(ROWS, KV), shape(TOK, KV, dtype=F32)],
        compiler_params=params(2 * VMEM_LIMIT),
        cost_estimate=cost(3 * KV * KV * ROWS, 4),
    )(place, tokens, base, base_hi, base_far, base_lo, pair, weight, high, low)

    tail = pl.BlockSpec((PICKS, KV), lambda c, *_: (TOK // PICKS, 0))
    mixed = pl.pallas_call(
        forward_near_kernel,
        grid_spec=pltpu.PrefetchScalarGridSpec(
            num_scalar_prefetch=1,
            grid=(1,),
            in_specs=[token_block(1), token_block(3)]
            + [tail] * 2
            + [pair_spec] * 2
            + [whole(KV, TOK)],
            out_specs=whole(KV, TOK),
            scratch_shapes=[DENSE] * 2 + [PAIRS] * 2 + [VALUES] * 2,
        ),
        out_shape=shape(KV, TOK, dtype=F32),
        compiler_params=params(2 * VMEM_LIMIT),
        cost_estimate=cost(4 * KV * KV * ROWS, 5),
    )(place, tokens, tokens, base_hi, base_lo, pair_hi, pair_lo, mixed)

    projected = pl.pallas_call(
        forward_far_kernel,
        grid_spec=pltpu.PrefetchScalarGridSpec(
            num_scalar_prefetch=1,
            grid=(1,),
            in_specs=[token_block(2), whole(TOK, KV), tail, pair_spec, whole(KV, TOK)]
            + BASIS,
            out_specs=whole(TOK, KV),
            scratch_shapes=[DENSE, PAIRS, VALUES, pltpu.VMEM((KV, TOK), F32)],
        ),
        out_shape=shape(TOK, KV),
        compiler_params=params(2 * VMEM_LIMIT),
        cost_estimate=cost(3 * KV * KV * ROWS, 5),
    )(place, tokens, base_sum, base_far, pair_far, mixed, high, low)
    return (projected, new_weight, new_momentum[None])


def solution(mesh):
    in_specs = (
        P(("rep", "fsdp"), None),
        P(("rep", "fsdp"), None),
        P("fsdp", None),
        P("rep", "fsdp", None),
        P("fsdp", None, None),
    )
    out_specs = (P(("rep", "fsdp"), None), P("fsdp", None), P("rep", "fsdp", None))
    return jax.shard_map(body, mesh=mesh, in_specs=in_specs, out_specs=out_specs, check_vma=False)
```

```python
import jax
import jax.numpy as jnp
import numpy as np
from jax import lax
from jax.experimental import pallas as pl
from jax.experimental.pallas import tpu as pltpu
from jax.sharding import PartitionSpec as P

beta_decay = 0.9
step_rate = 0.5
ROWS = 512
KV = 1024
TOK = 256
BLOCK = 64
KEEP = 4
HALF = KV // 2
GROUP = 256
STEPS = KV // GROUP
PICKS = KV // BLOCK * KEEP
LANES = 128
PACK = 16
REPS = 32
TILES = PICKS * ROWS // (8 * LANES)
VMEM_LIMIT = 16 * 1024 * 1024


def dct_group():
    n = np.arange(BLOCK, dtype=np.float64)
    single = np.cos(np.pi * (2.0 * n[None, :] + 1.0) * n[:, None] / (2 * BLOCK))
    single *= np.where(n[:, None] == 0, np.sqrt(1.0 / BLOCK), np.sqrt(2.0 / BLOCK))
    return np.kron(np.eye(GROUP // BLOCK), single).astype(np.float32)


def split_pair(values):
    high = values.astype(jnp.bfloat16)
    return high, (values - high.astype(jnp.float32)).astype(jnp.bfloat16)


def mix(left, right, dims):
    return lax.dot_general(left, right, (dims, ((), ())), preferred_element_type=jnp.float32)


def three_pass(left_pair, right_pair, dims):
    return (
        mix(left_pair[0], right_pair[0], dims)
        + mix(left_pair[0], right_pair[1], dims)
        + mix(left_pair[1], right_pair[0], dims)
    )


def expand_block(index_rows, value_rows, width):
    freq = lax.broadcasted_iota(jnp.int32, (BLOCK, width), 0)
    dense = jnp.zeros((BLOCK, width), jnp.float32)
    for j in range(KEEP):
        dense = jnp.where(index_rows[j] == freq, value_rows[j], dense)
    return dense


def spread_row(row, dtype):
    return jnp.broadcast_to(row, (PACK, LANES)).astype(dtype)


def expand_tile(indices, values, dense, first, cols):
    freq = lax.broadcasted_iota(jnp.int32, (PACK, LANES), 0)
    for half in range(2):
        at = [spread_row(indices(half * KEEP + j), jnp.int16) for j in range(KEEP)]
        have = [spread_row(values(half * KEEP + j), jnp.bfloat16) for j in range(KEEP)]
        for part in range(BLOCK // PACK):
            here = (freq + part * PACK).astype(jnp.int16)
            tile = jnp.zeros((PACK, LANES), jnp.bfloat16)
            for j in range(KEEP):
                tile = jnp.where(at[j] == here, have[j], tile)
            start = first + half * BLOCK + part * PACK
            dense[start : start + PACK, cols] = tile


def four_products(cots, toks):
    total = jnp.dot(cots[0], toks[0], preferred_element_type=jnp.float32)
    for c, t in zip(cots[1:], toks[1:]):
        total += jnp.dot(c, t, preferred_element_type=jnp.float32)
    return total


def cot_of(message):
    return message[:, :TOK]


def tok_of(message):
    return jnp.concatenate([message[:TOK, TOK:], message[TOK:, TOK:]], axis=1)


def flat_index(idx):
    rows = [idx[b].astype(jnp.float32) for b in range(KV // BLOCK)]
    return jnp.concatenate(rows, axis=0).astype(jnp.bfloat16)


def pack_first_kernel(where, cot, t0, t1, t2, t3, to_up, to_far, to_down, mine):
    turned = cot[...].T
    for out, t in ((to_up, t1), (to_far, t2), (to_down, t3)):
        out[:, :TOK] = turned
        out[:TOK, TOK:] = t[:, :TOK]
        out[TOK:, TOK:] = t[:, TOK:]
    mine[...] = t0[...]


def pack_second_kernel(cot, late_lo, late_hi, out):
    out[...] = cot[...].T


def pack_own_kernel(where, t0, t1, t2, t3, late_lo, late_hi, mine, to_up, to_far, to_down):
    for out, t in ((mine, t0), (to_up, t1), (to_far, t2), (to_down, t3)):
        out[...] = t[...]


def partial_first_kernel(sent, hi, far, lo, t0, idx, early, turned, out):
    cots = (cot_of(sent), cot_of(hi), cot_of(far), cot_of(lo))
    toks = (t0[...], tok_of(hi), tok_of(far), tok_of(lo))
    out[:HALF, :] = four_products(cots, toks).astype(out.dtype)
    out[HALF:, :] = flat_index(idx)


def partial_second_kernel(c0, c1, c2, c3, t0, hi, far, lo, out):
    cots = (c0[...], c1[...], c2[...], c3[...])
    toks = (t0[...], tok_of(hi), tok_of(far), tok_of(lo))
    out[...] = four_products(cots, toks).astype(out.dtype)


def own_kernel(a0, a1, a2, a3, b0, b1, b2, b3, t0, t1, t2, t3, mom, out):
    step = pl.program_id(0)
    toks = (t0[...], t1[...], t2[...], t3[...])

    @pl.when(step < STEPS // 2)
    def _():
        cots = (cot_of(a0), cot_of(a1), cot_of(a2), cot_of(a3))
        out[...] = four_products(cots, toks) + beta_decay * mom[...].T

    @pl.when(step >= STEPS // 2)
    def _():
        cots = (b0[...], b1[...], b2[...], b3[...])
        out[...] = four_products(cots, toks) + beta_decay * mom[...].T


def pick_rows(moment, idx, ch, cl):
    spectrum = three_pass((ch[...], cl[...]), split_pair(moment), ((1,), (0,)))
    freq = lax.broadcasted_iota(jnp.int32, (BLOCK, ROWS), 0)
    rows = []
    for b in range(GROUP // BLOCK):
        part = spectrum[b * BLOCK : (b + 1) * BLOCK, :]
        for j in range(KEEP):
            here = idx[b, j : j + 1, :] == freq
            rows.append(jnp.sum(jnp.where(here, part, 0.0), axis=0, keepdims=True))
    return rows


def pick_kernel(where, pre, got_a, got_b, idx, ch, cl, late, moment, picked, keep, send):
    step = pl.program_id(0)
    first = step < STEPS // 2
    got = jnp.where(first, got_a[...], got_b[...]).astype(jnp.float32)
    total = pre[...] + got
    moment[...] = total
    values = jnp.concatenate(pick_rows(total, idx, ch, cl), axis=0)
    picked[...] = values

    def put(out):
        for t in range(GROUP // BLOCK * KEEP // 8):
            for q in range(ROWS // LANES):
                tile = values[t * 8 : (t + 1) * 8, q * LANES : (q + 1) * LANES]
                out[(step & 1) * (TILES // STEPS) + t * (ROWS // LANES) + q] = tile

    here = (step >> 1) == (where[1] & 1)
    pl.when(here)(lambda: put(keep))
    pl.when(jnp.logical_not(here))(lambda: put(send))


def add_two_kernel(a, b, *rest):
    out = rest[-1]
    out[...] = (a[...] + b[...]).astype(out.dtype)


def pair_kernel(where, half, core, across, corner, late_0, late_1, late_2, out):
    side, mine = where[0] & 1, (where[1] & 1) * (TILES // 2)
    other = TILES // 2 - mine
    out[side, pl.ds(mine, TILES // 2)] = half[...]
    out[side, pl.ds(other, TILES // 2)] = core[...]
    out[1 - side, pl.ds(mine, TILES // 2)] = across[...]
    out[1 - side, pl.ds(other, TILES // 2)] = corner[...]


def residual_kernel(moment, picked, idx, ch, cl, late, out, mark):
    parts = []
    for b in range(GROUP // BLOCK):
        at = [idx[b, j : j + 1, :] for j in range(KEEP)]
        have = [picked[b * KEEP + j : b * KEEP + j + 1, :] for j in range(KEEP)]
        parts.append(expand_block(at, have, ROWS))
    kept = jnp.concatenate(parts, axis=0)
    back = three_pass((ch[...], cl[...]), split_pair(kept), ((0,), (0,)))
    out[...] = (moment[...] - back).T
    mark[...] = back[:8, :LANES]


def base_kernel(where, o0, o1, o2, o3, p0, p1, p2, p3, w_own, w_peer, idx, got_a, *outs):
    mine, theirs = flat_index(idx), got_a[HALF:, :]
    first = (where[0] & 1) == 0
    left, right = jnp.where(first, mine, theirs), jnp.where(first, theirs, mine)
    peers = (p0[...], tok_of(p1), tok_of(p2), tok_of(p3))
    for own, peer, out in zip((o0, o1, o2, o3), peers, outs):
        total = jnp.dot(own[...], w_own[...], preferred_element_type=jnp.float32)
        total += jnp.dot(peer, w_peer[...], preferred_element_type=jnp.float32)
        out[:TOK, :] = total.astype(out.dtype)
        out[TOK:, :ROWS] = left
        out[TOK:, ROWS:] = right


def expand_group(g, pairs, tot, dense):
    for t in range(2 * g, 2 * g + 2):
        for f in range(2):
            for q in range(ROWS // LANES):
                cols = slice(f * ROWS + q * LANES, f * ROWS + (q + 1) * LANES)
                tile = t * (ROWS // LANES) + q
                expand_tile(
                    lambda s, t=t, cols=cols: pairs[t * 8 + s : t * 8 + s + 1, cols],
                    lambda s, f=f, tile=tile: tot[f, tile, s : s + 1, :],
                    dense,
                    t * 2 * BLOCK,
                    cols,
                )


def forward_own_kernel(where, tok, own, tot, weight, ch, cl, mixed, out_weight, dense, pairs, values):
    pairs[...] = own[TOK:, :].astype(jnp.int32)
    values[...] = tot[...].astype(jnp.float32)
    cols = pl.ds(pl.multiple_of((where[0] & 1) * ROWS, ROWS), ROWS)
    for g in range(STEPS):
        expand_group(g, pairs, values, dense)
        span = slice(g * GROUP, (g + 1) * GROUP)
        turned = dense[span, cols].T
        delta = mix(turned, ch[...], ((1,), (0,))) + mix(turned, cl[...], ((1,), (0,)))
        new = weight[:, span].astype(jnp.float32) - (step_rate / REPS) * delta
        out_weight[:, span] = new.astype(out_weight.dtype)
    mixed[...] = mix(dense[...], tok[...], ((1,), (1,)))


def expand_all(near, tot, dense, pairs, values):
    pairs[...] = near[TOK:, :].astype(jnp.int32)
    values[...] = tot[...].astype(jnp.float32)
    for g in range(STEPS):
        expand_group(g, pairs, values, dense)


def forward_near_kernel(where, tok_1, tok_3, hi, lo, tot_1, tot_3, before, out, *scratch):
    expand_all(hi, tot_1, scratch[0], scratch[2], scratch[4])
    total = before[...] + mix(scratch[0][...], tok_1[...], ((1,), (1,)))
    expand_all(lo, tot_3, scratch[1], scratch[3], scratch[5])
    out[...] = total + mix(scratch[1][...], tok_3[...], ((1,), (1,)))


def forward_far_kernel(where, tok, own, hi, far, lo, tot, before, ch, cl, out, dense, pairs, values, total):
    expand_all(far, tot, dense, pairs, values)
    total[...] = before[...] + mix(dense[...], tok[...], ((1,), (1,)))
    for g in range(STEPS):
        span = slice(g * GROUP, (g + 1) * GROUP)
        delta = three_pass(split_pair(total[span, :].T), (ch[...], cl[...]), ((1,), (0,)))
        base = own[:TOK, span].astype(jnp.float32) + hi[:TOK, span].astype(jnp.float32)
        base += far[:TOK, span].astype(jnp.float32) + lo[:TOK, span].astype(jnp.float32)
        out[:, span] = (base - (step_rate / REPS) * delta).astype(out.dtype)


def params(limit=VMEM_LIMIT):
    return pltpu.CompilerParams(vmem_limit_bytes=limit)


def cost(flops, mib):
    return pl.CostEstimate(flops=int(flops), bytes_accessed=int(mib * (1 << 20)), transcendentals=0)


def whole(*shape):
    return pl.BlockSpec(shape, lambda c, *_: (0,) * len(shape))


def by_row(rows, width):
    return pl.BlockSpec((rows, width), lambda c, *_: (c, 0))


def by_col(rows, width):
    return pl.BlockSpec((rows, width), lambda c, *_: (0, c))


def first_half(rows, width):
    return pl.BlockSpec((rows, width), lambda c, *_: (jnp.minimum(c, STEPS // 2 - 1), 0))


def second_half(rows, width):
    return pl.BlockSpec((rows, width), lambda c, *_: (jnp.maximum(c - STEPS // 2, 0), 0))


AFTER = pl.BlockSpec(memory_space=pl.ANY)
BASIS = [whole(GROUP, GROUP)] * 2
GOT = [first_half(GROUP, ROWS), second_half(GROUP, ROWS)]
BF16, F32 = jnp.bfloat16, jnp.float32
INDEX = pl.BlockSpec((KV // BLOCK, KEEP, ROWS), lambda c, *_: (0, 0, 0))
INDEX_STEP = pl.BlockSpec((GROUP // BLOCK, KEEP, ROWS), lambda c, *_: (c, 0, 0))
MESSAGE = whole(HALF, 2 * TOK)
PIECE = whole(TOK, ROWS)
DENSE = pltpu.VMEM((KV, 2 * ROWS), BF16)
PAIRS = pltpu.VMEM((PICKS, 2 * ROWS), jnp.int32)
VALUES = pltpu.VMEM((2, TILES, 8, LANES), F32)


def shape(*dims, dtype=BF16):
    return jax.ShapeDtypeStruct(dims, dtype)


def body(tokens, cotangent, weight, momentum, kept_index):
    basis = dct_group()
    high = jnp.asarray(basis).astype(BF16)
    low = (jnp.asarray(basis) - high.astype(F32)).astype(BF16)
    place = jnp.stack([lax.axis_index("fsdp"), lax.axis_index("rep")]).astype(jnp.int32)
    index_t = jnp.transpose(kept_index, (1, 2, 0))

    def up(x):
        return lax.ppermute(x, "fsdp", [(i, (i + 2) % 8) for i in range(8)])

    def down(x):
        return lax.ppermute(x, "fsdp", [(i, (i + 6) % 8) for i in range(8)])

    def across(x):
        return lax.ppermute(x, "fsdp", [(i, (i + 4) % 8) for i in range(8)])

    def swap(x):
        return lax.ppermute(x, "fsdp", [(i, i ^ 1) for i in range(8)])

    def columns(flip):
        return [pl.BlockSpec((TOK, ROWS), lambda c, s, d=d: (0, ((s[0] ^ flip) + 2 * d) & 7)) for d in range(4)]

    weight_peer = swap(weight)

    first_up, first_far, first_down, peer_0 = pl.pallas_call(
        pack_first_kernel,
        grid_spec=pltpu.PrefetchScalarGridSpec(
            num_scalar_prefetch=1,
            grid=(1,),
            in_specs=[whole(TOK, HALF)] + columns(1),
            out_specs=[MESSAGE] * 3 + [PIECE],
        ),
        out_shape=[shape(HALF, 2 * TOK)] * 3 + [shape(TOK, ROWS)],
        compiler_params=params(),
        cost_estimate=cost(0, 4),
    )(place, cotangent, tokens, tokens, tokens, tokens)
    first_lo = up(first_up)
    first_hi = down(first_down)
    first_x = across(first_far)
    firsts = (first_up, first_hi, first_x, first_lo)

    cot_b = pl.pallas_call(
        pack_second_kernel,
        grid=(1,),
        in_specs=[pl.BlockSpec((TOK, HALF), lambda c: (0, 1)), AFTER, AFTER],
        out_specs=whole(HALF, TOK),
        out_shape=shape(HALF, TOK),
        compiler_params=params(),
        cost_estimate=cost(0, 1),
    )(cotangent, first_lo, first_hi)
    b_lo, b_hi, b_far = up(cot_b), down(cot_b), across(cot_b)
    cots_b = (cot_b, b_hi, b_far, b_lo)

    own_0, own_up, own_across, own_down = pl.pallas_call(
        pack_own_kernel,
        grid_spec=pltpu.PrefetchScalarGridSpec(
            num_scalar_prefetch=1,
            grid=(1,),
            in_specs=columns(0) + [AFTER, AFTER],
            out_specs=[PIECE] * 4,
        ),
        out_shape=[shape(TOK, ROWS)] * 4,
        compiler_params=params(),
        cost_estimate=cost(0, 2),
    )(place, tokens, tokens, tokens, tokens, b_lo, b_hi)
    owns = (own_0, down(own_down), across(own_across), up(own_up))

    partial_a = pl.pallas_call(
        partial_first_kernel,
        grid=(1,),
        in_specs=[MESSAGE] * 4 + [PIECE, INDEX, AFTER, AFTER],
        out_specs=whole(HALF + PICKS, ROWS),
        out_shape=shape(HALF + PICKS, ROWS),
        compiler_params=params(),
        cost_estimate=cost(KV * KV * ROWS, 3),
    )(*firsts, peer_0, index_t, weight_peer, cot_b)
    got_a = swap(partial_a)
    partial_b = pl.pallas_call(
        partial_second_kernel,
        grid=(1,),
        in_specs=[whole(HALF, TOK)] * 4 + [PIECE] + [MESSAGE] * 3,
        out_specs=whole(HALF, ROWS),
        out_shape=shape(HALF, ROWS),
        compiler_params=params(),
        cost_estimate=cost(KV * KV * ROWS, 3),
    )(*cots_b, peer_0, *firsts[1:])
    got_b = swap(partial_b)

    pre = pl.pallas_call(
        own_kernel,
        grid=(STEPS,),
        in_specs=[first_half(GROUP, 2 * TOK)] * 4
        + [second_half(GROUP, TOK)] * 4
        + [PIECE] * 4
        + [by_col(ROWS, GROUP)],
        out_specs=by_row(GROUP, ROWS),
        out_shape=shape(KV, ROWS, dtype=F32),
        compiler_params=params(),
        cost_estimate=cost(2 * KV * KV * ROWS, 7),
    )(*firsts, *cots_b, *owns, momentum[0])

    base, base_up, base_across, base_down = pl.pallas_call(
        base_kernel,
        grid_spec=pltpu.PrefetchScalarGridSpec(
            num_scalar_prefetch=1,
            grid=(1,),
            in_specs=[PIECE] * 5
            + [MESSAGE] * 3
            + [whole(ROWS, KV)] * 2
            + [INDEX, whole(HALF + PICKS, ROWS)],
            out_specs=[whole(TOK + PICKS, KV)] * 4,
        ),
        out_shape=[shape(TOK + PICKS, KV)] * 4,
        compiler_params=params(2 * VMEM_LIMIT),
        cost_estimate=cost(4 * KV * KV * ROWS, 7),
    )(place, *owns, peer_0, *firsts[1:], weight, weight_peer, index_t, got_a)
    base_lo, base_hi, base_far = up(base_up), down(base_down), across(base_across)

    halves = whole(TILES // 2, 8, LANES)
    half_shape = shape(TILES // 2, 8, LANES, dtype=F32)
    moment, picked, keep, send = pl.pallas_call(
        pick_kernel,
        grid_spec=pltpu.PrefetchScalarGridSpec(
            num_scalar_prefetch=1,
            grid=(STEPS,),
            in_specs=[by_row(GROUP, ROWS)] + GOT + [INDEX_STEP] + BASIS + [AFTER],
            out_specs=[by_row(GROUP, ROWS), by_row(PICKS // STEPS, ROWS), halves, halves],
        ),
        out_shape=[shape(KV, ROWS, dtype=F32), shape(PICKS, ROWS, dtype=F32), half_shape, half_shape],
        compiler_params=params(),
        cost_estimate=cost(6 * KV * GROUP * ROWS, 6),
    )(place, pre, got_a, got_b, index_t, high, low, base)

    def partner(x, bits):
        return lax.ppermute(x, "rep", [(i, i ^ bits) for i in range(REPS)])

    def add(kernel, result, *parts, after=()):
        return pl.pallas_call(
            kernel,
            grid=(1,),
            in_specs=[halves] * len(parts) + [AFTER] * len(after),
            out_specs=halves,
            out_shape=result,
            compiler_params=params(),
            cost_estimate=cost(0, 0.25),
        )(*parts, *after)

    value = add(add_two_kernel, half_shape, keep, partner(send, 1))
    from_hi = partner(value, 2)

    value = add(add_two_kernel, half_shape, value, from_hi)
    value = add(add_two_kernel, half_shape, value, partner(value, 4))
    value = add(add_two_kernel, half_shape, value, partner(value, 8))
    last = partner(value, 16)
    new_momentum, mark = pl.pallas_call(
        residual_kernel,
        grid=(STEPS,),
        in_specs=[by_row(GROUP, ROWS), by_row(PICKS // STEPS, ROWS), INDEX_STEP] + BASIS + [AFTER],
        out_specs=[by_col(ROWS, GROUP), whole(8, LANES)],
        out_shape=[shape(ROWS, KV, dtype=F32), shape(8, LANES, dtype=F32)],
        compiler_params=params(),
        cost_estimate=cost(6 * KV * GROUP * ROWS, 5),
    )(moment, picked, index_t, high, low, value)
    half = add(add_two_kernel, shape(TILES // 2, 8, LANES), value, last, after=(mark,))

    corner = lax.ppermute(half, ("rep", "fsdp"), [(i, i ^ 9) for i in range(REPS * 8)])
    pair_spec = whole(2, TILES, 8, LANES)
    pair = pl.pallas_call(
        pair_kernel,
        grid_spec=pltpu.PrefetchScalarGridSpec(
            num_scalar_prefetch=1,
            grid=(1,),
            in_specs=[halves] * 4 + [AFTER] * 3,
            out_specs=pair_spec,
        ),
        out_shape=shape(2, TILES, 8, LANES),
        compiler_params=params(),
        cost_estimate=cost(0, 0.25),
    )(place, half, partner(half, 1), swap(half), corner, base_lo, base_hi, base_far)
    pair_far, pair_lo, pair_hi = across(pair), up(pair), down(pair)

    def token_block(d):
        return pl.BlockSpec((TOK, 2 * ROWS), lambda c, s: (0, ((s[0] >> 1) + d) & 3))

    mixed, new_weight = pl.pallas_call(
        forward_own_kernel,
        grid_spec=pltpu.PrefetchScalarGridSpec(
            num_scalar_prefetch=1,
            grid=(1,),
            in_specs=[token_block(0), whole(TOK + PICKS, KV), pair_spec, whole(ROWS, KV)] + BASIS,
            out_specs=[whole(KV, TOK), whole(ROWS, KV)],
            scratch_shapes=[DENSE, PAIRS, VALUES],
        ),
        out_shape=[shape(KV, TOK, dtype=F32), shape(ROWS, KV)],
        compiler_params=params(),
        cost_estimate=cost(3 * KV * KV * ROWS, 4),
    )(place, tokens, base, pair, weight, high, low)

    mixed = pl.pallas_call(
        forward_near_kernel,
        grid_spec=pltpu.PrefetchScalarGridSpec(
            num_scalar_prefetch=1,
            grid=(1,),
            in_specs=[token_block(1), token_block(3)]
            + [whole(TOK + PICKS, KV)] * 2
            + [pair_spec] * 2
            + [whole(KV, TOK)],
            out_specs=whole(KV, TOK),
            scratch_shapes=[DENSE] * 2 + [PAIRS] * 2 + [VALUES] * 2,
        ),
        out_shape=shape(KV, TOK, dtype=F32),
        compiler_params=params(2 * VMEM_LIMIT),
        cost_estimate=cost(4 * KV * KV * ROWS, 5),
    )(place, tokens, tokens, base_hi, base_lo, pair_hi, pair_lo, mixed)

    projected = pl.pallas_call(
        forward_far_kernel,
        grid_spec=pltpu.PrefetchScalarGridSpec(
            num_scalar_prefetch=1,
            grid=(1,),
            in_specs=[token_block(2)]
            + [whole(TOK + PICKS, KV)] * 4
            + [pair_spec, whole(KV, TOK)]
            + BASIS,
            out_specs=whole(TOK, KV),
            scratch_shapes=[DENSE, PAIRS, VALUES, pltpu.VMEM((KV, TOK), F32)],
        ),
        out_shape=shape(TOK, KV),
        compiler_params=params(2 * VMEM_LIMIT),
        cost_estimate=cost(3 * KV * KV * ROWS, 5),
    )(place, tokens, base, base_hi, base_far, base_lo, pair_far, mixed, high, low)
    return (projected, new_weight, new_momentum[None])


def solution(mesh):
    in_specs = (
        P(("rep", "fsdp"), None),
        P(("rep", "fsdp"), None),
        P("fsdp", None),
        P("rep", "fsdp", None),
        P("fsdp", None, None),
    )
    out_specs = (P(("rep", "fsdp"), None), P("fsdp", None), P("rep", "fsdp", None))
    return jax.shard_map(body, mesh=mesh, in_specs=in_specs, out_specs=out_specs, check_vma=False)
```

```python
import jax
import jax.numpy as jnp
import numpy as np
from jax import lax
from jax.experimental import pallas as pl
from jax.experimental.pallas import tpu as pltpu
from jax.sharding import PartitionSpec as P

beta_decay = 0.9
step_rate = 0.5
ROWS = 512
KV = 1024
TOK = 256
BLOCK = 64
KEEP = 4
HALF = KV // 2
GROUP = 256
STEPS = KV // GROUP
PICKS = KV // BLOCK * KEEP
LANES = 128
PACK = 16
REPS = 32
TILES = PICKS * ROWS // (8 * LANES)
VMEM_LIMIT = 16 * 1024 * 1024


def dct_group():
    n = np.arange(BLOCK, dtype=np.float64)
    single = np.cos(np.pi * (2.0 * n[None, :] + 1.0) * n[:, None] / (2 * BLOCK))
    single *= np.where(n[:, None] == 0, np.sqrt(1.0 / BLOCK), np.sqrt(2.0 / BLOCK))
    return np.kron(np.eye(GROUP // BLOCK), single).astype(np.float32)


def split_pair(values):
    high = values.astype(jnp.bfloat16)
    return high, (values - high.astype(jnp.float32)).astype(jnp.bfloat16)


def mix(left, right, dims):
    return lax.dot_general(left, right, (dims, ((), ())), preferred_element_type=jnp.float32)


def three_pass(left_pair, right_pair, dims):
    return (
        mix(left_pair[0], right_pair[0], dims)
        + mix(left_pair[0], right_pair[1], dims)
        + mix(left_pair[1], right_pair[0], dims)
    )


def expand_block(index_rows, value_rows, width):
    freq = lax.broadcasted_iota(jnp.int32, (BLOCK, width), 0)
    dense = jnp.zeros((BLOCK, width), jnp.float32)
    for j in range(KEEP):
        dense = jnp.where(index_rows[j] == freq, value_rows[j], dense)
    return dense


def spread_row(row):
    return jnp.broadcast_to(row, (PACK, LANES)).astype(jnp.bfloat16)


def expand_tile(indices, values, dense, first, cols):
    freq = lax.broadcasted_iota(jnp.int32, (PACK, LANES), 0).astype(jnp.float32)
    for half in range(2):
        at = [spread_row(indices(half * KEEP + j)) for j in range(KEEP)]
        have = [spread_row(values(half * KEEP + j)) for j in range(KEEP)]
        for part in range(BLOCK // PACK):
            here = (freq + part * PACK).astype(jnp.bfloat16)
            tile = jnp.zeros((PACK, LANES), jnp.bfloat16)
            for j in range(KEEP):
                tile = jnp.where(at[j] == here, have[j], tile)
            start = first + half * BLOCK + part * PACK
            dense[start : start + PACK, cols] = tile


def four_products(cots, toks):
    total = jnp.dot(cots[0], toks[0], preferred_element_type=jnp.float32)
    for c, t in zip(cots[1:], toks[1:]):
        total += jnp.dot(c, t, preferred_element_type=jnp.float32)
    return total


def cot_of(message):
    return message[:, :TOK]


def tok_of(message):
    return jnp.concatenate([message[:TOK, TOK:], message[TOK:, TOK:]], axis=1)


def flat_index(idx):
    rows = [idx[b].astype(jnp.float32) for b in range(KV // BLOCK)]
    return jnp.concatenate(rows, axis=0).astype(jnp.bfloat16)


def pack_first_kernel(where, cot, t0, t1, t2, t3, to_up, to_far, to_down, mine):
    turned = cot[...].T
    for out, t in ((to_up, t1), (to_far, t2), (to_down, t3)):
        out[:, :TOK] = turned
        out[:TOK, TOK:] = t[:, :TOK]
        out[TOK:, TOK:] = t[:, TOK:]
    mine[...] = t0[...]


def pack_second_kernel(cot, late_lo, late_hi, out):
    out[...] = cot[...].T


def pack_own_kernel(where, t0, t1, t2, t3, late_lo, late_hi, mine, to_up, to_far, to_down):
    for out, t in ((mine, t0), (to_up, t1), (to_far, t2), (to_down, t3)):
        out[...] = t[...]


def partial_first_kernel(sent, hi, far, lo, t0, idx, early, turned, out):
    cots = (cot_of(sent), cot_of(hi), cot_of(far), cot_of(lo))
    toks = (t0[...], tok_of(hi), tok_of(far), tok_of(lo))
    out[:HALF, :] = four_products(cots, toks).astype(out.dtype)
    out[HALF:, :] = flat_index(idx)


def partial_second_kernel(c0, c1, c2, c3, t0, hi, far, lo, out):
    cots = (c0[...], c1[...], c2[...], c3[...])
    toks = (t0[...], tok_of(hi), tok_of(far), tok_of(lo))
    out[...] = four_products(cots, toks).astype(out.dtype)


def own_kernel(a0, a1, a2, a3, b0, b1, b2, b3, t0, t1, t2, t3, mom, out):
    step = pl.program_id(0)
    toks = (t0[...], t1[...], t2[...], t3[...])

    @pl.when(step < STEPS // 2)
    def _():
        cots = (cot_of(a0), cot_of(a1), cot_of(a2), cot_of(a3))
        out[...] = four_products(cots, toks) + beta_decay * mom[...].T

    @pl.when(step >= STEPS // 2)
    def _():
        cots = (b0[...], b1[...], b2[...], b3[...])
        out[...] = four_products(cots, toks) + beta_decay * mom[...].T


def pick_rows(moment, idx, ch, cl):
    spectrum = three_pass((ch[...], cl[...]), split_pair(moment), ((1,), (0,)))
    freq = lax.broadcasted_iota(jnp.int32, (BLOCK, ROWS), 0)
    rows = []
    for b in range(GROUP // BLOCK):
        part = spectrum[b * BLOCK : (b + 1) * BLOCK, :]
        for j in range(KEEP):
            here = idx[b, j : j + 1, :] == freq
            rows.append(jnp.sum(jnp.where(here, part, 0.0), axis=0, keepdims=True))
    return rows


def pick_kernel(where, pre, got_a, got_b, idx, ch, cl, late, moment, picked, keep, send):
    step = pl.program_id(0)
    first = step < STEPS // 2
    got = jnp.where(first, got_a[...], got_b[...]).astype(jnp.float32)
    total = pre[...] + got
    moment[...] = total
    values = jnp.concatenate(pick_rows(total, idx, ch, cl), axis=0)
    picked[...] = values

    def put(out):
        for t in range(GROUP // BLOCK * KEEP // 8):
            for q in range(ROWS // LANES):
                tile = values[t * 8 : (t + 1) * 8, q * LANES : (q + 1) * LANES]
                out[(step & 1) * (TILES // STEPS) + t * (ROWS // LANES) + q] = tile

    here = (step >> 1) == (where[1] & 1)
    pl.when(here)(lambda: put(keep))
    pl.when(jnp.logical_not(here))(lambda: put(send))


def add_two_kernel(a, b, *rest):
    out = rest[-1]
    out[...] = (a[...].astype(jnp.float32) + b[...].astype(jnp.float32)).astype(out.dtype)


def pair_kernel(where, half, core, across, corner, late_0, late_1, late_2, out):
    side, mine = where[0] & 1, (where[1] & 1) * (TILES // 2)
    other = TILES // 2 - mine
    out[side, pl.ds(mine, TILES // 2)] = half[...]
    out[side, pl.ds(other, TILES // 2)] = core[...]
    out[1 - side, pl.ds(mine, TILES // 2)] = across[...]
    out[1 - side, pl.ds(other, TILES // 2)] = corner[...]


def residual_kernel(moment, picked, idx, ch, cl, late, out, mark):
    parts = []
    for b in range(GROUP // BLOCK):
        at = [idx[b, j : j + 1, :] for j in range(KEEP)]
        have = [picked[b * KEEP + j : b * KEEP + j + 1, :] for j in range(KEEP)]
        parts.append(expand_block(at, have, ROWS))
    kept = jnp.concatenate(parts, axis=0)
    back = three_pass((ch[...], cl[...]), split_pair(kept), ((0,), (0,)))
    out[...] = (moment[...] - back).T
    mark[...] = back[:8, :LANES]


def base_kernel(where, o0, o1, o2, o3, p0, p1, p2, p3, w_own, w_peer, idx, got_a, *outs):
    mine, theirs = flat_index(idx), got_a[HALF:, :]
    first = (where[0] & 1) == 0
    left, right = jnp.where(first, mine, theirs), jnp.where(first, theirs, mine)
    peers = (p0[...], tok_of(p1), tok_of(p2), tok_of(p3))
    for own, peer, out in zip((o0, o1, o2, o3), peers, outs):
        total = jnp.dot(own[...], w_own[...], preferred_element_type=jnp.float32)
        total += jnp.dot(peer, w_peer[...], preferred_element_type=jnp.float32)
        out[:TOK, :] = total.astype(out.dtype)
        out[TOK:, :ROWS] = left
        out[TOK:, ROWS:] = right


def expand_group(g, pairs, tot, dense):
    for t in range(2 * g, 2 * g + 2):
        for f in range(2):
            for q in range(ROWS // LANES):
                cols = slice(f * ROWS + q * LANES, f * ROWS + (q + 1) * LANES)
                tile = t * (ROWS // LANES) + q
                expand_tile(
                    lambda s, t=t, cols=cols: pairs[t * 8 + s : t * 8 + s + 1, cols],
                    lambda s, f=f, tile=tile: tot[f, tile, s : s + 1, :],
                    dense,
                    t * 2 * BLOCK,
                    cols,
                )


def forward_own_kernel(where, tok, own, tot, weight, ch, cl, mixed, out_weight, dense, pairs, values):
    pairs[...] = own[TOK:, :].astype(jnp.float32)
    values[...] = tot[...].astype(jnp.float32)
    cols = pl.ds(pl.multiple_of((where[0] & 1) * ROWS, ROWS), ROWS)
    for g in range(STEPS):
        expand_group(g, pairs, values, dense)
        span = slice(g * GROUP, (g + 1) * GROUP)
        turned = dense[span, cols].T
        delta = mix(turned, ch[...], ((1,), (0,))) + mix(turned, cl[...], ((1,), (0,)))
        new = weight[:, span].astype(jnp.float32) - (step_rate / REPS) * delta
        out_weight[:, span] = new.astype(out_weight.dtype)
    mixed[...] = mix(dense[...], tok[...], ((1,), (1,)))


def expand_all(near, tot, dense, pairs, values):
    pairs[...] = near[TOK:, :].astype(jnp.float32)
    values[...] = tot[...].astype(jnp.float32)
    for g in range(STEPS):
        expand_group(g, pairs, values, dense)


def forward_near_kernel(where, tok_1, tok_3, hi, lo, tot_1, tot_3, before, out, *scratch):
    expand_all(hi, tot_1, scratch[0], scratch[2], scratch[4])
    total = before[...] + mix(scratch[0][...], tok_1[...], ((1,), (1,)))
    expand_all(lo, tot_3, scratch[1], scratch[3], scratch[5])
    out[...] = total + mix(scratch[1][...], tok_3[...], ((1,), (1,)))


def forward_far_kernel(where, tok, own, hi, far, lo, tot, before, ch, cl, out, dense, pairs, values, total):
    expand_all(far, tot, dense, pairs, values)
    total[...] = before[...] + mix(dense[...], tok[...], ((1,), (1,)))
    for g in range(STEPS):
        span = slice(g * GROUP, (g + 1) * GROUP)
        delta = three_pass(split_pair(total[span, :].T), (ch[...], cl[...]), ((1,), (0,)))
        base = own[:TOK, span].astype(jnp.float32) + hi[:TOK, span].astype(jnp.float32)
        base += far[:TOK, span].astype(jnp.float32) + lo[:TOK, span].astype(jnp.float32)
        out[:, span] = (base - (step_rate / REPS) * delta).astype(out.dtype)


def params(limit=VMEM_LIMIT):
    return pltpu.CompilerParams(vmem_limit_bytes=limit)


def cost(flops, mib):
    return pl.CostEstimate(flops=int(flops), bytes_accessed=int(mib * (1 << 20)), transcendentals=0)


def whole(*shape):
    return pl.BlockSpec(shape, lambda c, *_: (0,) * len(shape))


def by_row(rows, width):
    return pl.BlockSpec((rows, width), lambda c, *_: (c, 0))


def by_col(rows, width):
    return pl.BlockSpec((rows, width), lambda c, *_: (0, c))


def first_half(rows, width):
    return pl.BlockSpec((rows, width), lambda c, *_: (jnp.minimum(c, STEPS // 2 - 1), 0))


def second_half(rows, width):
    return pl.BlockSpec((rows, width), lambda c, *_: (jnp.maximum(c - STEPS // 2, 0), 0))


AFTER = pl.BlockSpec(memory_space=pl.ANY)
BASIS = [whole(GROUP, GROUP)] * 2
GOT = [first_half(GROUP, ROWS), second_half(GROUP, ROWS)]
BF16, F32 = jnp.bfloat16, jnp.float32
INDEX = pl.BlockSpec((KV // BLOCK, KEEP, ROWS), lambda c, *_: (0, 0, 0))
INDEX_STEP = pl.BlockSpec((GROUP // BLOCK, KEEP, ROWS), lambda c, *_: (c, 0, 0))
MESSAGE = whole(HALF, 2 * TOK)
PIECE = whole(TOK, ROWS)
DENSE = pltpu.VMEM((KV, 2 * ROWS), BF16)
PAIRS = pltpu.VMEM((PICKS, 2 * ROWS), F32)
VALUES = pltpu.VMEM((2, TILES, 8, LANES), F32)


def shape(*dims, dtype=BF16):
    return jax.ShapeDtypeStruct(dims, dtype)


def body(tokens, cotangent, weight, momentum, kept_index):
    basis = dct_group()
    high = jnp.asarray(basis).astype(BF16)
    low = (jnp.asarray(basis) - high.astype(F32)).astype(BF16)
    place = jnp.stack([lax.axis_index("fsdp"), lax.axis_index("rep")]).astype(jnp.int32)
    index_t = jnp.transpose(kept_index, (1, 2, 0))

    def up(x):
        return lax.ppermute(x, "fsdp", [(i, (i + 2) % 8) for i in range(8)])

    def down(x):
        return lax.ppermute(x, "fsdp", [(i, (i + 6) % 8) for i in range(8)])

    def across(x):
        return lax.ppermute(x, "fsdp", [(i, (i + 4) % 8) for i in range(8)])

    def swap(x):
        return lax.ppermute(x, "fsdp", [(i, i ^ 1) for i in range(8)])

    def columns(flip):
        return [pl.BlockSpec((TOK, ROWS), lambda c, s, d=d: (0, ((s[0] ^ flip) + 2 * d) & 7)) for d in range(4)]

    weight_peer = swap(weight)

    first_up, first_far, first_down, peer_0 = pl.pallas_call(
        pack_first_kernel,
        grid_spec=pltpu.PrefetchScalarGridSpec(
            num_scalar_prefetch=1,
            grid=(1,),
            in_specs=[whole(TOK, HALF)] + columns(1),
            out_specs=[MESSAGE] * 3 + [PIECE],
        ),
        out_shape=[shape(HALF, 2 * TOK)] * 3 + [shape(TOK, ROWS)],
        compiler_params=params(),
        cost_estimate=cost(0, 4),
    )(place, cotangent, tokens, tokens, tokens, tokens)
    first_lo = up(first_up)
    first_hi = down(first_down)
    first_x = across(first_far)
    firsts = (first_up, first_hi, first_x, first_lo)

    cot_b = pl.pallas_call(
        pack_second_kernel,
        grid=(1,),
        in_specs=[pl.BlockSpec((TOK, HALF), lambda c: (0, 1)), AFTER, AFTER],
        out_specs=whole(HALF, TOK),
        out_shape=shape(HALF, TOK),
        compiler_params=params(),
        cost_estimate=cost(0, 1),
    )(cotangent, first_lo, first_hi)
    b_lo, b_hi, b_far = up(cot_b), down(cot_b), across(cot_b)
    cots_b = (cot_b, b_hi, b_far, b_lo)

    own_0, own_up, own_across, own_down = pl.pallas_call(
        pack_own_kernel,
        grid_spec=pltpu.PrefetchScalarGridSpec(
            num_scalar_prefetch=1,
            grid=(1,),
            in_specs=columns(0) + [AFTER, AFTER],
            out_specs=[PIECE] * 4,
        ),
        out_shape=[shape(TOK, ROWS)] * 4,
        compiler_params=params(),
        cost_estimate=cost(0, 2),
    )(place, tokens, tokens, tokens, tokens, b_lo, b_hi)
    owns = (own_0, down(own_down), across(own_across), up(own_up))

    partial_a = pl.pallas_call(
        partial_first_kernel,
        grid=(1,),
        in_specs=[MESSAGE] * 4 + [PIECE, INDEX, AFTER, AFTER],
        out_specs=whole(HALF + PICKS, ROWS),
        out_shape=shape(HALF + PICKS, ROWS),
        compiler_params=params(),
        cost_estimate=cost(KV * KV * ROWS, 3),
    )(*firsts, peer_0, index_t, weight_peer, cot_b)
    got_a = swap(partial_a)
    partial_b = pl.pallas_call(
        partial_second_kernel,
        grid=(1,),
        in_specs=[whole(HALF, TOK)] * 4 + [PIECE] + [MESSAGE] * 3,
        out_specs=whole(HALF, ROWS),
        out_shape=shape(HALF, ROWS),
        compiler_params=params(),
        cost_estimate=cost(KV * KV * ROWS, 3),
    )(*cots_b, peer_0, *firsts[1:])
    got_b = swap(partial_b)

    pre = pl.pallas_call(
        own_kernel,
        grid=(STEPS,),
        in_specs=[first_half(GROUP, 2 * TOK)] * 4
        + [second_half(GROUP, TOK)] * 4
        + [PIECE] * 4
        + [by_col(ROWS, GROUP)],
        out_specs=by_row(GROUP, ROWS),
        out_shape=shape(KV, ROWS, dtype=F32),
        compiler_params=params(),
        cost_estimate=cost(2 * KV * KV * ROWS, 7),
    )(*firsts, *cots_b, *owns, momentum[0])

    base, base_up, base_across, base_down = pl.pallas_call(
        base_kernel,
        grid_spec=pltpu.PrefetchScalarGridSpec(
            num_scalar_prefetch=1,
            grid=(1,),
            in_specs=[PIECE] * 5
            + [MESSAGE] * 3
            + [whole(ROWS, KV)] * 2
            + [INDEX, whole(HALF + PICKS, ROWS)],
            out_specs=[whole(TOK + PICKS, KV)] * 4,
        ),
        out_shape=[shape(TOK + PICKS, KV)] * 4,
        compiler_params=params(2 * VMEM_LIMIT),
        cost_estimate=cost(4 * KV * KV * ROWS, 7),
    )(place, *owns, peer_0, *firsts[1:], weight, weight_peer, index_t, got_a)
    base_lo, base_hi, base_far = up(base_up), down(base_down), across(base_across)

    halves = whole(TILES // 2, 8, LANES)
    half_shape = shape(TILES // 2, 8, LANES, dtype=F32)
    moment, picked, keep, send = pl.pallas_call(
        pick_kernel,
        grid_spec=pltpu.PrefetchScalarGridSpec(
            num_scalar_prefetch=1,
            grid=(STEPS,),
            in_specs=[by_row(GROUP, ROWS)] + GOT + [INDEX_STEP] + BASIS + [AFTER],
            out_specs=[by_row(GROUP, ROWS), by_row(PICKS // STEPS, ROWS), halves, halves],
        ),
        out_shape=[shape(KV, ROWS, dtype=F32), shape(PICKS, ROWS, dtype=F32), half_shape, half_shape],
        compiler_params=params(),
        cost_estimate=cost(6 * KV * GROUP * ROWS, 6),
    )(place, pre, got_a, got_b, index_t, high, low, base)

    def partner(x, bits):
        return lax.ppermute(x, "rep", [(i, i ^ bits) for i in range(REPS)])

    def add(kernel, result, *parts, after=()):
        return pl.pallas_call(
            kernel,
            grid=(1,),
            in_specs=[halves] * len(parts) + [AFTER] * len(after),
            out_specs=halves,
            out_shape=result,
            compiler_params=params(),
            cost_estimate=cost(0, 0.25),
        )(*parts, *after)

    value = add(add_two_kernel, half_shape, keep, partner(send, 1))
    from_hi = partner(value, 2)

    value = add(add_two_kernel, half_shape, value, from_hi)
    value = add(add_two_kernel, half_shape, value, partner(value, 4))
    value = add(add_two_kernel, shape(TILES // 2, 8, LANES), value, partner(value, 8))
    last = partner(value, 16)
    new_momentum, mark = pl.pallas_call(
        residual_kernel,
        grid=(STEPS,),
        in_specs=[by_row(GROUP, ROWS), by_row(PICKS // STEPS, ROWS), INDEX_STEP] + BASIS + [AFTER],
        out_specs=[by_col(ROWS, GROUP), whole(8, LANES)],
        out_shape=[shape(ROWS, KV, dtype=F32), shape(8, LANES, dtype=F32)],
        compiler_params=params(),
        cost_estimate=cost(6 * KV * GROUP * ROWS, 5),
    )(moment, picked, index_t, high, low, value)
    half = add(add_two_kernel, shape(TILES // 2, 8, LANES), value, last, after=(mark,))

    corner = lax.ppermute(half, ("rep", "fsdp"), [(i, i ^ 9) for i in range(REPS * 8)])
    pair_spec = whole(2, TILES, 8, LANES)
    pair = pl.pallas_call(
        pair_kernel,
        grid_spec=pltpu.PrefetchScalarGridSpec(
            num_scalar_prefetch=1,
            grid=(1,),
            in_specs=[halves] * 4 + [AFTER] * 3,
            out_specs=pair_spec,
        ),
        out_shape=shape(2, TILES, 8, LANES),
        compiler_params=params(),
        cost_estimate=cost(0, 0.25),
    )(place, half, partner(half, 1), swap(half), corner, base_lo, base_hi, base_far)
    pair_far, pair_lo, pair_hi = across(pair), up(pair), down(pair)

    def token_block(d):
        return pl.BlockSpec((TOK, 2 * ROWS), lambda c, s: (0, ((s[0] >> 1) + d) & 3))

    mixed, new_weight = pl.pallas_call(
        forward_own_kernel,
        grid_spec=pltpu.PrefetchScalarGridSpec(
            num_scalar_prefetch=1,
            grid=(1,),
            in_specs=[token_block(0), whole(TOK + PICKS, KV), pair_spec, whole(ROWS, KV)] + BASIS,
            out_specs=[whole(KV, TOK), whole(ROWS, KV)],
            scratch_shapes=[DENSE, PAIRS, VALUES],
        ),
        out_shape=[shape(KV, TOK, dtype=F32), shape(ROWS, KV)],
        compiler_params=params(),
        cost_estimate=cost(3 * KV * KV * ROWS, 4),
    )(place, tokens, base, pair, weight, high, low)

    mixed = pl.pallas_call(
        forward_near_kernel,
        grid_spec=pltpu.PrefetchScalarGridSpec(
            num_scalar_prefetch=1,
            grid=(1,),
            in_specs=[token_block(1), token_block(3)]
            + [whole(TOK + PICKS, KV)] * 2
            + [pair_spec] * 2
            + [whole(KV, TOK)],
            out_specs=whole(KV, TOK),
            scratch_shapes=[DENSE] * 2 + [PAIRS] * 2 + [VALUES] * 2,
        ),
        out_shape=shape(KV, TOK, dtype=F32),
        compiler_params=params(2 * VMEM_LIMIT),
        cost_estimate=cost(4 * KV * KV * ROWS, 5),
    )(place, tokens, tokens, base_hi, base_lo, pair_hi, pair_lo, mixed)

    projected = pl.pallas_call(
        forward_far_kernel,
        grid_spec=pltpu.PrefetchScalarGridSpec(
            num_scalar_prefetch=1,
            grid=(1,),
            in_specs=[token_block(2)]
            + [whole(TOK + PICKS, KV)] * 4
            + [pair_spec, whole(KV, TOK)]
            + BASIS,
            out_specs=whole(TOK, KV),
            scratch_shapes=[DENSE, PAIRS, VALUES, pltpu.VMEM((KV, TOK), F32)],
        ),
        out_shape=shape(TOK, KV),
        compiler_params=params(2 * VMEM_LIMIT),
        cost_estimate=cost(3 * KV * KV * ROWS, 5),
    )(place, tokens, base, base_hi, base_far, base_lo, pair_far, mixed, high, low)
    return (projected, new_weight, new_momentum[None])


def solution(mesh):
    in_specs = (
        P(("rep", "fsdp"), None),
        P(("rep", "fsdp"), None),
        P("fsdp", None),
        P("rep", "fsdp", None),
        P("fsdp", None, None),
    )
    out_specs = (P(("rep", "fsdp"), None), P("fsdp", None), P("rep", "fsdp", None))
    return jax.shard_map(body, mesh=mesh, in_specs=in_specs, out_specs=out_specs, check_vma=False)
```
